32 devices in a mesh: dp: 8 (over z, y), tensor: 4 (over x, core).
Axes of the slice: x: 2, y: 2, z: 4, core: 2. Of those that a mesh axis runs over, the one named last changes fastest.
Arguments:
- source_tokens: bfloat16 [8192, 1024], P(('dp', 'tensor')), may hold values from -6 to 6
- target_tokens: bfloat16 [8192, 1024], P(('dp', 'tensor')), may hold values from -6 to 6
- source_lengths: int32 [8, 8], P('dp'), may hold values from 1 to 1024, as said below
- target_lengths: int32 [8, 8], P('dp'), may hold values from 1 to 1024, as said below
- bucket_kinds: int32 [8], P('dp'), may hold values from 0 to 1, as said below
- source_cotangent: float32 [8192, 1024], P(('dp', 'tensor')), may hold values from -6 to 6
- target_cotangent: float32 [8192, 1024], P(('dp', 'tensor')), may hold values from -6 to 6
- attention_in: float32 [3, 3, 1024, 1024], P(None, None, 'dp', 'tensor')
- attention_out: float32 [3, 1024, 1024], P(None, 'tensor', 'dp')
- hidden_in: float32 [2, 1024, 4096], P(None, 'dp', 'tensor')
- hidden_out: float32 [2, 4096, 1024], P(None, 'tensor', 'dp')
- vectors: float32 [25, 1024], P(None, 'dp')
- hidden_bias: float32 [2, 4096], P(None, 'dp'), may hold values from -1.75 to 1.75
- first_attention_in: float32 [3, 3, 1024, 1024], P(None, None, 'dp', 'tensor')
- first_attention_out: float32 [3, 1024, 1024], P(None, 'tensor', 'dp')
- first_hidden_in: float32 [2, 1024, 4096], P(None, 'dp', 'tensor')
- first_hidden_out: float32 [2, 4096, 1024], P(None, 'tensor', 'dp')
- first_vectors: float32 [25, 1024], P(None, 'dp')
- first_hidden_bias: float32 [2, 4096], P(None, 'dp')
- second_attention_in: float32 [3, 3, 1024, 1024], P(None, None, 'dp', 'tensor'), as said below
- second_attention_out: float32 [3, 1024, 1024], P(None, 'tensor', 'dp'), as said below
- second_hidden_in: float32 [2, 1024, 4096], P(None, 'dp', 'tensor'), as said below
- second_hidden_out: float32 [2, 4096, 1024], P(None, 'tensor', 'dp'), as said below
- second_vectors: float32 [25, 1024], P(None, 'dp'), as said below
- second_hidden_bias: float32 [2, 4096], P(None, 'dp'), as said below
Outputs:
- encoder_output: float32 [8192, 1024], P(('dp', 'tensor'))
- decoder_output: float32 [8192, 1024], P(('dp', 'tensor'))
- source_grad: float32 [8192, 1024], P(('dp', 'tensor'))
- target_grad: float32 [8192, 1024], P(('dp', 'tensor'))
- grad_norm: float32 [], replicated
- grad_attention_in: float32 [3, 3, 1024, 1024], P(None, None, 'dp', 'tensor')
- new_second_attention_in: float32 [3, 3, 1024, 1024], P(None, None, 'dp', 'tensor')
- new_attention_in: float32 [3, 3, 1024, 1024], P(None, None, 'dp', 'tensor')
- grad_attention_out: float32 [3, 1024, 1024], P(None, 'tensor', 'dp')
- new_second_attention_out: float32 [3, 1024, 1024], P(None, 'tensor', 'dp')
- new_attention_out: float32 [3, 1024, 1024], P(None, 'tensor', 'dp')
- grad_hidden_in: float32 [2, 1024, 4096], P(None, 'dp', 'tensor')
- new_second_hidden_in: float32 [2, 1024, 4096], P(None, 'dp', 'tensor')
- new_hidden_in: float32 [2, 1024, 4096], P(None, 'dp', 'tensor')
- grad_hidden_out: float32 [2, 4096, 1024], P(None, 'tensor', 'dp')
- new_second_hidden_out: float32 [2, 4096, 1024], P(None, 'tensor', 'dp')
- new_hidden_out: float32 [2, 4096, 1024], P(None, 'tensor', 'dp')
- grad_vectors: float32 [25, 1024], P(None, 'dp')
- new_second_vectors: float32 [25, 1024], P(None, 'dp')
- new_vectors: float32 [25, 1024], P(None, 'dp')
- grad_hidden_bias: float32 [2, 4096], P(None, 'dp')
- new_second_hidden_bias: float32 [2, 4096], P(None, 'dp')
- new_hidden_bias: float32 [2, 4096], P(None, 'dp')
- output_bias_grad: float32 [2, 1024], P(None, 'dp')
The draws below stay inside these ranges and needn't reach their ends.
Inputs may be any that keep to these rules, and one draw needn't show every extreme that they name: `bucket_kinds`: 0 marks a row of 8 items of 128 positions, 1 a row holding one item of 1024 positions; every draw has rows of both kinds. `source_lengths`: in a row of kind 0 every entry is at most 128 and some entry equals 128. In a row of kind 1 only the first entry is read; it is above 768, and in some row it equals 1024; the others lie in 1 to 128. `target_lengths`: as for source_lengths, drawn apart. `second_attention_in`: positive. `second_attention_out`: positive. `second_hidden_in`: positive. `second_hidden_out`: positive. `second_vectors`: positive. `second_hidden_bias`: positive.
All inputs are finite; a program needn't handle non-finite values.
Results may differ from the reference program's by a relative error of at most 0.015.
The reference program's roundings to bfloat16 on the way count: a program that leaves them out, or rounds other values in their place, can miss the bound.
Values may be sent and summed in bfloat16 or wider, within the bound.
No kernel may reach another device: no remote copies, remote signals or barrier semaphores. Data moves between devices by JAX's collectives and lax.ppermute only.
A program may use at most 256 MiB of HBM per device.

```python
import math
import jax
import jax.numpy as jnp
from jax import lax

D = 1024
HEADS = 16
FF = 4096
L = 1024
ITEMS = 8
STEP = 10
HEAD = 64
ITEM = 128
ROWS = 8
TOKENS = 8192
PARAMS = 29393920


def bucket_layout(key):
    layout_key = jax.random.fold_in(key, 101)
    kind_key, pick_key, source_key, target_key = jax.random.split(layout_key, 4)
    row_ids = jnp.arange(ROWS, dtype=jnp.int32)
    bucket_kinds = jax.random.randint(kind_key, (ROWS,), 0, 2, dtype=jnp.int32)
    special = jax.random.randint(pick_key, (), 0, ROWS, dtype=jnp.int32)
    bucket_kinds = jnp.where(row_ids == special, 1, bucket_kinds)
    bucket_kinds = jnp.where(row_ids == (special + 1) % ROWS, 0, bucket_kinds)
    length_sets = []
    for side_key in (source_key, target_key):
        short_key, full_key, long_key = jax.random.split(side_key, 3)
        short_lengths = jax.random.randint(short_key, (ROWS, ITEMS), 1, ITEM + 1, dtype=jnp.int32)
        full_item = jax.random.randint(full_key, (ROWS, 1), 0, ITEMS, dtype=jnp.int32)
        short_lengths = jnp.where(jnp.arange(ITEMS, dtype=jnp.int32)[None, :] == full_item, ITEM, short_lengths)
        long_lengths = jax.random.randint(long_key, (ROWS,), 3 * L // 4 + 1, L + 1, dtype=jnp.int32)
        long_lengths = jnp.where(row_ids == special, L, long_lengths)
        leading = jnp.where(bucket_kinds == 1, long_lengths, short_lengths[:, 0])
        length_sets.append(short_lengths.at[:, 0].set(leading).astype(jnp.int32))
    return (bucket_kinds.astype(jnp.int32), length_sets[0], length_sets[1])


def draw_bucket_kinds(key, part):
    shared = bucket_layout(key)
    return shared[0]


def draw_source_lengths(key, part):
    shared = bucket_layout(key)
    return shared[1]


def draw_target_lengths(key, part):
    shared = bucket_layout(key)
    return shared[2]


def linear_ramp(entries, low_end, high_end):
    return low_end + (high_end - low_end) * jnp.arange(entries, dtype=jnp.float32) / max(entries - 1, 1)


def ramped(base_draw, fan_in, ramp_axis, low_end, high_end):
    dims_list = [1] * base_draw.ndim
    dims_list[ramp_axis] = base_draw.shape[ramp_axis]
    return base_draw * fan_in ** (-0.5) * linear_ramp(base_draw.shape[ramp_axis], low_end, high_end).reshape(dims_list)


def unit_normal(key, full_shape):
    return jax.random.normal(key, full_shape, jnp.float32)


def draw_attention_in(key, part):
    key = jax.random.fold_in(key, 11)
    return ramped(unit_normal(key, (3, 3, D, D)), D, 3, 0.5, 0.9)


def draw_attention_out(key, part):
    key = jax.random.fold_in(key, 12)
    return ramped(unit_normal(key, (3, D, D)), D // 8, 1, 0.6, 1.8)


def draw_hidden_in(key, part):
    key = jax.random.fold_in(key, 13)
    return ramped(unit_normal(key, (2, D, FF)), D, 2, 0.6, 1.8)


def draw_hidden_out(key, part):
    key = jax.random.fold_in(key, 14)
    return ramped(unit_normal(key, (2, FF, D)), FF, 1, 0.6, 1.8)


def gain_rows(key, low_end, high_end):
    rough = jax.random.uniform(key, (7, D), jnp.float32, 0.85, 1.15)
    return rough * linear_ramp(D, low_end, high_end)[None, :]


def draw_vectors(key, part):
    key = jax.random.fold_in(key, 15)
    gain_key, offset_key = jax.random.split(key)
    gains = gain_rows(gain_key, 0.6, 1.8)
    offsets = 0.3 * jax.random.normal(offset_key, (18, D), jnp.float32)
    return jnp.concatenate([gains, offsets], axis=0)


def first_state(key, full_shape, multiple):
    grad_size = multiple * PARAMS ** (-0.5)
    return 0.111 * grad_size * jax.random.normal(key, full_shape, jnp.float32)


def second_state(key, full_shape, multiple):
    grad_size = multiple * PARAMS ** (-0.5)
    spread = jnp.exp(jax.random.uniform(key, full_shape, jnp.float32, 0.0, math.log(4.0)))
    return 0.002 * grad_size * grad_size * spread


def draw_first_attention_in(key, part):
    key = jax.random.fold_in(key, 21)
    return first_state(key, (3, 3, D, D), 0.5)


def draw_first_attention_out(key, part):
    key = jax.random.fold_in(key, 22)
    return first_state(key, (3, D, D), 1.0)


def draw_first_hidden_in(key, part):
    key = jax.random.fold_in(key, 23)
    return first_state(key, (2, D, FF), 1.0)


def draw_first_hidden_out(key, part):
    key = jax.random.fold_in(key, 24)
    return first_state(key, (2, FF, D), 1.0)


def draw_first_vectors(key, part):
    key = jax.random.fold_in(key, 25)
    return first_state(key, (25, D), 3.0)


def draw_first_hidden_bias(key, part):
    key = jax.random.fold_in(key, 26)
    return first_state(key, (2, FF), 0.5)


def draw_second_attention_in(key, part):
    key = jax.random.fold_in(key, 31)
    return second_state(key, (3, 3, D, D), 0.5)


def draw_second_attention_out(key, part):
    key = jax.random.fold_in(key, 32)
    return second_state(key, (3, D, D), 1.0)


def draw_second_hidden_in(key, part):
    key = jax.random.fold_in(key, 33)
    return second_state(key, (2, D, FF), 1.0)


def draw_second_hidden_out(key, part):
    key = jax.random.fold_in(key, 34)
    return second_state(key, (2, FF, D), 1.0)


def draw_second_vectors(key, part):
    key = jax.random.fold_in(key, 35)
    return second_state(key, (25, D), 3.0)


def draw_second_hidden_bias(key, part):
    key = jax.random.fold_in(key, 36)
    return second_state(key, (2, FF), 0.5)


def block_scale(key, extent, shards, least, high):
    def one(position, blocks):
        draws = jax.random.uniform(jax.random.fold_in(jax.random.fold_in(key, 6), position), (blocks,), jnp.float32, least / len(shards), high / len(shards))
        return jnp.repeat(jnp.exp(draws), extent[position] // blocks).reshape((-1,) + (1,) * (len(extent) - position - 1))

    level = one(*shards[0])
    for cut in shards[1:]:
        level = level * one(*cut)
    return level


def normal_values(rng, shape, scale, bound, shards=(), kind=jnp.bfloat16):
    factor_of = block_scale(rng, shape, shards, -0.22, 0.18) if shards else 1.0
    values = jax.random.normal(rng, shape, jnp.float32) * scale * factor_of
    return jnp.minimum(jnp.maximum(values, -bound), bound).astype(kind)


def setup_inputs(seed: int = 0) -> dict:
    streams_of = jax.random.split(jax.random.key(seed), 26)
    source_tokens = normal_values(streams_of[0], (TOKENS, D), 1.0, 6.0, ((0, 32),))
    target_tokens = normal_values(streams_of[1], (TOKENS, D), 1.0, 6.0, ((0, 32),))
    source_lengths = draw_source_lengths(jax.random.fold_in(streams_of[25], 71), 0)
    target_lengths = draw_target_lengths(jax.random.fold_in(streams_of[25], 71), 0)
    bucket_kinds = draw_bucket_kinds(jax.random.fold_in(streams_of[25], 71), 0)
    source_cotangent = normal_values(streams_of[5], (TOKENS, D), 1.0, 6.0, ((0, 32),), jnp.float32)
    target_cotangent = normal_values(streams_of[6], (TOKENS, D), 1.0, 6.0, ((0, 32),), jnp.float32)
    attention_in = draw_attention_in(jax.random.fold_in(streams_of[25], 71), 0)
    attention_out = draw_attention_out(jax.random.fold_in(streams_of[25], 71), 0)
    hidden_in = draw_hidden_in(jax.random.fold_in(streams_of[25], 71), 0)
    hidden_out = draw_hidden_out(jax.random.fold_in(streams_of[25], 71), 0)
    vectors = draw_vectors(jax.random.fold_in(streams_of[25], 71), 0)
    hidden_bias = normal_values(streams_of[12], (2, FF), 0.3, 1.75, ((1, 8),), jnp.float32)
    first_attention_in = draw_first_attention_in(jax.random.fold_in(streams_of[25], 71), 0)
    first_attention_out = draw_first_attention_out(jax.random.fold_in(streams_of[25], 71), 0)
    first_hidden_in = draw_first_hidden_in(jax.random.fold_in(streams_of[25], 71), 0)
    first_hidden_out = draw_first_hidden_out(jax.random.fold_in(streams_of[25], 71), 0)
    first_vectors = draw_first_vectors(jax.random.fold_in(streams_of[25], 71), 0)
    first_hidden_bias = draw_first_hidden_bias(jax.random.fold_in(streams_of[25], 71), 0)
    second_attention_in = draw_second_attention_in(jax.random.fold_in(streams_of[25], 71), 0)
    second_attention_out = draw_second_attention_out(jax.random.fold_in(streams_of[25], 71), 0)
    second_hidden_in = draw_second_hidden_in(jax.random.fold_in(streams_of[25], 71), 0)
    second_hidden_out = draw_second_hidden_out(jax.random.fold_in(streams_of[25], 71), 0)
    second_vectors = draw_second_vectors(jax.random.fold_in(streams_of[25], 71), 0)
    second_hidden_bias = draw_second_hidden_bias(jax.random.fold_in(streams_of[25], 71), 0)
    return dict(source_tokens=source_tokens, target_tokens=target_tokens, source_lengths=source_lengths, target_lengths=target_lengths, bucket_kinds=bucket_kinds, source_cotangent=source_cotangent, target_cotangent=target_cotangent, attention_in=attention_in, attention_out=attention_out, hidden_in=hidden_in, hidden_out=hidden_out, vectors=vectors, hidden_bias=hidden_bias, first_attention_in=first_attention_in, first_attention_out=first_attention_out, first_hidden_in=first_hidden_in, first_hidden_out=first_hidden_out, first_vectors=first_vectors, first_hidden_bias=first_hidden_bias, second_attention_in=second_attention_in, second_attention_out=second_attention_out, second_hidden_in=second_hidden_in, second_hidden_out=second_hidden_out, second_vectors=second_vectors, second_hidden_bias=second_hidden_bias)


@jax.custom_vjp
def low(v):
    return lax.optimization_barrier(v.astype(jnp.bfloat16)).astype(jnp.float32)

@jax.custom_vjp
def low_back(v):
    return v

def low_keep(v):
    return (low(v), None)

def low_pass(kept, grad):
    return (grad,)

def back_keep(v):
    return (v, None)

def back_low(kept, grad):
    return (low(grad),)
low.defvjp(low_keep, low_pass)
low_back.defvjp(back_keep, back_low)
NORM_EPS = 1e-05
CLIP_NORM = 1.0
BETA_FIRST = 0.9
BETA_SECOND = 0.999
ADAM_EPS = 1e-08
MATRIX_DECAY = 0.01
MASKED = -1e+30
HIGHEST = lax.Precision.HIGHEST

def round_both(values):
    return low(low_back(values))

def matmul(operand, weight_mat):
    return jnp.dot(operand, weight_mat, precision=HIGHEST, preferred_element_type=jnp.float32)

def layer_norm(hidden, gain_vec, offset):
    center = hidden - lax.optimization_barrier(jnp.mean(hidden, axis=-1, keepdims=True))
    spread = lax.optimization_barrier(jnp.mean(center * center, axis=-1, keepdims=True))
    return center * lax.rsqrt(spread + NORM_EPS) * gain_vec + offset

def item_layout(row_kind, lengths):
    places = jnp.arange(L, dtype=jnp.int32)
    item_ids = jnp.where(row_kind == 1, 0, places // ITEM).astype(jnp.int32)
    within = jnp.where(row_kind == 1, places, places % ITEM).astype(jnp.int32)
    chosen = item_ids[:, None] == jnp.arange(ITEMS, dtype=jnp.int32)[None, :]
    item_length = lax.optimization_barrier(jnp.sum(jnp.where(chosen, lengths[None, :], 0), axis=1)).astype(jnp.int32)
    return (item_ids, within < item_length)

def attend_block(queries, key_rows, value_rows, query_items, key_items, key_live, query_place):
    key_place = jnp.arange(key_rows.shape[0], dtype=jnp.int32)
    allowed = (query_items[:, None] == key_items[None, :]) & key_live[None, :] & (key_place[None, :] <= query_place[:, None])
    scores = jnp.einsum('qhd,khd->hqk', queries, key_rows, precision=HIGHEST) * HEAD ** (-0.5)
    scores = low_back(scores)
    scores = jnp.where(allowed[None], scores, MASKED)
    largest = lax.optimization_barrier(jnp.max(scores, axis=-1, keepdims=True))
    weights = jnp.exp(scores - largest)
    weights = weights / lax.optimization_barrier(jnp.sum(weights, axis=-1, keepdims=True))
    return jnp.einsum('hqk,khd->qhd', low(weights), value_rows, precision=HIGHEST)
checked_block = jax.checkpoint(attend_block)

def attend_rows(queries, key_rows, value_rows, query_items, key_items, key_live, causal):
    block_rows = min(L, 512)
    places = jnp.arange(L, dtype=jnp.int32)
    if causal:
        query_place = places
    else:
        query_place = jnp.full((L,), L - 1, jnp.int32)

    def one_row(operands):
        row_queries, row_keys, row_values, row_items, row_key_items, row_live = operands
        pieces = []
        for first_row in range(0, L, block_rows):
            pieces.append(checked_block(row_queries[first_row:first_row + block_rows], row_keys, row_values, row_items[first_row:first_row + block_rows], row_key_items, row_live, query_place[first_row:first_row + block_rows]))
        return jnp.concatenate(pieces, axis=0)
    return lax.map(one_row, (queries, key_rows, value_rows, query_items, key_items, key_live))

def as_heads(matrix):
    return matrix.reshape(-1, L, HEADS, HEAD)

def attention_branch(slot_id, normed, memory, attn_in, attn_out, vectors, query_items, key_items, key_live, causal):
    queries = round_both(matmul(normed, attn_in[slot_id, 0]) + vectors[14 + 2 * slot_id])
    key_rows = round_both(matmul(memory, attn_in[slot_id, 1]))
    value_rows = round_both(matmul(memory, attn_in[slot_id, 2]) + vectors[15 + 2 * slot_id])
    context = attend_rows(as_heads(queries), as_heads(key_rows), as_heads(value_rows), query_items, key_items, key_live, causal)
    context = round_both(context.reshape(-1, D))
    return low_back(matmul(context, attn_out[slot_id])) + vectors[20 + slot_id]

def feed_forward(slot_id, normed, up_weights, down_weights, unit_bias, vectors):
    pre_act = low_back(matmul(normed, up_weights[slot_id]) + unit_bias[slot_id])
    activated = low(jax.nn.gelu(pre_act, approximate=True))
    return low_back(matmul(activated, down_weights[slot_id])) + vectors[23 + slot_id]

def forward(param_list, source, target, kind_rows, source_rows, target_rows):
    attn_in, attn_out, up_weights, down_weights, vectors, unit_bias = [low(weight) for weight in param_list]
    source_items, source_live = jax.vmap(item_layout)(kind_rows, source_rows)
    target_items, target_live = jax.vmap(item_layout)(kind_rows, target_rows)
    normed = low(layer_norm(source, vectors[0], vectors[7]))
    stream = source + attention_branch(0, normed, normed, attn_in, attn_out, vectors, source_items, source_items, source_live, False)
    normed = low(layer_norm(stream, vectors[1], vectors[8]))
    stream = stream + feed_forward(0, normed, up_weights, down_weights, unit_bias, vectors)
    memory = layer_norm(stream, vectors[2], vectors[9])
    memory_low = low(memory)
    normed = low(layer_norm(target, vectors[3], vectors[10]))
    flow = target + attention_branch(1, normed, normed, attn_in, attn_out, vectors, target_items, target_items, target_live, True)
    normed = low(layer_norm(flow, vectors[4], vectors[11]))
    flow = flow + attention_branch(2, normed, memory_low, attn_in, attn_out, vectors, target_items, source_items, source_live, False)
    normed = low(layer_norm(flow, vectors[5], vectors[12]))
    flow = flow + feed_forward(1, normed, up_weights, down_weights, unit_bias, vectors)
    return (memory, layer_norm(flow, vectors[6], vectors[13]))

def reference(source_tokens, target_tokens, source_lengths, target_lengths, bucket_kinds, source_cotangent, target_cotangent, attention_in, attention_out, hidden_in, hidden_out, vectors, hidden_bias, first_attention_in, first_attention_out, first_hidden_in, first_hidden_out, first_vectors, first_hidden_bias, second_attention_in, second_attention_out, second_hidden_in, second_hidden_out, second_vectors, second_hidden_bias):
    params = (attention_in, attention_out, hidden_in, hidden_out, vectors, hidden_bias)
    group_rows = math.gcd(ROWS, max(1, 4096 // L))
    groups = ROWS // group_rows

    def to_groups(values):
        return values.astype(jnp.float32).reshape(groups, group_rows * L, D)

    def one_group(totals, operands):
        source, target, source_back, target_back, kind_rows, source_rows, target_rows = operands

        def mapped(param_list, source_in, target_in):
            return forward(param_list, source_in, target_in, kind_rows, source_rows, target_rows)
        outputs, pullback = jax.vjp(mapped, params, source, target)
        param_grads, source_grads, target_grads = pullback((source_back, target_back))
        totals = jax.tree.map(jnp.add, totals, param_grads)
        return (totals, (outputs[0], outputs[1], source_grads, target_grads))
    zero_grads = jax.tree.map(jnp.zeros_like, params)
    totals, stacked = lax.scan(one_group, zero_grads, (to_groups(source_tokens), to_groups(target_tokens), to_groups(source_cotangent), to_groups(target_cotangent), bucket_kinds.reshape(groups, group_rows), source_lengths.reshape(groups, group_rows, ITEMS), target_lengths.reshape(groups, group_rows, ITEMS)))
    encoder_output = stacked[0].reshape(TOKENS, D)
    decoder_output = stacked[1].reshape(TOKENS, D)
    source_grad = stacked[2].reshape(TOKENS, D)
    target_grad = stacked[3].reshape(TOKENS, D)
    squares = sum([jnp.sum(gradient * gradient) for gradient in totals])
    grad_norm = jnp.sqrt(squares)
    factor = jnp.minimum(1.0, CLIP_NORM / (grad_norm + 1e-06))
    rates = (0.5 * D ** (-0.5), 0.5 * (D // 8) ** (-0.5), 0.5 * D ** (-0.5), 0.5 * FF ** (-0.5), 0.3, 0.3)
    decays = (MATRIX_DECAY, MATRIX_DECAY, MATRIX_DECAY, MATRIX_DECAY, 0.0, 0.0)
    firsts = (first_attention_in, first_attention_out, first_hidden_in, first_hidden_out, first_vectors, first_hidden_bias)
    seconds = (second_attention_in, second_attention_out, second_hidden_in, second_hidden_out, second_vectors, second_hidden_bias)
    results = []
    for weight, gradient, first_old, second_old, step_rate, decay_rate in zip(params, totals, firsts, seconds, rates, decays):
        clipped = gradient * factor
        moment = BETA_FIRST * first_old + (1.0 - BETA_FIRST) * clipped
        second_new = BETA_SECOND * second_old + (1.0 - BETA_SECOND) * clipped * clipped
        fixed_first = moment / (1.0 - BETA_FIRST ** STEP)
        fixed_second = second_new / (1.0 - BETA_SECOND ** STEP)
        updated = weight - step_rate * (fixed_first / (jnp.sqrt(fixed_second) + ADAM_EPS) + decay_rate * weight)
        results.append(clipped)
        results.append(second_new)
        results.append(updated)
    return (encoder_output, decoder_output, source_grad, target_grad, grad_norm, results[0], results[1], results[2], results[3], results[4], results[5], results[6], results[7], results[8], results[9], results[10], results[11], results[12], results[13], results[14], results[15], results[16], results[17], results[12][23:25])
```

```python
from functools import partial

import jax
import jax.numpy as jnp
from jax import lax
from jax.sharding import PartitionSpec as P

D = 1024
FF = 4096
L = 1024
ITEMS = 8
STEP = 10
HEAD = 64
ITEM = 128


NORM_EPS = 1e-05
CLIP_NORM = 1.0
BETA_FIRST = 0.9
BETA_SECOND = 0.999
ADAM_EPS = 1e-08
MATRIX_DECAY = 0.01
MASKED = -1e30

BF16 = jnp.bfloat16
F32 = jnp.float32


def layer_norm(hidden, gain_vec, offset):
    center = hidden - jnp.mean(hidden, axis=-1, keepdims=True)
    spread = jnp.mean(center * center, axis=-1, keepdims=True)
    return center * lax.rsqrt(spread + NORM_EPS) * gain_vec + offset


def norm_back(hidden, gain_vec, offset, upstream):
    unused, pullback = jax.vjp(layer_norm, hidden, gain_vec, offset)
    return pullback(upstream)


def gelu_tanh(pre_value):
    return jax.nn.gelu(pre_value, approximate=True)


def matmul(operand, weight_mat):
    return jnp.dot(operand, weight_mat, preferred_element_type=F32)


def contract_rows(operand, other_side):
    return lax.dot_general(
        operand, other_side, (((0,), (0,)), ((), ())), preferred_element_type=F32
    )


def contract_last(operand, other_side):
    return lax.dot_general(
        operand, other_side, (((1,), (1,)), ((), ())), preferred_element_type=F32
    )


class TensorMoves:
    def __init__(self):
        self.count = lax.axis_size("tensor")
        assert self.count == 4
        self.me = lax.axis_index("tensor")

    def swap(self, values, bit):
        pairs = [(index, index ^ bit) for index in range(self.count)]
        return lax.ppermute(values, "tensor", pairs)

    def gather(self, shard):
        far = self.swap(shard, 2)
        near = self.swap(shard, 1)
        far_near = self.swap(far, 1)
        return jnp.concatenate([shard, near], 0), jnp.concatenate([far, far_near], 0)

    def scatter(self, near_part, far_part):
        rows = near_part.shape[0] // 2
        far_in = self.swap(far_part[rows:].astype(BF16), 1)
        near_in = self.swap(near_part[rows:].astype(BF16), 1)
        crossing = (far_part[:rows] + far_in.astype(F32)).astype(BF16)
        arrived = self.swap(crossing, 2)
        return near_part[:rows] + near_in.astype(F32) + arrived.astype(F32)

    def total(self, values):
        values = values + self.swap(values, 1)
        return values + self.swap(values, 2)


class PlainRows:
    def __init__(self):
        self.count = lax.axis_size("dp")
        self.me = lax.axis_index("dp")

    def enter(self, values):
        return values

    leave = enter

    def gather(self, shard):
        return lax.all_gather(shard, "dp", axis=0, tiled=True)

    def stack(self, shard):
        return lax.all_gather(shard, "dp", axis=0)

    def scatter(self, near_part, far_part):
        return self.spread(jnp.concatenate([near_part, far_part], 0))

    def spread(self, values):
        return lax.psum_scatter(values, "dp", scatter_dimension=0, tiled=True)

    def place(self, index):
        return index

    def total(self, values):
        return lax.psum(values, "dp")


class CrossRows(PlainRows):
    ORDER = (0, 2, 4, 6, 1, 3, 5, 7)

    def swap(self, values, bits):
        pairs = [(index, index ^ bits) for index in range(self.count)]
        return lax.ppermute(values, "dp", pairs)

    def enter(self, values):
        blocks = values.reshape(values.shape[0], self.count, -1)
        picked = [lax.dynamic_index_in_dim(blocks, self.me ^ k, 1, False) for k in self.ORDER]
        return jnp.concatenate(picked, axis=1)

    def place(self, index):
        distance = index ^ self.me
        return (distance & 1) * 4 + (distance >> 1)

    def leave(self, values):
        blocks = values.reshape(values.shape[0], self.count, -1)
        picked = [
            lax.dynamic_index_in_dim(blocks, self.place(index), 1, False)
            for index in range(self.count)
        ]
        return jnp.concatenate(picked, axis=1)

    def pieces(self, shard):
        near = [shard] + [self.swap(shard, bits) for bits in (2, 4, 6)]
        return near + [self.swap(piece, 1) for piece in near]

    def gather(self, shard):
        return jnp.concatenate(self.pieces(shard), axis=0)

    def stack(self, shard):
        return jnp.stack(self.pieces(shard))

    def scatter(self, near_part, far_part):
        rows = near_part.shape[0] // 4
        part = near_part + self.swap(far_part.astype(BF16), 1).astype(F32)
        sent = part[rows:].astype(BF16)
        total = part[:rows]
        for k, bits in ((0, 2), (1, 4), (2, 6)):
            total = total + self.swap(sent[k * rows : (k + 1) * rows], bits).astype(F32)
        return total

    def spread(self, values):
        half = values.shape[0] // 2
        part = values[:half] + self.swap(values[half:], 1)
        rows = half // 4
        total = part[:rows]
        for k, bits in ((1, 2), (2, 4), (3, 6)):
            total = total + self.swap(part[k * rows : (k + 1) * rows], bits)
        return total

    def total(self, values):
        for bits in (1, 2, 4):
            values = values + self.swap(values, bits)
        return values


def item_codes(row_kind, lengths, places):
    items = jnp.where(row_kind == 1, 0, places // ITEM)
    within = jnp.where(row_kind == 1, places, places % ITEM)
    limit = jnp.zeros_like(places)
    for index in range(ITEMS):
        limit = jnp.where(items == index, lengths[index], limit)
    return items, jnp.where(within < limit, items, -1)


def allowed_pairs(query_codes, key_codes, query_places, key_places, causal):
    allowed = query_codes[:, None] == key_codes[None, :]
    if causal:
        allowed = allowed & (key_places[None, :] <= query_places[:, None])
    return allowed


def masked_scores(query_block, key_rows, allowed):
    factor = query_block.shape[-1] ** (-0.5)
    scores = (
        jnp.einsum("qhd,khd->hqk", query_block, key_rows, preferred_element_type=F32) * factor
    )
    return jnp.where(allowed[None], scores, MASKED)


def as_heads(matrix):
    return matrix.reshape(matrix.shape[0], matrix.shape[1] // HEAD, HEAD)


def attend_forward(queries, key_rows, value_rows, layout, causal):
    query_codes, key_codes, places = layout
    queries, key_rows, value_rows = as_heads(queries), as_heads(key_rows), as_heads(value_rows)
    length = queries.shape[0]
    block_rows = min(length, 512)
    contexts = []
    totals = []
    for first_row in range(0, length, block_rows):
        span = slice(first_row, first_row + block_rows)
        allowed = allowed_pairs(query_codes[span], key_codes, places[span], places, causal)
        scores = masked_scores(queries[span], key_rows, allowed)
        largest = jnp.max(scores, axis=-1, keepdims=True)
        weights = jnp.exp(scores - largest)
        row_total = jnp.sum(weights, axis=-1, keepdims=True)
        weights = weights / row_total
        contexts.append(
            jnp.einsum(
                "hqk,khd->qhd", weights.astype(BF16), value_rows, preferred_element_type=F32
            )
        )
        totals.append((largest + jnp.log(row_total))[..., 0])
    context = jnp.concatenate(contexts, axis=0)
    return context.reshape(length, -1).astype(BF16), jnp.concatenate(totals, axis=1)


def attend_backward(queries, key_rows, value_rows, context_grad, log_totals, layout, causal):
    query_codes, key_codes, places = layout
    shape = queries.shape
    queries, key_rows, value_rows = as_heads(queries), as_heads(key_rows), as_heads(value_rows)
    context_grad = as_heads(context_grad)
    length = queries.shape[0]
    block_rows = min(length, 512)
    factor = queries.shape[-1] ** (-0.5)
    query_grads = []
    key_grad = jnp.zeros(key_rows.shape, F32)
    value_grad = jnp.zeros(value_rows.shape, F32)
    for first_row in range(0, length, block_rows):
        span = slice(first_row, first_row + block_rows)
        query_block = queries[span]
        grad_block = context_grad[span]
        allowed = allowed_pairs(query_codes[span], key_codes, places[span], places, causal)
        scores = masked_scores(query_block, key_rows, allowed)
        weights = jnp.exp(scores - log_totals[:, span, None])
        weight_grad = jnp.einsum(
            "qhd,khd->hqk", grad_block, value_rows, preferred_element_type=F32
        )
        diagonal = jnp.sum(weights * weight_grad, axis=-1, keepdims=True)
        score_grad = (weights * (weight_grad - diagonal)).astype(BF16)
        query_grads.append(
            jnp.einsum("hqk,khd->qhd", score_grad, key_rows, preferred_element_type=F32) * factor
        )
        key_grad = (
            key_grad
            + jnp.einsum("hqk,qhd->khd", score_grad, query_block, preferred_element_type=F32)
            * factor
        )
        value_grad = value_grad + jnp.einsum(
            "hqk,qhd->khd", weights.astype(BF16), grad_block, preferred_element_type=F32
        )
    return (
        jnp.concatenate(query_grads, axis=0).reshape(shape).astype(BF16),
        key_grad.reshape(shape).astype(BF16),
        value_grad.reshape(shape).astype(BF16),
    )


def rows_of(pair):
    return jnp.concatenate(pair, axis=0)


def attention_forward(moves, full, normed, memory, bias_query, bias_value, layout, causal):
    wide = full.shape[1] // 4
    near, far = normed
    is_cross = memory is not normed
    normed_rows = rows_of(normed)
    memory_rows = rows_of(memory)
    if is_cross:
        queries = matmul(normed_rows, full[:, :wide])
        others = matmul(memory_rows, full[:, wide : 3 * wide])
        key_rows, value_rows = others[:, :wide], others[:, wide:]
    else:
        together = matmul(normed_rows, full[:, : 3 * wide])
        queries = together[:, :wide]
        key_rows, value_rows = together[:, wide : 2 * wide], together[:, 2 * wide :]
    queries = (queries + bias_query).astype(BF16)
    key_rows = key_rows.astype(BF16)
    value_rows = (value_rows + bias_value).astype(BF16)
    context, log_totals = attend_forward(queries, key_rows, value_rows, layout, causal)
    half = context.shape[0] // 2
    out = full[:, 3 * wide :]
    far_part = contract_last(context[half:], out)
    near_part = contract_last(context[:half], out)
    branch = moves.scatter(near_part, far_part)
    return branch, (queries, key_rows, value_rows, context, log_totals)


def attention_backward(moves, full, upstream, stored, normed, memory, layout, causal):
    queries, key_rows, value_rows, context, log_totals = stored
    wide = full.shape[1] // 4
    is_cross = memory is not normed
    out_bias = jnp.sum(upstream, axis=0)
    upstream_rows = rows_of(moves.gather(upstream.astype(BF16)))
    context_grad = matmul(upstream_rows, full[:, 3 * wide :]).astype(BF16)
    out_weight = contract_rows(upstream_rows, context)
    query_low, key_low, value_low = attend_backward(
        queries, key_rows, value_rows, context_grad, log_totals, layout, causal
    )
    normed_rows = rows_of(normed)
    half = query_low.shape[0] // 2
    bias_query = jnp.sum(query_low.astype(F32), axis=0)
    bias_value = jnp.sum(value_low.astype(F32), axis=0)
    if is_cross:
        memory_rows = rows_of(memory)
        pair_low = jnp.concatenate([key_low, value_low], axis=1)
        memory_grad = moves.scatter(
            contract_last(pair_low[:half], full[:, wide : 3 * wide]),
            contract_last(pair_low[half:], full[:, wide : 3 * wide]),
        )
        normed_grad = moves.scatter(
            contract_last(query_low[:half], full[:, :wide]),
            contract_last(query_low[half:], full[:, :wide]),
        )
        in_weight = jnp.concatenate(
            [contract_rows(normed_rows, query_low), contract_rows(memory_rows, pair_low)], axis=1
        )
    else:
        all_low = jnp.concatenate([query_low, key_low, value_low], axis=1)
        normed_grad = moves.scatter(
            contract_last(all_low[:half], full[:, : 3 * wide]),
            contract_last(all_low[half:], full[:, : 3 * wide]),
        )
        memory_grad = None
        in_weight = contract_rows(normed_rows, all_low)
    weight_grad = jnp.concatenate([in_weight, out_weight], axis=1)
    return normed_grad, memory_grad, weight_grad, bias_query, bias_value, out_bias


def feed_forward(moves, up_full, down_full, normed, unit_bias):
    states = []
    parts = []
    for rows in normed:
        pre_act = matmul(rows, up_full) + unit_bias
        activated = gelu_tanh(pre_act).astype(BF16)
        states.append((pre_act, activated))
        parts.append(contract_last(activated, down_full))
    return moves.scatter(*parts), states


def feed_backward(moves, up_full, down_full, upstream, states, normed):
    out_bias = jnp.sum(upstream, axis=0)
    upstream_pair = moves.gather(upstream.astype(BF16))
    pre_grads = []
    parts = []
    for rows, (pre_act, activated) in zip(upstream_pair, states):
        act_grad = matmul(rows, down_full)
        unused, pullback = jax.vjp(gelu_tanh, pre_act)
        pre_grad = pullback(act_grad)[0].astype(BF16)
        pre_grads.append(pre_grad)
        parts.append(contract_last(pre_grad, up_full))
    normed_grad = moves.scatter(*parts)
    pre_grad = rows_of(pre_grads)
    unit_grad = jnp.sum(pre_grad.astype(F32), axis=0)
    up_weight = contract_rows(rows_of(normed), pre_grad)
    down_weight = contract_rows(
        rows_of(upstream_pair), rows_of([activated for unused, activated in states])
    )
    return normed_grad, up_weight, down_weight, unit_grad, out_bias


def body(
    source_tokens,
    target_tokens,
    source_lengths,
    target_lengths,
    bucket_kinds,
    source_cotangent,
    target_cotangent,
    attention_in,
    attention_out,
    hidden_in,
    hidden_out,
    vectors,
    hidden_bias,
    first_attention_in,
    first_attention_out,
    first_hidden_in,
    first_hidden_out,
    first_vectors,
    first_hidden_bias,
    second_attention_in,
    second_attention_out,
    second_hidden_in,
    second_hidden_out,
    second_vectors,
    second_hidden_bias,
):
    moves = TensorMoves()
    split = CrossRows() if lax.axis_size("dp") == 8 else PlainRows()
    assert bucket_kinds.shape[0] == 1
    shard_rows = attention_in.shape[2]
    head_width = attention_in.shape[3]
    unit_width = hidden_in.shape[2]
    shard_units = hidden_bias.shape[1]

    def attention_shard(slot_id):
        parts = [attention_in[slot_id, which] for which in range(3)]
        return jnp.concatenate(parts + [attention_out[slot_id].T], axis=1).astype(BF16)

    attn_shards = [attention_shard(slot_id) for slot_id in range(3)]
    up_shards = [hidden_in[slot_id].astype(BF16) for slot_id in range(2)]
    down_shards = [hidden_out[slot_id].T.astype(BF16) for slot_id in range(2)]

    vector_parts = vectors.astype(BF16)
    unit_parts = hidden_bias.astype(BF16).reshape(-1, shard_rows)
    small = split.stack(jnp.concatenate([vector_parts, unit_parts], axis=0)).astype(F32)
    attn_full = [None] * 3
    up_full = [None] * 2
    down_full = [None] * 2
    attn_full[0] = split.gather(attn_shards[0])
    up_full[0] = split.gather(up_shards[0])
    down_full[0] = split.gather(down_shards[0])
    attn_full[1] = split.gather(attn_shards[1])
    attn_full[2] = split.gather(attn_shards[2])
    up_full[1] = split.gather(up_shards[1])
    down_full[1] = split.gather(down_shards[1])

    def wide_vector(row_number):
        return small[:, row_number, :].reshape(-1)

    vector_full = [wide_vector(row_number) for row_number in range(25)]
    head_blocks = head_width // shard_rows
    unit_blocks = unit_width // shard_units

    def own_blocks(count):
        return [
            lax.dynamic_index_in_dim(small, split.place(moves.me * count + index), 0, False)
            for index in range(count)
        ]

    head_small = jnp.concatenate([block[14:20] for block in own_blocks(head_blocks)], axis=1)
    unit_small = jnp.concatenate(
        [block[25:].reshape(2, shard_units) for block in own_blocks(unit_blocks)], axis=1
    )

    block_rows = source_tokens.shape[0]
    places = jnp.concatenate(
        [
            (moves.me ^ index) * block_rows + jnp.arange(block_rows, dtype=jnp.int32)
            for index in range(moves.count)
        ]
    )
    source_items, source_live = item_codes(bucket_kinds[0], source_lengths[0], places)
    target_items, target_live = item_codes(bucket_kinds[0], target_lengths[0], places)
    encoder_layout = (source_items, source_live, places)
    self_layout = (target_items, target_live, places)
    cross_layout = (target_items, source_live, places)

    source = split.enter(source_tokens).astype(F32)
    target = split.enter(target_tokens).astype(F32)
    source_cotangent = split.enter(source_cotangent)
    target_cotangent = split.enter(target_cotangent)

    def norm_rows(hidden, index):
        return layer_norm(hidden, vector_full[index], vector_full[7 + index])

    def gather_norm(hidden, index):
        return moves.gather(norm_rows(hidden, index).astype(BF16))

    source_norm_one = gather_norm(source, 0)
    target_norm_one = gather_norm(target, 3)
    branch, source_attn_state = attention_forward(
        moves,
        attn_full[0],
        source_norm_one,
        source_norm_one,
        head_small[0],
        head_small[1],
        encoder_layout,
        False,
    )
    source_mid = source + (branch + vector_full[20])
    source_norm_two = gather_norm(source_mid, 1)
    branch, source_ffn_state = feed_forward(
        moves, up_full[0], down_full[0], source_norm_two, unit_small[0]
    )
    source_last = source_mid + (branch + vector_full[23])
    encoder_output = norm_rows(source_last, 2)
    memory = moves.gather(encoder_output.astype(BF16))
    branch, self_state = attention_forward(
        moves,
        attn_full[1],
        target_norm_one,
        target_norm_one,
        head_small[2],
        head_small[3],
        self_layout,
        True,
    )
    target_mid = target + (branch + vector_full[21])
    target_norm_two = gather_norm(target_mid, 4)
    branch, cross_state = attention_forward(
        moves,
        attn_full[2],
        target_norm_two,
        memory,
        head_small[4],
        head_small[5],
        cross_layout,
        False,
    )
    target_cross = target_mid + (branch + vector_full[22])
    target_norm_three = gather_norm(target_cross, 5)
    branch, target_ffn_state = feed_forward(
        moves, up_full[1], down_full[1], target_norm_three, unit_small[1]
    )
    target_last = target_cross + (branch + vector_full[24])
    decoder_output = norm_rows(target_last, 6)

    def back_norm(hidden, index, upstream):
        return norm_back(hidden, vector_full[index], vector_full[7 + index], upstream)

    half = D // 2

    def reduce_weight(gradient):
        return split.scatter(gradient[:half], gradient[half:])

    flow_grad, gain_six, offset_six = back_norm(target_last, 6, target_cotangent)
    target_ffn_back = feed_backward(
        moves, up_full[1], down_full[1], flow_grad, target_ffn_state, target_norm_three
    )
    up_grad_one = reduce_weight(target_ffn_back[1])
    down_grad_one = reduce_weight(target_ffn_back[2])
    extra_grad, gain_five, offset_five = back_norm(target_cross, 5, target_ffn_back[0])
    flow_grad = flow_grad + extra_grad
    cross_back = attention_backward(
        moves, attn_full[2], flow_grad, cross_state, target_norm_two, memory, cross_layout, False
    )
    attn_grad_two = reduce_weight(cross_back[2])
    extra_grad, gain_four, offset_four = back_norm(target_mid, 4, cross_back[0])
    flow_grad = flow_grad + extra_grad
    memory_total = source_cotangent + cross_back[1]
    source_flow, gain_two, offset_two = back_norm(source_last, 2, memory_total)
    source_ffn_back = feed_backward(
        moves, up_full[0], down_full[0], source_flow, source_ffn_state, source_norm_two
    )
    up_grad_zero = reduce_weight(source_ffn_back[1])
    down_grad_zero = reduce_weight(source_ffn_back[2])
    self_back = attention_backward(
        moves,
        attn_full[1],
        flow_grad,
        self_state,
        target_norm_one,
        target_norm_one,
        self_layout,
        True,
    )
    attn_grad_one = reduce_weight(self_back[2])
    extra_grad, gain_three, offset_three = back_norm(target, 3, self_back[0])
    target_grad = flow_grad + extra_grad
    extra_grad, gain_one, offset_one = back_norm(source_mid, 1, source_ffn_back[0])
    source_flow = source_flow + extra_grad
    source_back = attention_backward(
        moves,
        attn_full[0],
        source_flow,
        source_attn_state,
        source_norm_one,
        source_norm_one,
        encoder_layout,
        False,
    )
    attn_grad_zero = reduce_weight(source_back[2])
    extra_grad, gain_zero, offset_zero = back_norm(source, 0, source_back[0])
    source_grad = source_flow + extra_grad

    wide_rows = jnp.stack(
        [
            gain_zero,
            gain_one,
            gain_two,
            gain_three,
            gain_four,
            gain_five,
            gain_six,
            offset_zero,
            offset_one,
            offset_two,
            offset_three,
            offset_four,
            offset_five,
            offset_six,
            source_back[5],
            self_back[5],
            cross_back[5],
            source_ffn_back[4],
            target_ffn_back[4],
        ]
    )
    wide_blocks = wide_rows.reshape(19, split.count, shard_rows).transpose(1, 0, 2)
    head_rows = jnp.stack(
        [
            source_back[3],
            source_back[4],
            self_back[3],
            self_back[4],
            cross_back[3],
            cross_back[4],
        ]
    )
    unit_rows = jnp.stack([source_ffn_back[3], target_ffn_back[3]])
    head_cut = head_rows.reshape(6, head_blocks, shard_rows).transpose(1, 0, 2)
    unit_cut = unit_rows.reshape(2, unit_blocks, shard_units).transpose(1, 0, 2)
    unit_cut = unit_cut.reshape(unit_blocks, -1, shard_rows)
    head_part = jnp.zeros((split.count, 6, shard_rows), F32)
    unit_part = jnp.zeros((split.count,) + unit_cut.shape[1:], F32)
    for index in range(head_blocks):
        where = split.place(moves.me * head_blocks + index)
        head_part = lax.dynamic_update_index_in_dim(head_part, head_cut[index], where, 0)
    for index in range(unit_blocks):
        where = split.place(moves.me * unit_blocks + index)
        unit_part = lax.dynamic_update_index_in_dim(unit_part, unit_cut[index], where, 0)
    small_part = jnp.concatenate(
        [wide_blocks[:, :14], head_part, wide_blocks[:, 14:], unit_part], axis=1
    )
    small_sum = split.spread(moves.total(small_part))[0]
    vector_grad = small_sum[:25]
    unit_grad = small_sum[25:].reshape(2, shard_units)

    weight_sums = (
        attn_grad_zero,
        attn_grad_one,
        attn_grad_two,
        up_grad_zero,
        up_grad_one,
        down_grad_zero,
        down_grad_one,
    )
    local_squares = sum([jnp.sum(gradient * gradient) for gradient in weight_sums])
    small_squares = jnp.sum(small_sum * small_sum)
    square_sum = split.total(moves.total(local_squares.reshape(1, 1)) + small_squares)
    grad_norm = jnp.sqrt(square_sum)[0, 0]
    factor = jnp.minimum(1.0, CLIP_NORM / (grad_norm + 1e-06))
    attn_in_grad = jnp.stack(
        [
            jnp.stack(
                [
                    gradient[:, which * head_width : (which + 1) * head_width]
                    for which in range(3)
                ]
            )
            for gradient in weight_sums[:3]
        ]
    )
    attn_out_grad = jnp.stack([gradient[:, 3 * head_width :].T for gradient in weight_sums[:3]])
    params = (attention_in, attention_out, hidden_in, hidden_out, vectors, hidden_bias)
    gradients = (
        attn_in_grad,
        attn_out_grad,
        jnp.stack([up_grad_zero, up_grad_one]),
        jnp.stack([down_grad_zero.T, down_grad_one.T]),
        vector_grad,
        unit_grad,
    )
    firsts = (
        first_attention_in,
        first_attention_out,
        first_hidden_in,
        first_hidden_out,
        first_vectors,
        first_hidden_bias,
    )
    seconds = (
        second_attention_in,
        second_attention_out,
        second_hidden_in,
        second_hidden_out,
        second_vectors,
        second_hidden_bias,
    )
    rates = (
        0.5 * D ** (-0.5),
        0.5 * (D // 8) ** (-0.5),
        0.5 * D ** (-0.5),
        0.5 * FF ** (-0.5),
        0.3,
        0.3,
    )
    decays = (MATRIX_DECAY, MATRIX_DECAY, MATRIX_DECAY, MATRIX_DECAY, 0.0, 0.0)
    results = []
    for weight, gradient, first_old, second_old, step_rate, decay_rate in zip(
        params, gradients, firsts, seconds, rates, decays
    ):
        clipped = gradient * factor
        moment = BETA_FIRST * first_old + (1.0 - BETA_FIRST) * clipped
        second_new = BETA_SECOND * second_old + (1.0 - BETA_SECOND) * clipped * clipped
        fixed_first = moment / (1.0 - BETA_FIRST**STEP)
        fixed_second = second_new / (1.0 - BETA_SECOND**STEP)
        updated = weight - step_rate * (
            fixed_first / (jnp.sqrt(fixed_second) + ADAM_EPS) + decay_rate * weight
        )
        results.append(clipped)
        results.append(second_new)
        results.append(updated)
    return (
        split.leave(encoder_output),
        split.leave(decoder_output),
        split.leave(source_grad),
        split.leave(target_grad),
        grad_norm,
        results[0],
        results[1],
        results[2],
        results[3],
        results[4],
        results[5],
        results[6],
        results[7],
        results[8],
        results[9],
        results[10],
        results[11],
        results[12],
        results[13],
        results[14],
        results[15],
        results[16],
        results[17],
        results[12][23:25],
    )


def solution(mesh):
    placed = (
        P(("dp", "tensor"), None),
        P(("dp", "tensor"), None),
        P("dp", None),
        P("dp", None),
        P("dp"),
        P(("dp", "tensor"), None),
        P(("dp", "tensor"), None),
        P(None, None, "dp", "tensor"),
        P(None, "tensor", "dp"),
        P(None, "dp", "tensor"),
        P(None, "tensor", "dp"),
        P(None, "dp"),
        P(None, "dp"),
        P(None, None, "dp", "tensor"),
        P(None, "tensor", "dp"),
        P(None, "dp", "tensor"),
        P(None, "tensor", "dp"),
        P(None, "dp"),
        P(None, "dp"),
        P(None, None, "dp", "tensor"),
        P(None, "tensor", "dp"),
        P(None, "dp", "tensor"),
        P(None, "tensor", "dp"),
        P(None, "dp"),
        P(None, "dp"),
    )
    return jax.shard_map(
        body,
        mesh=mesh,
        in_specs=placed,
        out_specs=(
            P(("dp", "tensor"), None),
            P(("dp", "tensor"), None),
            P(("dp", "tensor"), None),
            P(("dp", "tensor"), None),
            P(),
            P(None, None, "dp", "tensor"),
            P(None, None, "dp", "tensor"),
            P(None, None, "dp", "tensor"),
            P(None, "tensor", "dp"),
            P(None, "tensor", "dp"),
            P(None, "tensor", "dp"),
            P(None, "dp", "tensor"),
            P(None, "dp", "tensor"),
            P(None, "dp", "tensor"),
            P(None, "tensor", "dp"),
            P(None, "tensor", "dp"),
            P(None, "tensor", "dp"),
            P(None, "dp"),
            P(None, "dp"),
            P(None, "dp"),
            P(None, "dp"),
            P(None, "dp"),
            P(None, "dp"),
            P(None, "dp"),
        ),
        check_vma=False,
    )
```

```python
from functools import partial

import jax
import jax.numpy as jnp
from jax import lax
from jax.experimental import pallas as pl
from jax.experimental.pallas import tpu as pltpu
from jax.sharding import PartitionSpec as P

D = 1024
FF = 4096
L = 1024
ITEMS = 8
STEP = 10
HEAD = 64
ITEM = 128


NORM_EPS = 1e-05
CLIP_NORM = 1.0
BETA_FIRST = 0.9
BETA_SECOND = 0.999
ADAM_EPS = 1e-08
MATRIX_DECAY = 0.01
MASKED = -1e30

BF16 = jnp.bfloat16
F32 = jnp.float32
VMEM_BYTES = 32 * 1024 * 1024


class TensorMoves:
    def __init__(self):
        self.count = lax.axis_size("tensor")
        assert self.count == 4
        self.me = lax.axis_index("tensor")

    def swap(self, values, bit):
        pairs = [(index, index ^ bit) for index in range(self.count)]
        return lax.ppermute(values, "tensor", pairs)

    def gather(self, shard):
        far = self.swap(shard, 2)
        near = self.swap(shard, 1)
        return shard, near, far, self.swap(far, 1)

    def scatter(self, near_part, far_part):
        far_in = self.swap(far_part[0], 1)
        near_in = self.swap(near_part[0], 1)
        crossing = (far_part[1] + far_in.astype(F32)).astype(BF16)
        arrived = self.swap(crossing, 2)
        return near_part[1], near_in, arrived

    def total(self, values):
        values = values + self.swap(values, 1)
        return values + self.swap(values, 2)


class PlainRows:
    def __init__(self):
        self.count = lax.axis_size("dp")
        self.me = lax.axis_index("dp")
        self.y = None

    def turn(self, stacked):
        return stacked

    def gather(self, shard):
        full = lax.all_gather(shard, "dp", axis=0, tiled=True)
        half = full.shape[0] // 2
        return full[:half], full[half:]

    def stack(self, shard):
        return lax.all_gather(shard, "dp", axis=0)

    def scatter(self, far_part, near_part):
        values = jnp.concatenate([near_part, far_part.astype(F32)], 0)
        return lax.psum_scatter(values, "dp", scatter_dimension=0, tiled=True)

    def total(self, values):
        return lax.psum(values, "dp")


class CrossRows(PlainRows):
    ALONG_Z = [[0, 2, 4, 6], [1, 3, 5, 7]]

    def __init__(self):
        super().__init__()
        self.z = self.me // 2
        self.y = self.me % 2

    def turn(self, stacked):
        near, far = stacked[:4], stacked[4:]
        even = self.y == 0
        pairs = jnp.stack([jnp.where(even, near, far), jnp.where(even, far, near)], axis=1)
        return pairs.reshape(stacked.shape)

    def swap(self, values, bits):
        pairs = [(index, index ^ bits) for index in range(self.count)]
        return lax.ppermute(values, "dp", pairs)

    def gather(self, shard):
        near = lax.all_gather(shard, "dp", axis=0, tiled=True, axis_index_groups=self.ALONG_Z)
        return near, self.swap(near, 1)

    def stack(self, shard):
        pieces = jnp.stack([shard] + [self.swap(shard, bits) for bits in (2, 4, 6)])
        near = jnp.stack(
            [lax.dynamic_index_in_dim(pieces, self.z ^ index, 0, False) for index in range(4)]
        )
        return jnp.concatenate([near, self.swap(near, 1)], axis=0)

    def scatter(self, far_part, near_part):
        part = (near_part + self.swap(far_part, 1).astype(F32)).astype(BF16)
        return lax.psum_scatter(
            part, "dp", scatter_dimension=0, tiled=True, axis_index_groups=self.ALONG_Z
        )

    def total(self, values):
        for bits in (1, 2, 4):
            values = values + self.swap(values, bits)
        return values


def item_codes(row_kind, lengths, places):
    items = jnp.where(row_kind == 1, 0, places // ITEM)
    within = jnp.where(row_kind == 1, places, places % ITEM)
    limit = jnp.zeros_like(places)
    for index in range(ITEMS):
        limit = jnp.where(items == index, lengths[index], limit)
    return items, jnp.where(within < limit, items, -1)


def dot_nn(left, right):
    return jnp.dot(left, right, preferred_element_type=F32)


def dot_nt(left, right):
    return lax.dot_general(left, right, (((1,), (1,)), ((), ())), preferred_element_type=F32)


def dot_tn(left, right):
    return lax.dot_general(left, right, (((0,), (0,)), ((), ())), preferred_element_type=F32)


def wide_dot(rows, near, far):
    half = near.shape[0]
    return dot_nn(rows[:, :half], near) + dot_nn(rows[:, half:], far)


def kernel_call(kernel, grid, in_specs, out_specs, out_shapes, scratch, flops, moved, name):
    return pl.pallas_call(
        kernel,
        grid=grid,
        in_specs=in_specs,
        out_specs=out_specs,
        out_shape=out_shapes,
        scratch_shapes=scratch,
        compiler_params=pltpu.CompilerParams(
            vmem_limit_bytes=VMEM_BYTES,
            dimension_semantics=("arbitrary",) * len(grid),
        ),
        cost_estimate=pl.CostEstimate(flops=flops, bytes_accessed=moved, transcendentals=0),
        name=name,
    )


def whole(shape):
    return pl.BlockSpec(shape, lambda step: (0,) * len(shape))


def pair_bias(key_codes, query_codes, key_places, query_places, causal):
    allowed = key_codes == query_codes
    if causal:
        allowed = allowed & (key_places <= query_places)
    return jnp.where(allowed, 0.0, MASKED).astype(F32)


def head_rows_only(block, head, scale=None):
    lanes = lax.broadcasted_iota(jnp.int32, block.shape, 1) // HEAD
    if scale is not None:
        block = block * jnp.asarray(scale, block.dtype)
    return jnp.where(lanes == head, block, jnp.zeros_like(block))


def over_keys(combine, values):
    parts = values.reshape(8, values.shape[0] // 8, values.shape[1])
    return combine(combine(parts, axis=0), axis=0, keepdims=True)


def attend_block(queries, key_rows, values_turned, bias, heads):
    scores = []
    for head in range(heads):
        picked = head_rows_only(queries, head, HEAD ** (-0.5))
        scores.append(dot_nt(key_rows, picked) + bias)
    largest = [over_keys(jnp.max, score) for score in scores]
    contexts = []
    totals = []
    for head in range(heads):
        weights = jnp.exp(scores[head] - largest[head])
        total = over_keys(jnp.sum, weights)
        context = dot_nn(
            values_turned[head * HEAD : (head + 1) * HEAD, :], weights.astype(BF16)
        )
        contexts.append(context * (1.0 / total))
        totals.append(largest[head] + jnp.log(total))
    return jnp.concatenate(contexts, axis=0).T, jnp.concatenate(totals, axis=0)


def out_parts(context, out_near, out_far, step, send_ref, keep_ref):
    half = out_near.shape[0]
    near = dot_nt(context, out_near)
    far = dot_nt(context, out_far)

    @pl.when(step == 0)
    def _():
        send_ref[:, :half] = near.astype(BF16)
        send_ref[:, half:] = far.astype(BF16)

    @pl.when(step == 1)
    def _():
        keep_ref[:, :half] = near
        keep_ref[:, half:] = far


def attend_tail(
    step, qkv_ref, turned_ref, codes, causal, out_near, out_far, first_row, outs, heads
):
    key_code_ref, query_code_ref, key_place_ref, query_place_ref = codes
    context_ref, total_ref, send_ref, keep_ref = outs
    rows = send_ref.shape[0]
    wide = context_ref.shape[1]
    start = pl.multiple_of(first_row + (1 - step) * rows, rows)
    bias = pair_bias(
        key_code_ref[...], query_code_ref[...], key_place_ref[...], query_place_ref[...], causal
    )
    context, totals = attend_block(
        qkv_ref[pl.ds(start, rows), :wide],
        qkv_ref[:, wide : 2 * wide],
        turned_ref[...],
        bias,
        heads,
    )
    context = context.astype(BF16)
    context_ref[...] = context
    total_ref[...] = totals
    out_parts(context, out_near, out_far, step, send_ref, keep_ref)


def attend_far_kernel(causal, is_cross, heads, *refs):
    normed_refs = memory_refs = refs[:4]
    refs = refs[4:]
    if is_cross:
        memory_refs, refs = refs[:4], refs[4:]
    full_near_ref, full_far_ref, bias_ref = refs[:3]
    codes = refs[3:7]
    qkv_ref, context_ref, total_ref, send_ref, keep_ref, turned_ref = refs[7:]
    step = pl.program_id(0)
    rows = send_ref.shape[0]
    wide = context_ref.shape[1]

    @pl.when(step == 0)
    def _():
        def project(source_refs, begin, end, biases):
            for index in range(4):
                part = source_refs[index][...]
                values = wide_dot(part, full_near_ref[:, begin:end], full_far_ref[:, begin:end])
                span = slice(index * rows, (index + 1) * rows)
                for place, which in enumerate(range(begin // wide, end // wide)):
                    piece = values[:, place * wide : (place + 1) * wide]
                    if biases[which] is not None:
                        piece = piece + bias_ref[biases[which] : biases[which] + 1, :]
                    qkv_ref[span, which * wide : (which + 1) * wide] = piece.astype(BF16)

        biases = (0, None, 1)
        if is_cross:
            project(normed_refs, 0, wide, biases)
            project(memory_refs, wide, 3 * wide, biases)
        else:
            project(normed_refs, 0, 3 * wide, biases)
        turned_ref[...] = qkv_ref[:, 2 * wide :].T

    attend_tail(
        step,
        qkv_ref,
        turned_ref,
        codes,
        causal,
        full_near_ref[:, 3 * wide :],
        full_far_ref[:, 3 * wide :],
        2 * rows,
        (context_ref, total_ref, send_ref, keep_ref),
        heads,
    )


def attend_near_kernel(causal, heads, *refs):
    qkv_ref, out_near_ref, out_far_ref = refs[:3]
    codes = refs[3:7]
    context_ref, total_ref, send_ref, keep_ref, turned_ref = refs[7:]
    step = pl.program_id(0)
    wide = context_ref.shape[1]

    @pl.when(step == 0)
    def _():
        turned_ref[...] = qkv_ref[:, 2 * wide :].T

    attend_tail(
        step,
        qkv_ref,
        turned_ref,
        codes,
        causal,
        out_near_ref[...],
        out_far_ref[...],
        0,
        (context_ref, total_ref, send_ref, keep_ref),
        heads,
    )


def attention_forward(moves, full, normed, memory, biases, layout, causal):
    key_codes, query_codes, key_places, query_places = layout
    length = key_codes.shape[0]
    rows = length // 4
    width = full[0].shape[1]
    wide = width // 4
    heads = wide // HEAD
    half = full[0].shape[0]
    is_cross = memory is not normed
    sources = tuple(normed) + (tuple(memory) if is_cross else ())
    pairs = 4 * rows * length // 2 * wide * heads

    def code_specs(first):
        return [
            whole((length, 1)),
            pl.BlockSpec((1, rows), lambda step: (0, first + 1 - step)),
            whole((length, 1)),
            pl.BlockSpec((1, rows), lambda step: (0, first + 1 - step)),
        ]

    half_outs = [
        jax.ShapeDtypeStruct((2 * rows, wide), BF16),
        jax.ShapeDtypeStruct((heads, 2 * rows), F32),
        jax.ShapeDtypeStruct((rows, 2 * half), BF16),
        jax.ShapeDtypeStruct((rows, 2 * half), F32),
    ]
    half_specs = [
        pl.BlockSpec((rows, wide), lambda step: (1 - step, 0)),
        pl.BlockSpec((heads, rows), lambda step: (0, 1 - step)),
        whole((rows, 2 * half)),
        whole((rows, 2 * half)),
    ]
    turned = pltpu.VMEM((wide, length), BF16)
    codes = (key_codes, query_codes, key_places, query_places)
    qkv, context_far, totals_far, send_far, keep_far = kernel_call(
        partial(attend_far_kernel, causal, is_cross, heads),
        (2,),
        [whole((rows, 2 * half))] * len(sources)
        + [whole((half, width))] * 2
        + [whole(biases.shape)]
        + code_specs(2),
        [whole((length, 3 * wide))] + half_specs,
        [jax.ShapeDtypeStruct((length, 3 * wide), BF16)] + half_outs,
        [turned],
        2 * length * 2 * half * 3 * wide + pairs,
        12 * length * 2 * half,
        "attend_far",
    )(*sources, *full, biases, *codes)
    context_near, totals_near, send_near, keep_near = kernel_call(
        partial(attend_near_kernel, causal, heads),
        (2,),
        [whole((length, 3 * wide))]
        + [pl.BlockSpec((half, wide), lambda step: (0, 3))] * 2
        + code_specs(0),
        half_specs,
        half_outs,
        [turned],
        pairs,
        6 * length * 2 * half,
        "attend_near",
    )(qkv, *full, *codes)
    branch = moves.scatter((send_near, keep_near), (send_far, keep_far))
    return branch, (qkv, (context_near, context_far), (totals_near, totals_far))


def attend_back_kernel(causal, heads, *refs):
    grad_refs, (out_near_ref, out_far_ref, qkv_ref) = refs[:4], refs[4:7]
    context_refs, total_refs = refs[7:9], refs[9:11]
    key_code_ref, query_code_ref, key_place_ref, query_place_ref = refs[11:15]
    grads_ref, sums_ref = refs[15:17]
    keys_turned_ref, key_sum_ref, value_sum_ref, grad_ref, context_ref, total_ref = refs[17:]
    step = pl.program_id(0)
    rows = context_ref.shape[0]
    wide = context_ref.shape[1]
    scale = HEAD ** (-0.5)

    @pl.when(step == 0)
    def _():
        keys_turned_ref[...] = qkv_ref[:, wide : 2 * wide].T
        key_sum_ref[...] = jnp.zeros_like(key_sum_ref)
        value_sum_ref[...] = jnp.zeros_like(value_sum_ref)

    for index in range(4):

        @pl.when(step == index)
        def _(index=index):
            span = slice((index % 2) * rows, (index % 2 + 1) * rows)
            grad_ref[...] = grad_refs[index][...]
            context_ref[...] = context_refs[index // 2][span, :]
            total_ref[...] = total_refs[index // 2][:, span]

    context_grad = wide_dot(grad_ref[...], out_near_ref[...], out_far_ref[...]).astype(BF16)
    products = (context_grad.astype(F32) * context_ref[...].astype(F32)).T
    bias = pair_bias(
        key_code_ref[...], query_code_ref[...], key_place_ref[...], query_place_ref[...], causal
    )
    start = pl.multiple_of(step * rows, rows)
    queries = qkv_ref[pl.ds(start, rows), :wide]
    key_rows = qkv_ref[:, wide : 2 * wide]
    value_rows = qkv_ref[:, 2 * wide :]
    query_grads = []
    for head in range(heads):
        span = slice(head * HEAD, (head + 1) * HEAD)
        picked = head_rows_only(queries, head, scale)
        picked_grad = head_rows_only(context_grad, head)
        scores = dot_nt(key_rows, picked) + bias
        weights = jnp.exp(scores - total_ref[head : head + 1, :])
        weight_grad = dot_nt(value_rows, picked_grad)
        diagonal = jnp.sum(products[span, :], axis=0, keepdims=True)
        score_grad = (weights * (weight_grad - diagonal)).astype(BF16)
        value_sum_ref[...] += dot_nn(weights.astype(BF16), picked_grad)
        key_sum_ref[...] += dot_nn(score_grad, picked)
        query_grads.append(dot_nn(keys_turned_ref[span, :], score_grad))
    query_grad = jnp.concatenate(query_grads, axis=0).T * scale
    grads_ref[pl.ds(start, rows), :wide] = query_grad.astype(BF16)

    @pl.when(step == 3)
    def _():
        grads_ref[:, wide : 2 * wide] = key_sum_ref[...].astype(BF16)
        grads_ref[:, 2 * wide :] = value_sum_ref[...].astype(BF16)
        for place, begin in ((0, 0), (1, 2 * wide)):
            values = grads_ref[:, begin : begin + wide].astype(F32)
            sums_ref[place : place + 1, :] = jnp.sum(values, axis=0, keepdims=True)


def spread_kernel(begin, end, rows_ref, near_ref, far_ref, send_ref, keep_ref):
    step = pl.program_id(0)
    part = rows_ref[:, begin:end]
    out_parts(part, near_ref[:, begin:end], far_ref[:, begin:end], step, send_ref, keep_ref)


def spread_rows(moves, grads, full, begin, end):
    rows = grads.shape[0] // 4
    half = full[0].shape[0]
    wide = grads.shape[1]
    parts = []
    for first in (2, 0):
        parts.append(
            kernel_call(
                partial(spread_kernel, begin, end),
                (2,),
                [pl.BlockSpec((rows, wide), lambda step, first=first: (first + 1 - step, 0))]
                + [whole((half, wide))] * 2,
                [whole((rows, 2 * half))] * 2,
                [
                    jax.ShapeDtypeStruct((rows, 2 * half), BF16),
                    jax.ShapeDtypeStruct((rows, 2 * half), F32),
                ],
                [],
                4 * rows * 2 * half * (end - begin),
                6 * rows * 2 * half + 4 * half * wide,
                "spread_rows",
            )(grads, *full)
        )
    return moves.scatter(parts[1], parts[0])


def rows_dot(left_refs, right, begin, end):
    total = None
    for index, left_ref in enumerate(left_refs):
        rows = left_ref.shape[0]
        if isinstance(right, tuple):
            first = (index % 2) * rows
            part = right[index // 2][first : first + rows, begin:end]
        else:
            part = right[index * rows : (index + 1) * rows, begin:end]
        product = dot_tn(left_ref[...], part)
        total = product if total is None else total + product
    return total


def attention_weight_kernel(is_cross, *refs):
    normed_refs = memory_refs = refs[:4]
    refs = refs[4:]
    if is_cross:
        memory_refs, refs = refs[:4], refs[4:]
    upstream_refs, grads_ref, context_refs, outs = refs[:4], refs[4], refs[5:7], refs[7:]
    send_ref, keep_ref = outs
    step = pl.program_id(0)
    wide = context_refs[0].shape[1]
    if is_cross:
        pieces = [
            rows_dot(normed_refs, grads_ref, 0, wide),
            rows_dot(memory_refs, grads_ref, wide, 3 * wide),
        ]
    else:
        pieces = [rows_dot(normed_refs, grads_ref, 0, 3 * wide)]
    pieces.append(rows_dot(upstream_refs, tuple(context_refs), 0, wide))

    @pl.when(step == 0)
    def _():
        send_ref[...] = jnp.concatenate(pieces, axis=1).astype(BF16)

    @pl.when(step == 1)
    def _():
        keep_ref[...] = jnp.concatenate(pieces, axis=1)


def attention_weights(normed, memory, upstream, grads, contexts):
    rows, width = normed[0].shape
    wide = contexts[0].shape[1]
    is_cross = memory is not normed
    sources = tuple(normed) + (tuple(memory) if is_cross else ()) + tuple(upstream)
    half = width // 2
    outs = (half, 4 * wide)
    return kernel_call(
        partial(attention_weight_kernel, is_cross),
        (2,),
        [pl.BlockSpec((rows, half), lambda step: (0, 1 - step))] * len(sources)
        + [whole(grads.shape)]
        + [whole((2 * rows, wide))] * 2,
        [whole(outs)] * 2,
        [jax.ShapeDtypeStruct(outs, BF16), jax.ShapeDtypeStruct(outs, F32)],
        [],
        8 * rows * width * 4 * wide,
        2 * rows * width * (len(sources) + 4) + 6 * half * 4 * wide,
        "attention_weights",
    )(*sources, grads, *contexts)


def attention_backward(moves, full, upstream, stored, normed, memory, layout, causal):
    qkv, contexts, totals = stored
    key_codes, query_codes, key_places, query_places = layout
    length = qkv.shape[0]
    rows = length // 4
    wide = qkv.shape[1] // 3
    heads = wide // HEAD
    half = full[0].shape[0]
    is_cross = memory is not normed
    upstream_rows = moves.gather(upstream)
    query_spec = pl.BlockSpec((1, rows), lambda step: (0, step))
    grads, sums = kernel_call(
        partial(attend_back_kernel, causal, heads),
        (4,),
        [whole((rows, 2 * half))] * 4
        + [pl.BlockSpec((half, wide), lambda step: (0, 3))] * 2
        + [whole(qkv.shape)]
        + [whole((2 * rows, wide))] * 2
        + [whole((heads, 2 * rows))] * 2
        + [whole((length, 1)), query_spec, whole((length, 1)), query_spec],
        [whole(qkv.shape), whole((2, wide))],
        [jax.ShapeDtypeStruct(qkv.shape, BF16), jax.ShapeDtypeStruct((2, wide), F32)],
        [
            pltpu.VMEM((wide, length), BF16),
            pltpu.VMEM((length, wide), F32),
            pltpu.VMEM((length, wide), F32),
            pltpu.VMEM((rows, 2 * half), BF16),
            pltpu.VMEM((rows, wide), BF16),
            pltpu.VMEM((heads, rows), F32),
        ],
        10 * length * length * wide * heads,
        12 * length * 2 * half,
        "attend_back",
    )(*upstream_rows, *full, qkv, *contexts, *totals, *layout)
    if is_cross:
        memory_grad = spread_rows(moves, grads, full, wide, 3 * wide)
        normed_grad = spread_rows(moves, grads, full, 0, wide)
    else:
        memory_grad = None
        normed_grad = spread_rows(moves, grads, full, 0, 3 * wide)
    weight_parts = attention_weights(normed, memory, upstream_rows, grads, contexts)
    return normed_grad, memory_grad, weight_parts, sums


GELU_SCALE = 0.7978845608028654
GELU_CUBE = 0.044715


def feed_kernel(own_ref, near_ref, up_near, up_far, down_near, down_far, bias_ref, *outs):
    activated_ref, slope_ref, send_ref, keep_ref = outs
    step = pl.program_id(0)
    rows = jnp.where(step == 0, near_ref[...], own_ref[...])
    pre_act = wide_dot(rows, up_near[...], up_far[...]) + bias_ref[...]
    square = pre_act * pre_act
    bent = jnp.tanh(GELU_SCALE * pre_act * (1.0 + GELU_CUBE * square))
    activated = (0.5 * pre_act * (1.0 + bent)).astype(BF16)
    inner = GELU_SCALE * (1.0 + 3.0 * GELU_CUBE * square)
    slope = 0.5 * (1.0 + bent) + 0.5 * pre_act * (1.0 - bent * bent) * inner
    activated_ref[...] = activated
    slope_ref[...] = slope.astype(BF16)
    out_parts(activated, down_near[...], down_far[...], step, send_ref, keep_ref)


def feed_forward(moves, up_full, down_full, normed, unit_bias):
    rows = normed[0].shape[0]
    half, units = up_full[0].shape
    states = []
    parts = []
    for pair_rows in (normed[:2], normed[2:]):
        activated, slope, send, keep = kernel_call(
            feed_kernel,
            (2,),
            [whole((rows, 2 * half))] * 2 + [whole((half, units))] * 4 + [whole((1, units))],
            [pl.BlockSpec((rows, units), lambda step: (1 - step, 0))] * 2
            + [whole((rows, 2 * half))] * 2,
            [jax.ShapeDtypeStruct((2 * rows, units), BF16)] * 2
            + [
                jax.ShapeDtypeStruct((rows, 2 * half), BF16),
                jax.ShapeDtypeStruct((rows, 2 * half), F32),
            ],
            [],
            16 * rows * half * units,
            20 * rows * units + 8 * half * units,
            "feed_forward",
        )(*pair_rows, *up_full, *down_full, unit_bias)
        states.append((activated, slope))
        parts.append((send, keep))
    return moves.scatter(*parts), states


def feed_back_kernel(
    own_ref, near_ref, slope_ref, up_near, up_far, down_near, down_far, *outs
):
    grad_ref, sum_ref, send_ref, keep_ref = outs
    step = pl.program_id(0)
    rows = jnp.where(step == 0, near_ref[...], own_ref[...])
    act_grad = wide_dot(rows, down_near[...], down_far[...])
    pre_grad = (act_grad * slope_ref[...].astype(F32)).astype(BF16)
    grad_ref[...] = pre_grad

    @pl.when(step == 0)
    def _():
        sum_ref[...] = jnp.zeros_like(sum_ref)

    sum_ref[...] += jnp.sum(pre_grad.astype(F32), axis=0, keepdims=True)
    out_parts(pre_grad, up_near[...], up_far[...], step, send_ref, keep_ref)


def feed_weight_kernel(*refs):
    left_refs, right_refs, (send_ref, keep_ref) = refs[:4], refs[4:6], refs[6:]
    step = pl.program_id(0)
    part = rows_dot(left_refs, tuple(right_refs), 0, send_ref.shape[1])

    @pl.when(step == 0)
    def _():
        send_ref[...] = part.astype(BF16)

    @pl.when(step == 1)
    def _():
        keep_ref[...] = part


def feed_weights(left, right):
    rows, width = left[0].shape
    units = right[0].shape[1]
    half = width // 2
    outs = (half, units)
    return kernel_call(
        feed_weight_kernel,
        (2,),
        [pl.BlockSpec((rows, half), lambda step: (0, 1 - step))] * 4
        + [whole((2 * rows, units))] * 2,
        [whole(outs)] * 2,
        [jax.ShapeDtypeStruct(outs, BF16), jax.ShapeDtypeStruct(outs, F32)],
        [],
        8 * rows * width * units,
        8 * rows * (width + units) + 6 * half * units,
        "feed_weights",
    )(*left, *right)


def feed_backward(moves, up_full, down_full, upstream, states, normed):
    rows = normed[0].shape[0]
    half, units = up_full[0].shape
    upstream_rows = moves.gather(upstream)
    pre_grads = []
    sums = []
    parts = []
    for pair_rows, (unused, slope) in zip((upstream_rows[:2], upstream_rows[2:]), states):
        pre_grad, unit_sum, send, keep = kernel_call(
            feed_back_kernel,
            (2,),
            [whole((rows, 2 * half))] * 2
            + [pl.BlockSpec((rows, units), lambda step: (1 - step, 0))]
            + [whole((half, units))] * 4,
            [pl.BlockSpec((rows, units), lambda step: (1 - step, 0)), whole((1, units))]
            + [whole((rows, 2 * half))] * 2,
            [
                jax.ShapeDtypeStruct((2 * rows, units), BF16),
                jax.ShapeDtypeStruct((1, units), F32),
                jax.ShapeDtypeStruct((rows, 2 * half), BF16),
                jax.ShapeDtypeStruct((rows, 2 * half), F32),
            ],
            [],
            16 * rows * half * units,
            20 * rows * units + 8 * half * units,
            "feed_backward",
        )(*pair_rows, slope, *up_full, *down_full)
        pre_grads.append(pre_grad)
        sums.append(unit_sum)
        parts.append((send, keep))
    normed_grad = moves.scatter(*parts)
    up_parts = feed_weights(normed, pre_grads)
    down_parts = feed_weights(upstream_rows, [activated for activated, unused in states])
    return normed_grad, up_parts, down_parts, sums[0] + sums[1]


class Norms:
    def __init__(self, table, y):
        self.table = table
        self.y = jnp.zeros((1,), jnp.int32) if y is None else y.astype(jnp.int32).reshape(1)
        self.ordered = y is None

    def enter(self, flag, values):
        if self.ordered:
            return values
        size = values.shape[1] // 8
        blocks = [values[:, index * size : (index + 1) * size] for index in range(8)]
        first = jnp.concatenate(blocks[0::2], axis=1)
        second = jnp.concatenate(blocks[1::2], axis=1)
        return jnp.concatenate(
            [jnp.where(flag == 0, first, second), jnp.where(flag == 0, second, first)], axis=1
        )

    def leave(self, flag, values):
        if self.ordered:
            return values
        half = values.shape[1] // 2
        near, far = values[:, :half], values[:, half:]
        first = jnp.where(flag == 0, near, far)
        second = jnp.where(flag == 0, far, near)
        size = half // 4
        blocks = []
        for index in range(4):
            span = slice(index * size, (index + 1) * size)
            blocks += [first[:, span], second[:, span]]
        return jnp.concatenate(blocks, axis=1)

    def call(self, kernel, operands, outs, name):
        rows, width = operands[0].shape
        block = rows // 4

        def spec(shape):
            if shape[0] == rows:
                return pl.BlockSpec((block, width), lambda step: (step, 0))
            return whole(shape)

        return kernel_call(
            kernel,
            (4,),
            [pl.BlockSpec(memory_space=pltpu.SMEM)]
            + [spec(operand.shape) for operand in operands]
            + [whole(self.table.shape)],
            [spec(out.shape) for out in outs],
            outs,
            [],
            20 * rows * width,
            sum(operand.size * operand.dtype.itemsize for operand in (*operands, *outs)),
            name,
        )(self.y, *operands, self.table)

    def forward(self, index, base, parts=(), bias=None, low=True, full=False):
        shape = base.shape
        entering = not parts
        outs = [jax.ShapeDtypeStruct(shape, F32)]
        if low:
            outs.append(jax.ShapeDtypeStruct(shape, BF16))
        if full:
            outs.append(jax.ShapeDtypeStruct(shape, F32))

        def kernel(flag_ref, base_ref, *refs):
            part_refs, table_ref, out_refs = refs[: len(parts)], refs[len(parts)], refs[len(parts) + 1 :]
            flag = flag_ref[0]
            hidden = base_ref[...].astype(F32)
            if entering:
                hidden = self.enter(flag, hidden)
            else:
                for part_ref in part_refs:
                    hidden = hidden + part_ref[...].astype(F32)
                hidden = hidden + table_ref[bias : bias + 1, :]
            out_refs[0][...] = hidden
            center = hidden - jnp.mean(hidden, axis=-1, keepdims=True)
            spread = jnp.mean(center * center, axis=-1, keepdims=True)
            normed = center * lax.rsqrt(spread + NORM_EPS) * table_ref[index : index + 1, :]
            normed = normed + table_ref[7 + index : 8 + index, :]
            if low:
                out_refs[1][...] = normed.astype(BF16)
            if full:
                out_refs[-1][...] = self.leave(flag, normed)

        return self.call(kernel, (base, *parts), outs, "norm_forward")

    def backward(self, index, hidden, parts, cotangent=None, flow=None, low=True, last=False):
        shape = hidden.shape
        operands = (hidden, *parts)
        if cotangent is not None:
            operands += (cotangent,)
        if flow is not None:
            operands += (flow,)
        outs = [jax.ShapeDtypeStruct(shape, F32), jax.ShapeDtypeStruct((3, shape[1]), F32)]
        if low:
            outs.append(jax.ShapeDtypeStruct(shape, BF16))

        def kernel(flag_ref, hidden_ref, *refs):
            flag = flag_ref[0]
            part_refs, refs = refs[: len(parts)], refs[len(parts) :]
            upstream = None
            for part_ref in part_refs:
                value = part_ref[...].astype(F32)
                upstream = value if upstream is None else upstream + value
            if cotangent is not None:
                value = self.enter(flag, refs[0][...])
                upstream = value if upstream is None else upstream + value
                refs = refs[1:]
            if flow is not None:
                passing = refs[0][...]
                refs = refs[1:]
            table_ref, grad_ref, sums_ref = refs[:3]
            values = hidden_ref[...]
            center = values - jnp.mean(values, axis=-1, keepdims=True)
            spread = jnp.mean(center * center, axis=-1, keepdims=True)
            scale = lax.rsqrt(spread + NORM_EPS)
            unit = center * scale
            pulled = upstream * table_ref[index : index + 1, :]
            level = jnp.mean(pulled, axis=-1, keepdims=True)
            tilt = jnp.mean(pulled * unit, axis=-1, keepdims=True)
            grad = scale * (pulled - level - unit * tilt)
            if flow is not None:
                grad = grad + passing
            if low:
                refs[3][...] = grad.astype(BF16)
            grad_ref[...] = self.leave(flag, grad) if last else grad

            @pl.when(pl.program_id(0) == 0)
            def _():
                sums_ref[...] = jnp.zeros_like(sums_ref)

            sums_ref[0:1, :] += jnp.sum(upstream * unit, axis=0, keepdims=True)
            sums_ref[1:2, :] += jnp.sum(upstream, axis=0, keepdims=True)
            sums_ref[2:3, :] += jnp.sum(grad, axis=0, keepdims=True)

            @pl.when(pl.program_id(0) == pl.num_programs(0) - 1)
            def _():
                sums_ref[...] = self.leave(flag, sums_ref[...])

        return self.call(kernel, operands, outs, "norm_backward")


def squares_kernel(*refs):
    *value_refs, out_ref = refs
    total = jnp.zeros((1, 1), F32)
    for value_ref in value_refs:
        values = value_ref[...].astype(F32)
        total = total + jnp.sum(values * values, keepdims=True).reshape(1, 1)
    out_ref[...] = total


def sum_of_squares(arrays):
    return kernel_call(
        squares_kernel,
        (1,),
        [whole(array.shape) for array in arrays],
        whole((1, 1)),
        jax.ShapeDtypeStruct((1, 1), F32),
        [],
        2 * sum(array.size for array in arrays),
        sum(array.size * array.dtype.itemsize for array in arrays),
        "squares",
    )(*arrays)


def clip_factor(square_sum):
    return jnp.minimum(1.0, CLIP_NORM / (jnp.sqrt(square_sum) + 1e-06))


def adam(gradient, weight, first_old, second_old, factor, step_rate, decay_rate):
    clipped = gradient * factor
    moment = BETA_FIRST * first_old + (1.0 - BETA_FIRST) * clipped
    second_new = BETA_SECOND * second_old + (1.0 - BETA_SECOND) * clipped * clipped
    fixed_first = moment / (1.0 - BETA_FIRST**STEP)
    fixed_second = second_new / (1.0 - BETA_SECOND**STEP)
    updated = weight - step_rate * (
        fixed_first / (jnp.sqrt(fixed_second) + ADAM_EPS) + decay_rate * weight
    )
    return clipped, second_new, updated


def update_kernel(cut, rates, count, *refs):
    square_ref, refs = refs[0], refs[1:]
    grad_refs, refs = refs[:count], refs[count:]
    in_refs, out_refs = refs[: 3 * len(rates)], refs[3 * len(rates) :]
    factor = clip_factor(square_ref[...])
    for index, gradient in enumerate(cut(grad_refs, pl.program_id(0))):
        values = [ref[...] for ref in in_refs[3 * index : 3 * index + 3]]
        shape = values[0].shape
        results = adam(
            gradient.reshape(shape), *values, factor.reshape((1,) * len(shape)), rates[index], MATRIX_DECAY
        )
        for out_ref, result in zip(out_refs[3 * index : 3 * index + 3], results):
            out_ref[...] = result


def choose(refs, step):
    value = refs[0][...]
    for index in range(1, len(refs)):
        value = jnp.where(step == index, refs[index][...], value)
    return value.astype(F32)


def update(square_sum, gradients, groups, rates, cut, name):
    arrays = [array for group in groups for array in group]

    def spec(shape):
        return pl.BlockSpec((1,) + shape[1:], lambda step: (step,) + (0,) * (len(shape) - 1))

    outs = [jax.ShapeDtypeStruct(array.shape, F32) for array in arrays]
    return kernel_call(
        partial(update_kernel, cut, rates, len(gradients)),
        (arrays[0].shape[0],),
        [whole((1, 1))]
        + [whole(gradient.shape) for gradient in gradients]
        + [spec(array.shape) for array in arrays],
        [spec(out.shape) for out in outs],
        outs,
        [],
        20 * sum(array.size for array in arrays) // 3,
        8 * sum(array.size for array in arrays),
        name,
    )(square_sum, *gradients, *arrays)


def body(
    source_tokens,
    target_tokens,
    source_lengths,
    target_lengths,
    bucket_kinds,
    source_cotangent,
    target_cotangent,
    attention_in,
    attention_out,
    hidden_in,
    hidden_out,
    vectors,
    hidden_bias,
    first_attention_in,
    first_attention_out,
    first_hidden_in,
    first_hidden_out,
    first_vectors,
    first_hidden_bias,
    second_attention_in,
    second_attention_out,
    second_hidden_in,
    second_hidden_out,
    second_vectors,
    second_hidden_bias,
):
    moves = TensorMoves()
    split = CrossRows() if lax.axis_size("dp") == 8 else PlainRows()
    assert bucket_kinds.shape[0] == 1
    shard_rows = attention_in.shape[2]
    head_width = attention_in.shape[3]
    unit_width = hidden_in.shape[2]
    shard_units = hidden_bias.shape[1]

    small_shard = jnp.concatenate([vectors, hidden_bias.reshape(-1, shard_rows)], axis=0)
    small = split.stack(small_shard.astype(BF16)).astype(F32)

    def attention_shard(slot_id):
        parts = [attention_in[slot_id, which].astype(BF16) for which in range(3)]
        return jnp.concatenate(parts + [attention_out[slot_id].astype(BF16).T], axis=1)

    attn_full = [None] * 3
    up_full = [None] * 2
    down_full = [None] * 2
    attn_full[0] = split.gather(attention_shard(0))
    attn_full[1] = split.gather(attention_shard(1))
    up_full[0] = split.gather(hidden_in[0].astype(BF16))
    down_full[0] = split.gather(hidden_out[0].astype(BF16).T)
    attn_full[2] = split.gather(attention_shard(2))
    up_full[1] = split.gather(hidden_in[1].astype(BF16))
    down_full[1] = split.gather(hidden_out[1].astype(BF16).T)

    norms = Norms(small[:, :25].transpose(1, 0, 2).reshape(25, -1), split.y)
    ordered = split.turn(small)
    head_bias = ordered[:, 14:20].transpose(1, 0, 2).reshape(6, -1)
    head_bias = lax.dynamic_slice_in_dim(head_bias, moves.me * head_width, head_width, 1)
    unit_bias = ordered[:, 25:].reshape(split.count, 2, shard_units)
    unit_bias = unit_bias.transpose(1, 0, 2).reshape(2, -1)
    unit_bias = lax.dynamic_slice_in_dim(unit_bias, moves.me * unit_width, unit_width, 1)

    block_rows = source_tokens.shape[0]
    places = jnp.concatenate(
        [
            (moves.me ^ index) * block_rows + jnp.arange(block_rows, dtype=jnp.int32)
            for index in range(moves.count)
        ]
    )
    source_items, source_live = item_codes(bucket_kinds[0], source_lengths[0], places)
    target_items, target_live = item_codes(bucket_kinds[0], target_lengths[0], places)

    def layout_of(key_codes, query_codes):
        return key_codes[:, None], query_codes[None, :], places[:, None], places[None, :]

    encoder_layout = layout_of(source_live, source_items)
    self_layout = layout_of(target_live, target_items)
    cross_layout = layout_of(source_live, target_items)

    source, low = norms.forward(0, source_tokens)
    source_norm_one = moves.gather(low)
    target, low = norms.forward(3, target_tokens)
    target_norm_one = moves.gather(low)
    branch, source_attn_state = attention_forward(
        moves, attn_full[0], source_norm_one, source_norm_one, head_bias[:2], encoder_layout, False
    )
    source_mid, low = norms.forward(1, source, branch, 20)
    source_norm_two = moves.gather(low)
    branch, self_state = attention_forward(
        moves, attn_full[1], target_norm_one, target_norm_one, head_bias[2:4], self_layout, True
    )
    target_mid, low = norms.forward(4, target, branch, 21)
    target_norm_two = moves.gather(low)
    branch, source_ffn_state = feed_forward(
        moves, up_full[0], down_full[0], source_norm_two, unit_bias[:1]
    )
    source_last, low, encoder_output = norms.forward(2, source_mid, branch, 23, full=True)
    memory = moves.gather(low)
    branch, cross_state = attention_forward(
        moves, attn_full[2], target_norm_two, memory, head_bias[4:], cross_layout, False
    )
    target_cross, low = norms.forward(5, target_mid, branch, 22)
    target_norm_three = moves.gather(low)
    branch, target_ffn_state = feed_forward(
        moves, up_full[1], down_full[1], target_norm_three, unit_bias[1:]
    )
    target_last, decoder_output = norms.forward(6, target_cross, branch, 24, low=False, full=True)

    def reduce_weight(parts):
        return split.scatter(*parts)

    target_flow, sums_six, low = norms.backward(6, target_last, (), target_cotangent)
    parts, up_parts, down_parts, unit_sums_one = feed_backward(
        moves, up_full[1], down_full[1], low, target_ffn_state, target_norm_three
    )
    up_grad_one = reduce_weight(up_parts)
    down_grad_one = reduce_weight(down_parts)
    target_flow, sums_five, low = norms.backward(5, target_cross, parts, None, target_flow)
    parts, memory_parts, weight_parts, cross_sums = attention_backward(
        moves, attn_full[2], low, cross_state, target_norm_two, memory, cross_layout, False
    )
    attn_grad_two = reduce_weight(weight_parts)
    source_flow, sums_two, source_low = norms.backward(
        2, source_last, memory_parts, source_cotangent
    )
    target_flow, sums_four, low = norms.backward(4, target_mid, parts, None, target_flow)
    parts, up_parts, down_parts, unit_sums_zero = feed_backward(
        moves, up_full[0], down_full[0], source_low, source_ffn_state, source_norm_two
    )
    up_grad_zero = reduce_weight(up_parts)
    down_grad_zero = reduce_weight(down_parts)
    source_flow, sums_one, source_low = norms.backward(1, source_mid, parts, None, source_flow)
    parts, unused, weight_parts, self_sums = attention_backward(
        moves, attn_full[1], low, self_state, target_norm_one, target_norm_one, self_layout, True
    )
    attn_grad_one = reduce_weight(weight_parts)
    target_grad, sums_three = norms.backward(
        3, target, parts, None, target_flow, low=False, last=True
    )
    parts, unused, weight_parts, source_sums = attention_backward(
        moves,
        attn_full[0],
        source_low,
        source_attn_state,
        source_norm_one,
        source_norm_one,
        encoder_layout,
        False,
    )
    attn_grad_zero = reduce_weight(weight_parts)
    source_grad, sums_zero = norms.backward(
        0, source, parts, None, source_flow, low=False, last=True
    )

    norm_sums = (sums_zero, sums_one, sums_two, sums_three, sums_four, sums_five, sums_six)
    wide_rows = [sums[0:1] for sums in norm_sums] + [sums[1:2] for sums in norm_sums]
    wide_rows += [sums[2:3] for sums in (sums_one, sums_four, sums_five, sums_two, sums_six)]
    unit_rows = [sums.reshape(-1, head_width) for sums in (unit_sums_zero, unit_sums_one)]
    part_rows = jnp.concatenate([source_sums, self_sums, cross_sums] + unit_rows, axis=0)
    columns = jnp.arange(moves.count * head_width, dtype=jnp.int32) // head_width
    placed = jnp.where(columns[None, :] == moves.me, jnp.tile(part_rows, (1, moves.count)), 0.0)
    small_sum = split.total(moves.total(jnp.concatenate(wide_rows + [placed], axis=0)))
    wide_grad = lax.dynamic_slice_in_dim(small_sum[:25], split.me * shard_rows, shard_rows, 1)
    wide_grad, head_grad = wide_grad[:19], wide_grad[19:]
    unit_grad = small_sum[25:].reshape(2, -1, moves.count, head_width).transpose(0, 2, 1, 3)
    unit_grad = lax.dynamic_slice_in_dim(
        unit_grad.reshape(2, -1), split.me * shard_units, shard_units, 1
    )
    vector_grad = jnp.concatenate([wide_grad[:14], head_grad, wide_grad[14:]], axis=0)

    attn_grads = (attn_grad_zero, attn_grad_one, attn_grad_two)
    up_grads = (up_grad_zero, up_grad_one)
    down_grads = (down_grad_zero, down_grad_one)
    local_squares = sum_of_squares((*attn_grads, *up_grads, *down_grads))
    small_squares = jnp.sum(vector_grad * vector_grad) + jnp.sum(unit_grad * unit_grad)
    square_sum = split.total(moves.total(local_squares) + small_squares)
    grad_norm = jnp.sqrt(square_sum)[0, 0]
    factor = clip_factor(square_sum)[0, 0]
    rate_in, rate_out, rate_down = (
        0.5 * D ** (-0.5),
        0.5 * (D // 8) ** (-0.5),
        0.5 * FF ** (-0.5),
    )

    def attention_cut(refs, step):
        values = choose(refs, step)
        inputs = [
            values[:, which * head_width : (which + 1) * head_width] for which in range(3)
        ]
        return jnp.stack(inputs), values[:, 3 * head_width :].T

    def up_cut(refs, step):
        return (choose(refs, step),)

    def down_cut(refs, step):
        return (choose(refs, step).T,)

    attn_new = update(
        square_sum,
        attn_grads,
        (
            (attention_in, first_attention_in, second_attention_in),
            (attention_out, first_attention_out, second_attention_out),
        ),
        (rate_in, rate_out),
        attention_cut,
        "update_attention",
    )
    up_new = update(
        square_sum,
        up_grads,
        ((hidden_in, first_hidden_in, second_hidden_in),),
        (rate_in,),
        up_cut,
        "update_up",
    )
    down_new = update(
        square_sum,
        down_grads,
        ((hidden_out, first_hidden_out, second_hidden_out),),
        (rate_down,),
        down_cut,
        "update_down",
    )
    vector_new = adam(vector_grad, vectors, first_vectors, second_vectors, factor, 0.3, 0.0)
    unit_new = adam(
        unit_grad, hidden_bias, first_hidden_bias, second_hidden_bias, factor, 0.3, 0.0
    )
    return (
        encoder_output,
        decoder_output,
        source_grad,
        target_grad,
        grad_norm,
        *attn_new,
        *up_new,
        *down_new,
        *vector_new,
        *unit_new,
        vector_new[0][23:25],
    )


def solution(mesh):
    placed = (
        P(("dp", "tensor"), None),
        P(("dp", "tensor"), None),
        P("dp", None),
        P("dp", None),
        P("dp"),
        P(("dp", "tensor"), None),
        P(("dp", "tensor"), None),
        P(None, None, "dp", "tensor"),
        P(None, "tensor", "dp"),
        P(None, "dp", "tensor"),
        P(None, "tensor", "dp"),
        P(None, "dp"),
        P(None, "dp"),
        P(None, None, "dp", "tensor"),
        P(None, "tensor", "dp"),
        P(None, "dp", "tensor"),
        P(None, "tensor", "dp"),
        P(None, "dp"),
        P(None, "dp"),
        P(None, None, "dp", "tensor"),
        P(None, "tensor", "dp"),
        P(None, "dp", "tensor"),
        P(None, "tensor", "dp"),
        P(None, "dp"),
        P(None, "dp"),
    )
    return jax.shard_map(
        body,
        mesh=mesh,
        in_specs=placed,
        out_specs=(
            P(("dp", "tensor"), None),
            P(("dp", "tensor"), None),
            P(("dp", "tensor"), None),
            P(("dp", "tensor"), None),
            P(),
            P(None, None, "dp", "tensor"),
            P(None, None, "dp", "tensor"),
            P(None, None, "dp", "tensor"),
            P(None, "tensor", "dp"),
            P(None, "tensor", "dp"),
            P(None, "tensor", "dp"),
            P(None, "dp", "tensor"),
            P(None, "dp", "tensor"),
            P(None, "dp", "tensor"),
            P(None, "tensor", "dp"),
            P(None, "tensor", "dp"),
            P(None, "tensor", "dp"),
            P(None, "dp"),
            P(None, "dp"),
            P(None, "dp"),
            P(None, "dp"),
            P(None, "dp"),
            P(None, "dp"),
            P(None, "dp"),
        ),
        check_vma=False,
    )
```

```python
from functools import partial

import jax
import jax.numpy as jnp
from jax import lax
from jax.experimental import pallas as pl
from jax.experimental.pallas import tpu as pltpu
from jax.sharding import PartitionSpec as P

D = 1024
FF = 4096
L = 1024
ITEMS = 8
STEP = 10
HEAD = 64
ITEM = 128


NORM_EPS = 1e-05
CLIP_NORM = 1.0
BETA_FIRST = 0.9
BETA_SECOND = 0.999
ADAM_EPS = 1e-08
MATRIX_DECAY = 0.01
MASKED = -1e30

BF16 = jnp.bfloat16
F32 = jnp.float32
VECTOR_RATE = 0.3
VMEM_BYTES = 24 * 1024 * 1024


class TensorMoves:
    def __init__(self, order):
        self.order = order
        self.count = lax.axis_size("tensor")
        assert self.count == 4
        self.me = lax.axis_index("tensor")

    def swap(self, values, bit):
        pairs = [(index, index ^ bit) for index in range(self.count)]
        return lax.ppermute(values, "tensor", pairs)

    def gather(self, shard):
        return self.gather_far(self.gather_near(shard))

    def gather_near(self, shard):
        return shard, self.swap(shard, 1), self.swap(shard, 2)

    def gather_far(self, rows):
        return *rows, self.swap(rows[2], 1)

    def gather_late(self, rows):
        return *rows, self.swap(self.order.after_last(rows[2]), 1)

    def cross(self, send, keep, first=()):
        send = lax.optimization_barrier((send, first))[0]
        crossing = (keep + self.swap(send, 1).astype(F32)).astype(BF16)
        self.order.before_next(crossing)
        return self.swap(crossing, 2)

    def parts(self, near, arrived):
        first, second, keep = near
        return keep, self.swap(first, 1), self.swap(second, 1), arrived

    @property
    def steps(self):
        return [lambda values, bit=bit: values + self.swap(values, bit) for bit in (1, 2)]

    def total(self, values):
        for step in self.steps:
            values = step(values)
        return values


class PlainRows:
    def __init__(self, order):
        self.order = order
        self.count = lax.axis_size("dp")
        self.me = lax.axis_index("dp")
        self.y = None

    def start(self, shard):
        return lax.all_gather(shard, "dp", axis=0, tiled=True)

    def finish(self, full):
        half = full.shape[0] // 2
        return full[:half], full[half:]

    def blocks(self, stacked, first, count):
        return [
            lax.dynamic_index_in_dim(stacked, first + index, 0, False) for index in range(count)
        ]

    def send(self, far_part):
        return far_part

    def settle(self, near_part, arrived):
        values = jnp.concatenate([near_part, arrived.astype(F32)], 0)
        return lax.psum_scatter(values, "dp", scatter_dimension=0, tiled=True)

    def stack(self, shard):
        return lax.all_gather(shard, "dp", axis=0)

    def spread(self, values):
        return lax.psum_scatter(values, "dp", scatter_dimension=1, tiled=True)

    @property
    def steps(self):
        return [lambda values: lax.psum(values, "dp")]

    def total(self, values):
        for step in self.steps:
            values = step(values)
        return values


class CrossRows(PlainRows):
    ALONG_Z = [[0, 2, 4, 6], [1, 3, 5, 7]]

    def __init__(self, order):
        super().__init__(order)
        self.z = self.me // 2
        self.y = self.me % 2

    def swap(self, values, bits):
        pairs = [(index, index ^ bits) for index in range(self.count)]
        return lax.ppermute(values, "dp", pairs)

    def start(self, shard):
        return lax.all_gather(shard, "dp", axis=0, tiled=True, axis_index_groups=self.ALONG_Z)

    def finish(self, near):
        return near, self.swap(near, 1)

    def blocks(self, stacked, first, count):
        assert count == 2
        near = lax.dynamic_index_in_dim(stacked, first // 2, 0, False)
        far = lax.dynamic_index_in_dim(stacked, first // 2 + 4, 0, False)
        even = self.y == 0
        return [jnp.where(even, near, far), jnp.where(even, far, near)]

    def send(self, far_part):
        return self.swap(far_part, 1)

    def settle(self, near_part, arrived):
        near_part, arrived = self.order.after_last((near_part, arrived))
        part = (near_part + arrived.astype(F32)).astype(BF16)
        self.order.before_next(part)
        return lax.psum_scatter(
            part, "dp", scatter_dimension=0, tiled=True, axis_index_groups=self.ALONG_Z
        )

    def stack(self, shard):
        pieces = jnp.stack([shard] + [self.swap(shard, bits) for bits in (2, 4, 6)])
        near = jnp.stack(
            [lax.dynamic_index_in_dim(pieces, self.z ^ index, 0, False) for index in range(4)]
        )
        return jnp.concatenate([near, self.swap(near, 1)], axis=0)

    def spread(self, values):
        rows = values.shape[0]
        blocks = values.reshape(rows, 4, 2, -1)
        first, second = [blocks[:, :, index].reshape(rows, -1) for index in range(2)]
        even = self.y == 0
        part = jnp.where(even, first, second) + self.swap(jnp.where(even, second, first), 1)
        size = part.shape[1] // 4
        total = lax.dynamic_slice_in_dim(part, self.z * size, size, 1)
        for bits in (2, 4, 6):
            sent = lax.dynamic_slice_in_dim(part, (self.z ^ (bits // 2)) * size, size, 1)
            total = total + self.swap(sent, bits)
        return total

    @property
    def steps(self):
        return [lambda values, bits=bits: values + self.swap(values, bits) for bits in (1, 2, 4)]


def item_codes(row_kind, lengths, places):
    items = jnp.where(row_kind == 1, 0, places // ITEM)
    within = jnp.where(row_kind == 1, places, places % ITEM)
    limit = jnp.zeros_like(places)
    for index in range(ITEMS):
        limit = jnp.where(items == index, lengths[index], limit)
    return items, jnp.where(within < limit, items, -1)


def dot_nn(left, right):
    return jnp.dot(left, right, preferred_element_type=F32)


def dot_nt(left, right):
    return lax.dot_general(left, right, (((1,), (1,)), ((), ())), preferred_element_type=F32)


def dot_tn(left, right):
    return lax.dot_general(left, right, (((0,), (0,)), ((), ())), preferred_element_type=F32)


def wide_dot(rows, near, far):
    half = near.shape[0]
    return dot_nn(rows[:, :half], near[...]) + dot_nn(rows[:, half:], far[...])


class Load:
    def __init__(self, shape, start=None):
        self.shape = shape
        self.start = start or (0,) * len(shape)


class Loaded:
    def __init__(self, copy, buffer, step):
        self.copy = copy
        self.buffer = buffer
        self.step = step
        self.waited = False

    @property
    def shape(self):
        return self.buffer.shape

    def ready(self):
        if not self.waited:
            self.waited = True
            pl.when(self.step == 0)(self.copy.wait)

    def wait_here(self):
        self.waited = True
        self.copy.wait()

    def __getitem__(self, where):
        self.ready()
        return self.buffer[where]


class Order:
    def __init__(self):
        self.marks = ()

    def call(self, kernel, grid, in_specs, out_specs, out_shapes, scratch, flops, moved, name):
        marks = self.marks
        loads = [(place, spec) for place, spec in enumerate(in_specs) if isinstance(spec, Load)]
        hbm = pl.BlockSpec(memory_space=pltpu.HBM)

        def marked(*refs):
            refs = list(refs[len(marks) :])
            step = pl.program_id(0)
            loaded = []
            if loads:
                *refs, semaphores = refs
                buffers = refs[-len(loads) :]
                refs = refs[: -len(loads)]
                for index, (place, spec) in enumerate(loads):
                    source = refs[place].at[
                        tuple(pl.ds(first, size) for first, size in zip(spec.start, spec.shape))
                    ]
                    copy = pltpu.make_async_copy(source, buffers[index], semaphores.at[index])
                    loaded.append(Loaded(copy, buffers[index], step))
                    refs[place] = loaded[-1]

                @pl.when(step == 0)
                def _():
                    for item in loaded:
                        item.copy.start()

            kernel(*refs)
            for item in loaded:
                item.ready()

        def run(*operands):
            operands = list(operands)
            buffers = []
            for place, spec in loads:
                buffers.append(pltpu.VMEM(spec.shape, operands[place].dtype))
                operands[place] = pltpu.with_memory_space_constraint(operands[place], pltpu.HBM)
            if loads:
                buffers.append(pltpu.SemaphoreType.DMA((len(loads),)))
            results = pl.pallas_call(
                marked,
                grid=grid,
                in_specs=[pl.BlockSpec(memory_space=pl.ANY)] * len(marks)
                + [hbm if isinstance(spec, Load) else spec for spec in in_specs],
                out_specs=out_specs,
                out_shape=out_shapes,
                scratch_shapes=list(scratch) + buffers,
                compiler_params=pltpu.CompilerParams(
                    vmem_limit_bytes=VMEM_BYTES,
                    dimension_semantics=("arbitrary",) * len(grid),
                ),
                cost_estimate=pl.CostEstimate(
                    flops=flops, bytes_accessed=moved, transcendentals=0
                ),
                name=name,
            )(*marks, *operands)
            self.marks = (min(jax.tree.leaves(results), key=lambda leaf: leaf.size),)
            return results

        return run

    def before_next(self, value):
        self.marks += (value,)

    def after_last(self, value):
        return lax.optimization_barrier((value, self.marks))[0]


def whole(shape):
    return pl.BlockSpec(
        shape, lambda step: (0,) * len(shape), pipeline_mode=pl.Buffered(buffer_count=1)
    )


def pair_bias(layout_ref, start, rows, causal):
    turned = layout_ref[...].T
    queries = pl.ds(start, rows)
    allowed = turned[:, 0:1] == layout_ref[2:3, queries]
    if causal:
        allowed = allowed & (turned[:, 1:2] <= layout_ref[1:2, queries])
    return jnp.where(allowed, 0.0, MASKED).astype(F32)


def head_rows_only(block, head, scale=None):
    lanes = lax.broadcasted_iota(jnp.int32, block.shape, 1) // HEAD
    if scale is not None:
        block = block * jnp.asarray(scale, block.dtype)
    return jnp.where(lanes == head, block, jnp.zeros_like(block))


def over_keys(combine, values):
    parts = values.reshape(8, values.shape[0] // 8, values.shape[1])
    return combine(combine(parts, axis=0), axis=0, keepdims=True)


def attend_block(queries, key_rows, values_turned, bias, heads):
    scores = []
    for head in range(heads):
        picked = head_rows_only(queries, head, HEAD ** (-0.5))
        scores.append(dot_nt(key_rows, picked) + bias)
    largest = [over_keys(jnp.max, score) for score in scores]
    contexts = []
    totals = []
    for head in range(heads):
        weights = jnp.exp(scores[head] - largest[head])
        total = over_keys(jnp.sum, weights)
        context = dot_nn(
            values_turned[head * HEAD : (head + 1) * HEAD, :], weights.astype(BF16)
        )
        contexts.append(context * (1.0 / total))
        totals.append(largest[head] + jnp.log(total))
    return jnp.concatenate(contexts, axis=0).T, jnp.concatenate(totals, axis=0)


def out_parts(rows, out_near, out_far, step, send_refs, keep_ref):
    half = out_near.shape[0]
    near = dot_nt(rows, out_near)
    far = dot_nt(rows, out_far)

    @pl.when(step == 0)
    def _():
        if len(send_refs) == 1:
            send_refs[0][:, :half] = near.astype(BF16)
            send_refs[0][:, half:] = far.astype(BF16)
        else:
            send_refs[0][...] = near.astype(BF16)
            send_refs[1][...] = far.astype(BF16)

    @pl.when(step == 1)
    def _():
        keep_ref[:, :half] = near
        keep_ref[:, half:] = far


def part_shapes(rows, half, halves):
    sends = [(rows, half)] * 2 if halves else [(rows, 2 * half)]
    return sends + [(rows, 2 * half)], [BF16] * len(sends) + [F32]


def part_outs(rows, half, halves):
    shapes, kinds = part_shapes(rows, half, halves)
    return [jax.ShapeDtypeStruct(shape, kind) for shape, kind in zip(shapes, kinds)]


def part_specs(rows, half, halves):
    return [whole(shape) for shape in part_shapes(rows, half, halves)[0]]


def attend_tail(
    step, qkv_ref, turned_ref, layout_ref, causal, out_near, out_far, first_row, outs, heads
):
    context_ref, total_ref, *send_refs, keep_ref = outs
    rows = keep_ref.shape[0]
    wide = context_ref.shape[1]
    start = pl.multiple_of(first_row + (1 - step) * rows, rows)
    bias = pair_bias(layout_ref, start, rows, causal)
    context, totals = attend_block(
        qkv_ref[pl.ds(start, rows), :wide],
        qkv_ref[:, wide : 2 * wide],
        turned_ref[...],
        bias,
        heads,
    )
    context = context.astype(BF16)
    context_ref[...] = context
    total_ref[...] = totals
    out_parts(context, out_near, out_far, step, send_refs, keep_ref)


def attend_far_kernel(causal, is_cross, heads, *refs):
    normed_refs = memory_refs = refs[:4]
    refs = refs[4:]
    if is_cross:
        memory_refs, refs = refs[:4], refs[4:]
    full_near_ref, full_far_ref, bias_ref = refs[:3]
    layout_ref = refs[3]
    qkv_ref, context_ref, *outs, turned_ref = refs[4:]
    step = pl.program_id(0)
    rows = outs[-1].shape[0]
    wide = context_ref.shape[1]

    @pl.when(step == 0)
    def _():
        def project(source_refs, begin, end, biases):
            for index in range(4):
                part = source_refs[index][...]
                values = wide_dot(part, full_near_ref[:, begin:end], full_far_ref[:, begin:end])
                span = slice(index * rows, (index + 1) * rows)
                for place, which in enumerate(range(begin // wide, end // wide)):
                    piece = values[:, place * wide : (place + 1) * wide]
                    if biases[which] is not None:
                        piece = piece + bias_ref[biases[which] : biases[which] + 1, :]
                    qkv_ref[span, which * wide : (which + 1) * wide] = piece.astype(BF16)

        biases = (0, None, 1)
        if is_cross:
            project(normed_refs, 0, wide, biases)
            project(memory_refs, wide, 3 * wide, biases)
        else:
            project(normed_refs, 0, 3 * wide, biases)
        turned_ref[...] = qkv_ref[:, 2 * wide :].T

    attend_tail(
        step,
        qkv_ref,
        turned_ref,
        layout_ref,
        causal,
        full_near_ref[:, 3 * wide :],
        full_far_ref[:, 3 * wide :],
        2 * rows,
        (context_ref, *outs),
        heads,
    )


def attend_near_kernel(causal, heads, *refs):
    qkv_ref, out_near_ref, out_far_ref = refs[:3]
    layout_ref = refs[3]
    context_ref, *outs, turned_ref = refs[4:]
    step = pl.program_id(0)
    wide = context_ref.shape[1]

    @pl.when(step == 0)
    def _():
        turned_ref[...] = qkv_ref[:, 2 * wide :].T

    attend_tail(
        step,
        qkv_ref,
        turned_ref,
        layout_ref,
        causal,
        out_near_ref[...],
        out_far_ref[...],
        0,
        (context_ref, *outs),
        heads,
    )


def attention_forward(order, moves, full, normed, memory, biases, layout, causal, first):
    length = layout.shape[1]
    rows = length // 4
    width = full[0].shape[1]
    wide = width // 4
    heads = wide // HEAD
    half = full[0].shape[0]
    is_cross = memory is not normed
    sources = tuple(normed) + (tuple(memory) if is_cross else ())
    pairs = 4 * rows * length // 2 * wide * heads

    half_outs = [
        jax.ShapeDtypeStruct((2 * rows, wide), BF16),
        jax.ShapeDtypeStruct((heads, 2 * rows), F32),
    ]
    half_specs = [
        pl.BlockSpec((rows, wide), lambda step: (1 - step, 0)),
        pl.BlockSpec((heads, rows), lambda step: (0, 1 - step)),
    ]
    turned = pltpu.VMEM((wide, length), BF16)
    qkv, context_far, totals_far, send_far, keep_far = order.call(
        partial(attend_far_kernel, causal, is_cross, heads),
        (2,),
        [whole((rows, 2 * half))] * len(sources)
        + [whole((half, width))] * 2
        + [whole(biases.shape), whole(layout.shape)],
        [whole((length, 3 * wide))] + half_specs + part_specs(rows, half, False),
        [jax.ShapeDtypeStruct((length, 3 * wide), BF16)]
        + half_outs
        + part_outs(rows, half, False),
        [turned],
        2 * length * 2 * half * 3 * wide + pairs,
        12 * length * 2 * half,
        "attend_far",
    )(*sources, *full, biases, layout)
    arrived = moves.cross(send_far, keep_far, first)
    yield
    context_near, totals_near, *near = order.call(
        partial(attend_near_kernel, causal, heads),
        (2,),
        [whole((length, 3 * wide))]
        + [pl.BlockSpec((half, wide), lambda step: (0, 3))] * 2
        + [whole(layout.shape)],
        half_specs + part_specs(rows, half, True),
        half_outs + part_outs(rows, half, True),
        [turned],
        pairs,
        6 * length * 2 * half,
        "attend_near",
    )(qkv, *full, layout)
    branch = moves.parts(near, arrived)
    yield branch, (qkv, (context_near, context_far), (totals_near, totals_far))


def attend_back_kernel(causal, heads, *refs):
    qkv_ref, first_ref, out_near_ref, out_far_ref = refs[:4]
    context_refs, total_refs, layout_ref = refs[4:6], refs[6:8], refs[8]
    grad_refs = (first_ref, *refs[9:12])
    grads_ref, sums_ref = refs[12:14]
    keys_turned_ref, key_sum_ref, value_sum_ref, grad_ref, context_ref, total_ref = refs[14:]
    step = pl.program_id(0)
    rows = context_ref.shape[0]
    wide = context_ref.shape[1]
    scale = HEAD ** (-0.5)

    @pl.when(step == 0)
    def _():
        keys_turned_ref[...] = qkv_ref[:, wide : 2 * wide].T
        key_sum_ref[...] = jnp.zeros_like(key_sum_ref)
        value_sum_ref[...] = jnp.zeros_like(value_sum_ref)

    for loaded in (*context_refs, *total_refs):
        loaded.ready()
    for index in range(4):

        @pl.when(step == index)
        def _(index=index):
            span = slice((index % 2) * rows, (index % 2 + 1) * rows)
            grad_refs[index].wait_here()
            grad_ref[...] = grad_refs[index][...]
            context_ref[...] = context_refs[index // 2][span, :]
            total_ref[...] = total_refs[index // 2][:, span]

    context_grad = wide_dot(grad_ref[...], out_near_ref, out_far_ref).astype(BF16)
    products = (context_grad.astype(F32) * context_ref[...].astype(F32)).T
    start = pl.multiple_of(step * rows, rows)
    bias = pair_bias(layout_ref, start, rows, causal)
    queries = qkv_ref[pl.ds(start, rows), :wide]
    key_rows = qkv_ref[:, wide : 2 * wide]
    value_rows = qkv_ref[:, 2 * wide :]
    query_grads = []
    for head in range(heads):
        span = slice(head * HEAD, (head + 1) * HEAD)
        picked = head_rows_only(queries, head, scale)
        picked_grad = head_rows_only(context_grad, head)
        scores = dot_nt(key_rows, picked) + bias
        weights = jnp.exp(scores - total_ref[head : head + 1, :])
        weight_grad = dot_nt(value_rows, picked_grad)
        diagonal = jnp.sum(products[span, :], axis=0, keepdims=True)
        score_grad = (weights * (weight_grad - diagonal)).astype(BF16)
        value_sum_ref[...] += dot_nn(weights.astype(BF16), picked_grad)
        key_sum_ref[...] += dot_nn(score_grad, picked)
        query_grads.append(dot_nn(keys_turned_ref[span, :], score_grad))
    query_grad = jnp.concatenate(query_grads, axis=0).T * scale
    grads_ref[pl.ds(start, rows), :wide] = query_grad.astype(BF16)

    @pl.when(step == 3)
    def _():
        grads_ref[:, wide : 2 * wide] = key_sum_ref[...].astype(BF16)
        grads_ref[:, 2 * wide :] = value_sum_ref[...].astype(BF16)
        for place, begin in ((0, 0), (1, 2 * wide)):
            values = grads_ref[:, begin : begin + wide].astype(F32)
            sums_ref[place : place + 1, :] = jnp.sum(values, axis=0, keepdims=True)


def spread_kernel(begin, end, rows_ref, near_ref, far_ref, *outs):
    step = pl.program_id(0)
    part = rows_ref[:, begin:end]
    out_parts(part, near_ref[:, begin:end], far_ref[:, begin:end], step, outs[:-1], outs[-1])


def spread_rows(order, grads, full, begin, end, first):
    rows = grads.shape[0] // 4
    half = full[0].shape[0]
    wide = grads.shape[1]
    return order.call(
        partial(spread_kernel, begin, end),
        (2,),
        [pl.BlockSpec((rows, wide), lambda step: (first + 1 - step, 0))]
        + [whole((half, wide))] * 2,
        part_specs(rows, half, first == 0),
        part_outs(rows, half, first == 0),
        [],
        4 * rows * 2 * half * (end - begin),
        6 * rows * 2 * half + 4 * half * wide,
        "spread_rows",
    )(grads, *full)


def later_half(step, size):
    return pl.ds(pl.multiple_of((1 - step) * size, size), size)


def rows_dot(left_refs, right, begin, end, columns=slice(None)):
    total = None
    for index, left_ref in enumerate(left_refs):
        rows = left_ref.shape[0]
        if isinstance(right, tuple):
            first = (index % 2) * rows
            part = right[index // 2][first : first + rows, begin:end]
        else:
            part = right[index * rows : (index + 1) * rows, begin:end]
        product = dot_tn(left_ref[:, columns], part)
        total = product if total is None else total + product
    return total


def attention_weight_kernel(is_cross, *refs):
    normed_refs = memory_refs = refs[:4]
    refs = refs[4:]
    if is_cross:
        memory_refs, refs = refs[:4], refs[4:]
    upstream_refs, grads_ref, context_refs, outs = refs[:4], refs[4], refs[5:7], refs[7:]
    send_ref, keep_ref = outs
    step = pl.program_id(0)
    wide = context_refs[0].shape[1]
    columns = later_half(step, send_ref.shape[0])
    if is_cross:
        pieces = [
            rows_dot(normed_refs, grads_ref, 0, wide, columns),
            rows_dot(memory_refs, grads_ref, wide, 3 * wide, columns),
        ]
    else:
        pieces = [rows_dot(normed_refs, grads_ref, 0, 3 * wide, columns)]
    pieces.append(rows_dot(upstream_refs, tuple(context_refs), 0, wide, columns))

    @pl.when(step == 0)
    def _():
        send_ref[...] = jnp.concatenate(pieces, axis=1).astype(BF16)

    @pl.when(step == 1)
    def _():
        keep_ref[...] = jnp.concatenate(pieces, axis=1)


def attention_weights(order, normed, memory, upstream, grads, contexts):
    rows, width = normed[0].shape
    wide = contexts[0].shape[1]
    is_cross = memory is not normed
    sources = tuple(normed) + (tuple(memory) if is_cross else ()) + tuple(upstream)
    half = width // 2
    outs = (half, 4 * wide)
    return order.call(
        partial(attention_weight_kernel, is_cross),
        (2,),
        [Load((rows, width))] * len(sources)
        + [whole(grads.shape)]
        + [Load((2 * rows, wide))] * 2,
        [whole(outs)] * 2,
        [jax.ShapeDtypeStruct(outs, BF16), jax.ShapeDtypeStruct(outs, F32)],
        [],
        8 * rows * width * 4 * wide,
        2 * rows * width * (len(sources) + 4) + 6 * half * 4 * wide,
        "attention_weights",
    )(*sources, grads, *contexts)


def attention_backward(order, full, upstream_rows, stored, layout, causal):
    qkv, contexts, totals = stored
    length = qkv.shape[0]
    rows = length // 4
    wide = qkv.shape[1] // 3
    heads = wide // HEAD
    half = full[0].shape[0]
    return order.call(
        partial(attend_back_kernel, causal, heads),
        (4,),
        [Load(qkv.shape), Load((rows, 2 * half))]
        + [Load((half, wide), (0, 3 * wide))] * 2
        + [Load((2 * rows, wide))] * 2
        + [Load((heads, 2 * rows))] * 2
        + [Load(layout.shape)]
        + [Load((rows, 2 * half))] * 3,
        [whole(qkv.shape), whole((2, wide))],
        [jax.ShapeDtypeStruct(qkv.shape, BF16), jax.ShapeDtypeStruct((2, wide), F32)],
        [
            pltpu.VMEM((wide, length), BF16),
            pltpu.VMEM((length, wide), F32),
            pltpu.VMEM((length, wide), F32),
            pltpu.VMEM((rows, 2 * half), BF16),
            pltpu.VMEM((rows, wide), BF16),
            pltpu.VMEM((heads, rows), F32),
        ],
        10 * length * length * wide * heads,
        12 * length * 2 * half,
        "attend_back",
    )(qkv, upstream_rows[0], *full, *contexts, *totals, layout, *upstream_rows[1:])


GELU_SCALE = 0.7978845608028654
GELU_CUBE = 0.044715


def feed_kernel(own_ref, near_ref, up_near, up_far, down_near, down_far, bias_ref, *outs):
    activated_ref, slope_ref, *send_refs, keep_ref = outs
    step = pl.program_id(0)
    rows = jnp.where(step == 0, near_ref[...], own_ref[...])
    pre_act = wide_dot(rows, up_near[...], up_far[...]) + bias_ref[...]
    square = pre_act * pre_act
    bent = jnp.tanh(GELU_SCALE * pre_act * (1.0 + GELU_CUBE * square))
    activated = (0.5 * pre_act * (1.0 + bent)).astype(BF16)
    inner = GELU_SCALE * (1.0 + 3.0 * GELU_CUBE * square)
    slope = 0.5 * (1.0 + bent) + 0.5 * pre_act * (1.0 - bent * bent) * inner
    activated_ref[...] = activated
    slope_ref[...] = slope.astype(BF16)
    out_parts(activated, down_near[...], down_far[...], step, send_refs, keep_ref)


def feed_forward(order, up_full, down_full, pair_rows, unit_bias, halves):
    rows = pair_rows[0].shape[0]
    half, units = up_full[0].shape
    return order.call(
        feed_kernel,
        (2,),
        [whole((rows, 2 * half))] * 2 + [whole((half, units))] * 4 + [whole((1, units))],
        [pl.BlockSpec((rows, units), lambda step: (1 - step, 0))] * 2
        + part_specs(rows, half, halves),
        [jax.ShapeDtypeStruct((2 * rows, units), BF16)] * 2 + part_outs(rows, half, halves),
        [],
        16 * rows * half * units,
        20 * rows * units + 8 * half * units,
        "feed_forward",
    )(*pair_rows, *up_full, *down_full, unit_bias)


def feed_back_kernel(
    own_ref, near_ref, slope_ref, up_near, up_far, down_near, down_far, *outs
):
    grad_ref, sum_ref, *send_refs, keep_ref = outs
    step = pl.program_id(0)
    rows = jnp.where(step == 0, near_ref[...], own_ref[...])
    act_grad = wide_dot(rows, down_near[...], down_far[...])
    pre_grad = (act_grad * slope_ref[...].astype(F32)).astype(BF16)
    grad_ref[...] = pre_grad

    @pl.when(step == 0)
    def _():
        sum_ref[...] = jnp.zeros_like(sum_ref)

    sum_ref[...] += jnp.sum(pre_grad.astype(F32), axis=0, keepdims=True)
    out_parts(pre_grad, up_near[...], up_far[...], step, send_refs, keep_ref)


def feed_weight_kernel(*refs):
    left_refs, right_refs, (send_ref, keep_ref) = refs[:4], refs[4:6], refs[6:]
    step = pl.program_id(0)
    part = rows_dot(left_refs, tuple(right_refs), 0, send_ref.shape[1])

    @pl.when(step == 0)
    def _():
        send_ref[...] = part.astype(BF16)

    @pl.when(step == 1)
    def _():
        keep_ref[...] = part


def feed_weights(order, left, right):
    rows, width = left[0].shape
    units = right[0].shape[1]
    half = width // 2
    outs = (half, units)
    return order.call(
        feed_weight_kernel,
        (2,),
        [pl.BlockSpec((rows, half), lambda step: (0, 1 - step))] * 4
        + [whole((2 * rows, units))] * 2,
        [whole(outs)] * 2,
        [jax.ShapeDtypeStruct(outs, BF16), jax.ShapeDtypeStruct(outs, F32)],
        [],
        8 * rows * width * units,
        8 * rows * (width + units) + 6 * half * units,
        "feed_weights",
    )(*left, *right)


def feed_backward(order, up_full, down_full, pair_rows, slope, halves):
    rows = pair_rows[0].shape[0]
    half, units = up_full[0].shape
    return order.call(
        feed_back_kernel,
        (2,),
        [whole((rows, 2 * half))] * 2
        + [pl.BlockSpec((rows, units), lambda step: (1 - step, 0))]
        + [whole((half, units))] * 4,
        [pl.BlockSpec((rows, units), lambda step: (1 - step, 0)), whole((1, units))]
        + part_specs(rows, half, halves),
        [
            jax.ShapeDtypeStruct((2 * rows, units), BF16),
            jax.ShapeDtypeStruct((1, units), F32),
        ]
        + part_outs(rows, half, halves),
        [],
        16 * rows * half * units,
        20 * rows * units + 8 * half * units,
        "feed_backward",
    )(*pair_rows, slope, *up_full, *down_full)


def attention_shard_kernel(in_ref, out_ref, shard_ref):
    wide = in_ref.shape[3]
    for which in range(3):
        shard_ref[:, which * wide : (which + 1) * wide] = in_ref[0, which].astype(BF16)
    shard_ref[:, 3 * wide :] = out_ref[0].T.astype(BF16)


def attention_shard(order, attention_in, attention_out, slot_id):
    rows, wide = attention_in.shape[2:]
    return order.call(
        attention_shard_kernel,
        (1,),
        [
            pl.BlockSpec((1, 3, rows, wide), lambda step: (slot_id, 0, 0, 0)),
            pl.BlockSpec((1, wide, rows), lambda step: (slot_id, 0, 0)),
        ],
        whole((rows, 4 * wide)),
        jax.ShapeDtypeStruct((rows, 4 * wide), BF16),
        [],
        0,
        24 * rows * wide,
        "attention_shard",
    )(attention_in, attention_out)


def feed_shard_kernel(up_ref, down_ref, up_shard_ref, down_shard_ref):
    up_shard_ref[...] = up_ref[0].astype(BF16)
    down_shard_ref[...] = down_ref[0].T.astype(BF16)


def feed_shard(order, hidden_in, hidden_out, slot_id):
    rows, units = hidden_in.shape[1:]
    return order.call(
        feed_shard_kernel,
        (1,),
        [
            pl.BlockSpec((1, rows, units), lambda step: (slot_id, 0, 0)),
            pl.BlockSpec((1, units, rows), lambda step: (slot_id, 0, 0)),
        ],
        [whole((rows, units))] * 2,
        [jax.ShapeDtypeStruct((rows, units), BF16)] * 2,
        [],
        0,
        12 * rows * units,
        "feed_shard",
    )(hidden_in, hidden_out)


class Norms:
    def __init__(self, order, table, y):
        self.order = order
        self.table = table
        self.y = jnp.zeros((1,), jnp.int32) if y is None else y.astype(jnp.int32).reshape(1)
        self.ordered = y is None

    def enter(self, flag, values):
        if self.ordered:
            return values
        size = values.shape[1] // 8
        blocks = [values[:, index * size : (index + 1) * size] for index in range(8)]
        first = jnp.concatenate(blocks[0::2], axis=1)
        second = jnp.concatenate(blocks[1::2], axis=1)
        return jnp.concatenate(
            [jnp.where(flag == 0, first, second), jnp.where(flag == 0, second, first)], axis=1
        )

    def leave(self, flag, values):
        if self.ordered:
            return values
        half = values.shape[1] // 2
        near, far = values[:, :half], values[:, half:]
        first = jnp.where(flag == 0, near, far)
        second = jnp.where(flag == 0, far, near)
        size = half // 4
        blocks = []
        for index in range(4):
            span = slice(index * size, (index + 1) * size)
            blocks += [first[:, span], second[:, span]]
        return jnp.concatenate(blocks, axis=1)

    def sum_parts(self, parts):
        keep, first, second, arrived = [part.astype(F32) for part in parts]
        return keep + jnp.concatenate([first, second], axis=1) + arrived

    def call(self, compute, operands, outs, sums, name):
        rows, width = operands[0].shape
        blocks = 4
        block = rows // blocks
        count = len(operands)

        def kernel(flag_ref, *refs):
            in_refs, refs = refs[:count], refs[count:]
            table_ref, refs = refs[0], refs[1:]
            out_refs, refs = refs[: len(outs)], refs[len(outs) :]
            if sums:
                sums_ref, refs = refs[0], refs[1:]
            in_buffers, refs = refs[:count], refs[count:]
            out_buffers, (in_marks, out_marks) = refs[: len(outs)], refs[len(outs) :]

            def span(index):
                return pl.ds(index * block, block)

            arriving = [
                [
                    pltpu.make_async_copy(
                        ref.at[span(index)], buffer.at[span(index)], in_marks.at[place, index]
                    )
                    for place, (ref, buffer) in enumerate(zip(in_refs, in_buffers))
                ]
                for index in range(blocks)
            ]
            for copies in arriving:
                for copy in copies:
                    copy.start()
            total = None
            leaving = []
            for index, copies in enumerate(arriving):
                for copy in copies:
                    copy.wait()
                values = [buffer[span(index), :] for buffer in in_buffers]
                results, added = compute(flag_ref[0], values, table_ref)
                for place, (ref, buffer) in enumerate(zip(out_refs, out_buffers)):
                    buffer[span(index), :] = results[place].astype(buffer.dtype)
                    copy = pltpu.make_async_copy(
                        buffer.at[span(index)], ref.at[span(index)], out_marks.at[place, index]
                    )
                    copy.start()
                    leaving.append(copy)
                if sums:
                    total = added if total is None else [a + b for a, b in zip(total, added)]
            if sums:
                values = self.leave(flag_ref[0], jnp.concatenate(total, axis=0))
                sums_ref[...] = values
            for copy in leaving:
                copy.wait()

        results = self.order.call(
            kernel,
            (1,),
            [pl.BlockSpec(memory_space=pltpu.SMEM)]
            + [pl.BlockSpec(memory_space=pltpu.HBM)] * count
            + [whole(self.table.shape)],
            [pl.BlockSpec(memory_space=pltpu.HBM)] * len(outs)
            + [whole((sums, width))] * (1 if sums else 0),
            [pltpu.HBM((rows, width), kind) for kind in outs]
            + [jax.ShapeDtypeStruct((sums, width), F32)] * (1 if sums else 0),
            [pltpu.VMEM(operand.shape, operand.dtype) for operand in operands]
            + [pltpu.VMEM((rows, width), kind) for kind in outs]
            + [
                pltpu.SemaphoreType.DMA((count, blocks)),
                pltpu.SemaphoreType.DMA((len(outs), blocks)),
            ],
            20 * rows * width,
            sum(operand.size * operand.dtype.itemsize for operand in operands),
            name,
        )(
            self.y,
            *[pltpu.with_memory_space_constraint(operand, pltpu.HBM) for operand in operands],
            self.table,
        )
        return results

    def forward(self, index, base, parts=(), bias=None, low=True, full=False):
        def compute(flag, values, table_ref):
            hidden = values[0].astype(F32)
            if parts:
                hidden = hidden + self.sum_parts(values[1:]) + table_ref[bias : bias + 1, :]
            else:
                hidden = self.enter(flag, hidden)
            center = hidden - jnp.mean(hidden, axis=-1, keepdims=True)
            spread = jnp.mean(center * center, axis=-1, keepdims=True)
            normed = center * lax.rsqrt(spread + NORM_EPS) * table_ref[index : index + 1, :]
            normed = normed + table_ref[7 + index : 8 + index, :]
            results = [hidden]
            if low:
                results.append(normed)
            if full:
                results.append(self.leave(flag, normed))
            return results, None

        outs = [F32] + [BF16] * low + [F32] * full
        return self.call(compute, (base, *parts), outs, 0, "norm_forward")

    def backward(self, index, hidden, parts, cotangent=None, flow=None, low=True, last=False):
        extras = [value for value in (cotangent, flow) if value is not None]

        def compute(flag, values, table_ref):
            values, others, passing = values[0], list(values[1:]), None
            if flow is not None:
                passing = others.pop()
            upstream = self.enter(flag, others.pop()) if cotangent is not None else None
            if parts:
                summed = self.sum_parts(others)
                upstream = summed if upstream is None else upstream + summed
            center = values - jnp.mean(values, axis=-1, keepdims=True)
            spread = jnp.mean(center * center, axis=-1, keepdims=True)
            scale = lax.rsqrt(spread + NORM_EPS)
            unit = center * scale
            pulled = upstream * table_ref[index : index + 1, :]
            level = jnp.mean(pulled, axis=-1, keepdims=True)
            tilt = jnp.mean(pulled * unit, axis=-1, keepdims=True)
            grad = scale * (pulled - level - unit * tilt)
            if flow is not None:
                grad = grad + passing
            added = [
                jnp.sum(value, axis=0, keepdims=True) for value in (upstream * unit, upstream, grad)
            ]
            results = [self.leave(flag, grad) if last else grad]
            if low:
                results.append(grad)
            return results, added

        grad, *rest, sums = self.call(
            compute, (hidden, *parts, *extras), [F32] + [BF16] * low, 3, "norm_backward"
        )
        return grad, sums, *rest


def squares_kernel(copies, *refs):
    *value_refs, small_ref, out_ref = refs

    def squares(ref):
        values = ref[...].astype(F32)
        return jnp.sum(values * values, keepdims=True).reshape(1, 1)

    total = squares(small_ref) * (1.0 / copies)
    for value_ref in value_refs:
        total = total + squares(value_ref)
    out_ref[...] = total


def sum_of_squares(order, arrays, small, copies):
    return order.call(
        partial(squares_kernel, copies),
        (1,),
        [whole(array.shape) for array in (*arrays, small)],
        whole((1, 1)),
        jax.ShapeDtypeStruct((1, 1), F32),
        [],
        2 * sum(array.size for array in arrays),
        sum(array.size * array.dtype.itemsize for array in arrays),
        "squares",
    )(*arrays, small)


def clip_factor(square_sum):
    return jnp.minimum(1.0, CLIP_NORM / (jnp.sqrt(square_sum) + 1e-06))


def adam(gradient, weight, first_old, second_old, factor, step_rate, decay_rate):
    clipped = gradient * factor
    moment = BETA_FIRST * first_old + (1.0 - BETA_FIRST) * clipped
    second_new = BETA_SECOND * second_old + (1.0 - BETA_SECOND) * clipped * clipped
    fixed_first = moment / (1.0 - BETA_FIRST**STEP)
    fixed_second = second_new / (1.0 - BETA_SECOND**STEP)
    updated = weight - step_rate * (
        fixed_first / (jnp.sqrt(fixed_second) + ADAM_EPS) + decay_rate * weight
    )
    return clipped, second_new, updated


def update_kernel(cut, rates, count, *refs):
    square_ref, refs = refs[0], refs[1:]
    grad_refs, refs = refs[:count], refs[count:]
    in_refs, out_refs = refs[: 3 * len(rates)], refs[3 * len(rates) :]
    factor = clip_factor(square_ref[...])
    for index, gradient in enumerate(cut(grad_refs, pl.program_id(0))):
        values = [ref[...] for ref in in_refs[3 * index : 3 * index + 3]]
        shape = values[0].shape
        results = adam(
            gradient.reshape(shape), *values, factor.reshape((1,) * len(shape)), rates[index], MATRIX_DECAY
        )
        for out_ref, result in zip(out_refs[3 * index : 3 * index + 3], results):
            out_ref[...] = result


def small_update_kernel(square_ref, small_ref, *refs):
    in_refs, out_refs, bias_ref = refs[:6], refs[6:12], refs[12]
    factor = clip_factor(square_ref[...])
    small = small_ref[...]
    vector_grad = jnp.concatenate([small[:14], small[19:25], small[14:19]], axis=0)
    count = (small.shape[0] - 25) // 2
    unit_rows = [
        jnp.concatenate(
            [small[25 + slot * count + index][None] for index in range(count)], axis=1
        )
        for slot in range(2)
    ]
    for index, gradient in enumerate((vector_grad, jnp.concatenate(unit_rows, axis=0))):
        values = [ref[...] for ref in in_refs[3 * index : 3 * index + 3]]
        results = adam(gradient, *values, factor, VECTOR_RATE, 0.0)
        for out_ref, result in zip(out_refs[3 * index : 3 * index + 3], results):
            out_ref[...] = result
    bias_ref[...] = out_refs[0][23:25, :]


def small_update(order, square_sum, small, vector_arrays, unit_arrays):
    arrays = (*vector_arrays, *unit_arrays)
    outs = [jax.ShapeDtypeStruct(array.shape, F32) for array in arrays]
    outs.append(jax.ShapeDtypeStruct((2, arrays[0].shape[1]), F32))
    return order.call(
        small_update_kernel,
        (1,),
        [whole((1, 1)), whole(small.shape)] + [whole(array.shape) for array in arrays],
        [whole(out.shape) for out in outs],
        outs,
        [],
        0,
        0,
        "update_small",
    )(square_sum, small, *arrays)


def choose(refs, step):
    value = refs[0][...]
    for index in range(1, len(refs)):
        value = jnp.where(step == index, refs[index][...], value)
    return value.astype(F32)


def update(order, square_sum, gradients, groups, rates, cut, name):
    arrays = [array for group in groups for array in group]

    def spec(shape):
        return pl.BlockSpec((1,) + shape[1:], lambda step: (step,) + (0,) * (len(shape) - 1))

    outs = [jax.ShapeDtypeStruct(array.shape, F32) for array in arrays]
    return order.call(
        partial(update_kernel, cut, rates, len(gradients)),
        (arrays[0].shape[0],),
        [whole((1, 1))]
        + [whole(gradient.shape) for gradient in gradients]
        + [spec(array.shape) for array in arrays],
        [spec(out.shape) for out in outs],
        outs,
        [],
        20 * sum(array.size for array in arrays) // 3,
        8 * sum(array.size for array in arrays),
        name,
    )(square_sum, *gradients, *arrays)


def body(
    source_tokens,
    target_tokens,
    source_lengths,
    target_lengths,
    bucket_kinds,
    source_cotangent,
    target_cotangent,
    attention_in,
    attention_out,
    hidden_in,
    hidden_out,
    vectors,
    hidden_bias,
    first_attention_in,
    first_attention_out,
    first_hidden_in,
    first_hidden_out,
    first_vectors,
    first_hidden_bias,
    second_attention_in,
    second_attention_out,
    second_hidden_in,
    second_hidden_out,
    second_vectors,
    second_hidden_bias,
):
    order = Order()
    moves = TensorMoves(order)
    split = CrossRows(order) if lax.axis_size("dp") == 8 else PlainRows(order)
    assert bucket_kinds.shape[0] == 1
    shard_rows = attention_in.shape[2]
    head_width = attention_in.shape[3]
    unit_width = hidden_in.shape[2]
    shard_units = hidden_bias.shape[1]

    small_shard = jnp.concatenate([vectors, hidden_bias.reshape(-1, shard_rows)], axis=0)
    small = split.stack(small_shard.astype(BF16)).astype(F32)

    attn_full = [None] * 3
    up_full = [None] * 2
    down_full = [None] * 2
    attn_zero = split.start(attention_shard(order, attention_in, attention_out, 0))
    attn_one = split.start(attention_shard(order, attention_in, attention_out, 1))
    up_shard, down_shard = feed_shard(order, hidden_in, hidden_out, 0)
    up_zero, down_zero = split.start(up_shard), split.start(down_shard)
    attn_two = split.start(attention_shard(order, attention_in, attention_out, 2))
    up_shard, down_shard = feed_shard(order, hidden_in, hidden_out, 1)
    up_one, down_one = split.start(up_shard), split.start(down_shard)

    norms = Norms(order, small[:, :25].transpose(1, 0, 2).reshape(25, -1), split.y)
    count = head_width // shard_rows
    own_blocks = split.blocks(small, moves.me * count, count)
    head_bias = jnp.concatenate([block[14:20] for block in own_blocks], axis=1)
    unit_bias = jnp.concatenate(
        [block[25:].reshape(2, shard_units) for block in own_blocks], axis=1
    )

    block_rows = source_tokens.shape[0]
    places = jnp.concatenate(
        [
            (moves.me ^ index) * block_rows + jnp.arange(block_rows, dtype=jnp.int32)
            for index in range(moves.count)
        ]
    )
    source_items, source_live = item_codes(bucket_kinds[0], source_lengths[0], places)
    target_items, target_live = item_codes(bucket_kinds[0], target_lengths[0], places)

    def layout_of(key_codes, query_codes):
        rows = jnp.stack([key_codes, places, query_codes])
        return jnp.pad(rows, ((0, 5), (0, 0))).astype(F32)

    encoder_layout = layout_of(source_live, source_items)
    self_layout = layout_of(target_live, target_items)
    cross_layout = layout_of(source_live, target_items)

    source, low = norms.forward(0, source_tokens)
    source_norm_one = moves.gather(low)
    target, low = norms.forward(3, target_tokens)
    target_norm_one = moves.gather(low)

    attn_full[0] = split.finish(attn_zero)
    attention = attention_forward(
        order,
        moves,
        attn_full[0],
        source_norm_one,
        source_norm_one,
        head_bias[:2],
        encoder_layout,
        False,
        (target_norm_one[2],),
    )
    next(attention)
    order.before_next(attn_one)
    attn_full[1] = split.finish(attn_one)
    branch, source_attn_state = next(attention)
    up_zero = order.after_last(up_zero)
    order.before_next(up_zero)
    up_full[0] = split.finish(up_zero)
    source_mid, low = norms.forward(1, source, branch, 20)
    source_norm_two = moves.gather(low)

    attention = attention_forward(
        order,
        moves,
        attn_full[1],
        target_norm_one,
        target_norm_one,
        head_bias[2:4],
        self_layout,
        True,
        (source_norm_two[2], up_full[0][1]),
    )
    next(attention)
    branch, self_state = next(attention)
    order.before_next(down_zero)
    down_full[0] = split.finish(down_zero)
    target_mid, low = norms.forward(4, target, branch, 21)
    target_norm_two = moves.gather(low)

    def feed_pair(slot_id, normed, first=()):
        weights = up_full[slot_id], down_full[slot_id]
        bias = unit_bias[slot_id : slot_id + 1]
        far = feed_forward(order, *weights, normed[2:], bias, False)
        arrived = moves.cross(*far[2:], first)
        near = feed_forward(order, *weights, normed[:2], bias, True)
        return moves.parts(near[2:], arrived), (near[:2], far[:2])

    order.before_next(attn_two)
    attn_full[2] = split.finish(attn_two)
    branch, source_ffn_state = feed_pair(0, source_norm_two, (target_norm_two[2],))
    order.before_next(up_one)
    up_full[1] = split.finish(up_one)
    source_last, low, encoder_output = norms.forward(2, source_mid, branch, 23, full=True)
    memory = moves.gather(low)

    attention = attention_forward(
        order,
        moves,
        attn_full[2],
        target_norm_two,
        memory,
        head_bias[4:],
        cross_layout,
        False,
        (up_full[1][1],),
    )
    next(attention)
    order.before_next(down_one)
    branch, cross_state = next(attention)
    down_full[1] = split.finish(down_one)
    target_cross, low = norms.forward(5, target_mid, branch, 22)
    low = lax.optimization_barrier((low, down_full[1][1]))[0]
    target_norm_three = moves.gather(low)
    branch, target_ffn_state = feed_pair(1, target_norm_three)
    target_last, decoder_output = norms.forward(6, target_cross, branch, 24, low=False, full=True)

    def feed_back_pair(slot_id, rows, states, first=()):
        weights = up_full[slot_id], down_full[slot_id]
        near = feed_backward(order, *weights, rows[:2], states[0][1], True)
        if len(rows) < 4:
            rows = moves.gather_late(rows)
        far = feed_backward(order, *weights, rows[2:], states[1][1], False)
        parts = moves.parts(near[2:], moves.cross(*far[2:], first))
        return rows, parts, (near[0], far[0]), near[1] + far[1]

    def feed_weight_pair(upstream_rows, states, normed, pre_grads):
        up_send, up_keep = feed_weights(order, normed, pre_grads)
        up_arrived = split.send(up_send)
        activated = (states[0][0], states[1][0])
        down_send, down_keep = feed_weights(order, upstream_rows, activated)
        return (up_keep, up_arrived), (down_keep, split.send(down_send))

    target_flow, sums_six, low = norms.backward(6, target_last, (), target_cotangent)
    upstream_rows, parts, pre_grads, unit_sums_one = feed_back_pair(
        1, moves.gather_near(low), target_ffn_state
    )
    up_parts, down_parts = feed_weight_pair(
        upstream_rows, target_ffn_state, target_norm_three, pre_grads
    )
    target_flow, sums_five, low = norms.backward(5, target_cross, parts, None, target_flow)
    upstream_rows = moves.gather(low)

    up_grad_one = split.settle(*up_parts)
    grads, cross_sums = attention_backward(
        order, attn_full[2], upstream_rows, cross_state, cross_layout, False
    )
    down_grad_one = split.settle(*down_parts)
    memory_arrived = moves.cross(
        *spread_rows(order, grads, attn_full[2], head_width, 3 * head_width, 2)
    )
    arrived = moves.cross(*spread_rows(order, grads, attn_full[2], 0, head_width, 2))
    near = spread_rows(order, grads, attn_full[2], head_width, 3 * head_width, 0)
    memory_parts = moves.parts(near, memory_arrived)
    near = spread_rows(order, grads, attn_full[2], 0, head_width, 0)
    parts = moves.parts(near, arrived)
    send, keep_two = attention_weights(
        order, target_norm_two, memory, upstream_rows, grads, cross_state[1]
    )
    arrived_two = split.send(send)
    source_flow, sums_two, low = norms.backward(2, source_last, memory_parts, source_cotangent)
    source_rows = moves.gather(lax.optimization_barrier((low, arrived))[0])
    target_flow, sums_four, low = norms.backward(4, target_mid, parts, None, target_flow)
    upstream_rows, parts, pre_grads, unit_sums_zero = feed_back_pair(
        0, source_rows, source_ffn_state, (arrived_two,)
    )
    self_upstream = moves.gather(low)
    attn_grad_two = split.settle(keep_two, arrived_two)
    up_parts, down_parts = feed_weight_pair(
        upstream_rows, source_ffn_state, source_norm_two, pre_grads
    )
    source_flow, sums_one, low = norms.backward(1, source_mid, parts, None, source_flow)
    upstream_rows = moves.gather(low)

    self_grads, self_sums = attention_backward(
        order, attn_full[1], self_upstream, self_state, self_layout, True
    )
    up_grad_zero = split.settle(*up_parts)
    self_arrived = moves.cross(
        *spread_rows(order, self_grads, attn_full[1], 0, 3 * head_width, 2), (upstream_rows[2],)
    )
    send, keep_one = attention_weights(
        order, target_norm_one, target_norm_one, self_upstream, self_grads, self_state[1]
    )
    arrived_one = split.send(send)
    grads, source_sums = attention_backward(
        order, attn_full[0], upstream_rows, source_attn_state, encoder_layout, False
    )
    down_grad_zero = split.settle(*down_parts)
    send, keep_zero = attention_weights(
        order, source_norm_one, source_norm_one, upstream_rows, grads, source_attn_state[1]
    )
    arrived_zero = split.send(send)
    arrived = moves.cross(
        *spread_rows(order, grads, attn_full[0], 0, 3 * head_width, 2), (arrived_one,)
    )
    attn_grad_one = split.settle(keep_one, arrived_one)
    near = spread_rows(order, grads, attn_full[0], 0, 3 * head_width, 0)
    parts = moves.parts(near, arrived)
    near = spread_rows(order, self_grads, attn_full[1], 0, 3 * head_width, 0)
    self_parts = moves.parts(near, self_arrived)
    target_grad, sums_three = norms.backward(
        3, target, self_parts, None, target_flow, low=False, last=True
    )
    source_grad, sums_zero = norms.backward(
        0, source, parts, None, source_flow, low=False, last=True
    )

    norm_sums = (sums_zero, sums_one, sums_two, sums_three, sums_four, sums_five, sums_six)
    vector_rows = [sums[0:1] for sums in norm_sums] + [sums[1:2] for sums in norm_sums]
    vector_rows += [sums[2:3] for sums in (sums_one, sums_four, sums_five, sums_two, sums_six)]
    attn_grad_zero = split.settle(keep_zero, arrived_zero)
    own_rows = [source_sums, self_sums, cross_sums]
    for sums in (unit_sums_zero, unit_sums_one):
        cut = sums.reshape(head_width // shard_rows, -1, shard_rows).transpose(1, 0, 2)
        own_rows.append(cut.reshape(-1, head_width))
    own_rows = jnp.concatenate(own_rows, axis=0)
    columns = jnp.arange(moves.count * head_width, dtype=jnp.int32) // head_width
    own_rows = jnp.where(columns[None, :] == moves.me, jnp.tile(own_rows, (1, moves.count)), 0.0)
    small_sum = split.spread(moves.total(jnp.concatenate(vector_rows + [own_rows], axis=0)))

    attn_grads = (attn_grad_zero, attn_grad_one, attn_grad_two)
    up_grads = (up_grad_zero, up_grad_one)
    down_grads = (down_grad_zero, down_grad_one)
    local_squares = sum_of_squares(
        order, (*attn_grads, *up_grads, *down_grads), small_sum, moves.count
    )
    square_sum = split.total(moves.total(local_squares))
    grad_norm = jnp.sqrt(square_sum)[0, 0]
    rate_in, rate_out, rate_down = (
        0.5 * D ** (-0.5),
        0.5 * (D // 8) ** (-0.5),
        0.5 * FF ** (-0.5),
    )

    def attention_cut(refs, step):
        values = choose(refs, step)
        inputs = [
            values[:, which * head_width : (which + 1) * head_width] for which in range(3)
        ]
        return jnp.stack(inputs), values[:, 3 * head_width :].T

    def up_cut(refs, step):
        return (choose(refs, step),)

    def down_cut(refs, step):
        return (choose(refs, step).T,)

    attn_new = update(
        order,
        square_sum,
        attn_grads,
        (
            (attention_in, first_attention_in, second_attention_in),
            (attention_out, first_attention_out, second_attention_out),
        ),
        (rate_in, rate_out),
        attention_cut,
        "update_attention",
    )
    up_new = update(
        order,
        square_sum,
        up_grads,
        ((hidden_in, first_hidden_in, second_hidden_in),),
        (rate_in,),
        up_cut,
        "update_up",
    )
    down_new = update(
        order,
        square_sum,
        down_grads,
        ((hidden_out, first_hidden_out, second_hidden_out),),
        (rate_down,),
        down_cut,
        "update_down",
    )
    *small_new, bias_grad = small_update(
        order,
        square_sum,
        small_sum,
        (vectors, first_vectors, second_vectors),
        (hidden_bias, first_hidden_bias, second_hidden_bias),
    )
    return (
        encoder_output,
        decoder_output,
        source_grad,
        target_grad,
        grad_norm,
        *attn_new,
        *up_new,
        *down_new,
        *small_new,
        bias_grad,
    )


def solution(mesh):
    placed = (
        P(("dp", "tensor"), None),
        P(("dp", "tensor"), None),
        P("dp", None),
        P("dp", None),
        P("dp"),
        P(("dp", "tensor"), None),
        P(("dp", "tensor"), None),
        P(None, None, "dp", "tensor"),
        P(None, "tensor", "dp"),
        P(None, "dp", "tensor"),
        P(None, "tensor", "dp"),
        P(None, "dp"),
        P(None, "dp"),
        P(None, None, "dp", "tensor"),
        P(None, "tensor", "dp"),
        P(None, "dp", "tensor"),
        P(None, "tensor", "dp"),
        P(None, "dp"),
        P(None, "dp"),
        P(None, None, "dp", "tensor"),
        P(None, "tensor", "dp"),
        P(None, "dp", "tensor"),
        P(None, "tensor", "dp"),
        P(None, "dp"),
        P(None, "dp"),
    )
    return jax.shard_map(
        body,
        mesh=mesh,
        in_specs=placed,
        out_specs=(
            P(("dp", "tensor"), None),
            P(("dp", "tensor"), None),
            P(("dp", "tensor"), None),
            P(("dp", "tensor"), None),
            P(),
            P(None, None, "dp", "tensor"),
            P(None, None, "dp", "tensor"),
            P(None, None, "dp", "tensor"),
            P(None, "tensor", "dp"),
            P(None, "tensor", "dp"),
            P(None, "tensor", "dp"),
            P(None, "dp", "tensor"),
            P(None, "dp", "tensor"),
            P(None, "dp", "tensor"),
            P(None, "tensor", "dp"),
            P(None, "tensor", "dp"),
            P(None, "tensor", "dp"),
            P(None, "dp"),
            P(None, "dp"),
            P(None, "dp"),
            P(None, "dp"),
            P(None, "dp"),
            P(None, "dp"),
            P(None, "dp"),
        ),
        check_vma=False,
    )
```

```python
from functools import partial

import jax
import jax.numpy as jnp
from jax import lax
from jax.experimental import pallas as pl
from jax.experimental.pallas import tpu as pltpu
from jax.sharding import PartitionSpec as P

D = 1024
FF = 4096
L = 1024
ITEMS = 8
STEP = 10
HEAD = 64
ITEM = 128


NORM_EPS = 1e-05
CLIP_NORM = 1.0
BETA_FIRST = 0.9
BETA_SECOND = 0.999
ADAM_EPS = 1e-08
MATRIX_DECAY = 0.01
MASKED = -1e30

BF16 = jnp.bfloat16
F32 = jnp.float32
VECTOR_RATE = 0.3
SMALL = 16384
VMEM_BYTES = 24 * 1024 * 1024


class TensorMoves:
    def __init__(self, order):
        self.order = order
        self.count = lax.axis_size("tensor")
        assert self.count == 4
        self.me = lax.axis_index("tensor")

    def swap(self, values, bit):
        pairs = [(index, index ^ bit) for index in range(self.count)]
        return lax.ppermute(values, "tensor", pairs)

    def gather(self, shard):
        return self.gather_far(self.gather_near(shard))

    def gather_near(self, shard):
        return shard, self.swap(shard, 1), self.swap(shard, 2)

    def gather_far(self, rows):
        return *rows, self.swap(rows[2], 1)

    def gather_late(self, rows):
        return *rows, self.swap(self.order.after_last(rows[2]), 1)

    def cross(self, send, keep, first=()):
        send = lax.optimization_barrier((send, first))[0]
        crossing = (keep + self.swap(send, 1).astype(F32)).astype(BF16)
        self.order.before_next(crossing)
        return self.swap(crossing, 2)

    def parts(self, near, arrived):
        first, second, keep = near
        return keep, self.swap(first, 1), self.swap(second, 1), arrived

    @property
    def steps(self):
        return [lambda values, bit=bit: values + self.swap(values, bit) for bit in (1, 2)]

    def total(self, values):
        for step in self.steps:
            values = step(values)
        return values


class PlainRows:
    def __init__(self, order):
        self.order = order
        self.count = lax.axis_size("dp")
        self.me = lax.axis_index("dp")
        self.y = None

    def start(self, shard):
        return lax.all_gather(shard, "dp", axis=0, tiled=True)

    def finish(self, full):
        half = full.shape[0] // 2
        return full[:half], full[half:]

    def blocks(self, stacked, first, count):
        return [
            lax.dynamic_index_in_dim(stacked, first + index, 0, False) for index in range(count)
        ]

    def send(self, far_part):
        return far_part

    def settle(self, near_part, arrived):
        values = jnp.concatenate([near_part, arrived.astype(F32)], 0)
        return lax.psum_scatter(values, "dp", scatter_dimension=0, tiled=True)

    def stack(self, shard):
        return lax.all_gather(shard, "dp", axis=0)

    def spread(self, values):
        return lax.psum_scatter(values, "dp", scatter_dimension=1, tiled=True)

    @property
    def steps(self):
        return [lambda values: lax.psum(values, "dp")]

    def total(self, values):
        for step in self.steps:
            values = step(values)
        return values


class CrossRows(PlainRows):
    ALONG_Z = [[0, 2, 4, 6], [1, 3, 5, 7]]

    def __init__(self, order):
        super().__init__(order)
        self.z = self.me // 2
        self.y = self.me % 2

    def swap(self, values, bits):
        pairs = [(index, index ^ bits) for index in range(self.count)]
        return lax.ppermute(values, "dp", pairs)

    def start(self, shard):
        return lax.all_gather(shard, "dp", axis=0, tiled=True, axis_index_groups=self.ALONG_Z)

    def finish(self, near):
        return near, self.swap(near, 1)

    def blocks(self, stacked, first, count):
        assert count == 2
        near = lax.dynamic_index_in_dim(stacked, first // 2, 0, False)
        far = lax.dynamic_index_in_dim(stacked, first // 2 + 4, 0, False)
        even = self.y == 0
        return [jnp.where(even, near, far), jnp.where(even, far, near)]

    def send(self, far_part):
        return self.swap(far_part, 1)

    def settle(self, near_part, arrived):
        near_part, arrived = self.order.after_last((near_part, arrived))
        part = (near_part + arrived.astype(F32)).astype(BF16)
        self.order.before_next(part)
        return lax.psum_scatter(
            part, "dp", scatter_dimension=0, tiled=True, axis_index_groups=self.ALONG_Z
        )

    def stack(self, shard):
        pieces = jnp.stack([shard] + [self.swap(shard, bits) for bits in (2, 4, 6)])
        near = jnp.stack(
            [lax.dynamic_index_in_dim(pieces, self.z ^ index, 0, False) for index in range(4)]
        )
        return jnp.concatenate([near, self.swap(near, 1)], axis=0)

    def spread(self, values):
        rows = values.shape[0]
        blocks = values.reshape(rows, 4, 2, -1)
        first, second = [blocks[:, :, index].reshape(rows, -1) for index in range(2)]
        even = self.y == 0
        part = jnp.where(even, first, second) + self.swap(jnp.where(even, second, first), 1)
        size = part.shape[1] // 4
        total = lax.dynamic_slice_in_dim(part, self.z * size, size, 1)
        for bits in (2, 4, 6):
            sent = lax.dynamic_slice_in_dim(part, (self.z ^ (bits // 2)) * size, size, 1)
            total = total + self.swap(sent, bits)
        return total

    @property
    def steps(self):
        return [lambda values, bits=bits: values + self.swap(values, bits) for bits in (1, 2, 4)]


def item_codes(row_kind, lengths, places):
    items = jnp.where(row_kind == 1, 0, places // ITEM)
    within = jnp.where(row_kind == 1, places, places % ITEM)
    limit = jnp.zeros_like(places)
    for index in range(ITEMS):
        limit = jnp.where(items == index, lengths[index], limit)
    return items, jnp.where(within < limit, items, -1)


def dot_nn(left, right):
    return jnp.dot(left, right, preferred_element_type=F32)


def dot_nt(left, right):
    return lax.dot_general(left, right, (((1,), (1,)), ((), ())), preferred_element_type=F32)


def dot_tn(left, right):
    return lax.dot_general(left, right, (((0,), (0,)), ((), ())), preferred_element_type=F32)


def wide_dot(rows, near, far):
    half = near.shape[0]
    return dot_nn(rows[:, :half], near[...]) + dot_nn(rows[:, half:], far[...])


class Load:
    def __init__(self, shape, start=None):
        self.shape = shape
        self.start = start or (0,) * len(shape)


class Loaded:
    def __init__(self, copy, buffer, step):
        self.copy = copy
        self.buffer = buffer
        self.step = step
        self.waited = False

    @property
    def shape(self):
        return self.buffer.shape

    def ready(self):
        if not self.waited:
            self.waited = True
            pl.when(self.step == 0)(self.copy.wait)

    def wait_here(self):
        self.waited = True
        self.copy.wait()

    def __getitem__(self, where):
        self.ready()
        return self.buffer[where]


class Order:
    def __init__(self):
        self.marks = ()

    def call(self, kernel, grid, in_specs, out_specs, out_shapes, scratch, flops, moved, name):
        marks = [
            pltpu.with_memory_space_constraint(mark, pltpu.HBM) if mark.size > SMALL else mark
            for mark in self.marks
        ]
        loads = [(place, spec) for place, spec in enumerate(in_specs) if isinstance(spec, Load)]
        hbm = pl.BlockSpec(memory_space=pltpu.HBM)

        def marked(*refs):
            refs = list(refs[len(marks) :])
            step = pl.program_id(0)
            loaded = []
            if loads:
                *refs, semaphores = refs
                buffers = refs[-len(loads) :]
                refs = refs[: -len(loads)]
                for index, (place, spec) in enumerate(loads):
                    source = refs[place].at[
                        tuple(pl.ds(first, size) for first, size in zip(spec.start, spec.shape))
                    ]
                    copy = pltpu.make_async_copy(source, buffers[index], semaphores.at[index])
                    loaded.append(Loaded(copy, buffers[index], step))
                    refs[place] = loaded[-1]

                @pl.when(step == 0)
                def _():
                    for item in loaded:
                        item.copy.start()

            kernel(*refs)
            for item in loaded:
                item.ready()

        def run(*operands):
            operands = list(operands)
            buffers = []
            for place, spec in loads:
                buffers.append(pltpu.VMEM(spec.shape, operands[place].dtype))
                operands[place] = pltpu.with_memory_space_constraint(operands[place], pltpu.HBM)
            if loads:
                buffers.append(pltpu.SemaphoreType.DMA((len(loads),)))
            results = pl.pallas_call(
                marked,
                grid=grid,
                in_specs=[
                    hbm if mark.size > SMALL else pl.BlockSpec(memory_space=pl.ANY)
                    for mark in marks
                ]
                + [hbm if isinstance(spec, Load) else spec for spec in in_specs],
                out_specs=out_specs,
                out_shape=out_shapes,
                scratch_shapes=list(scratch) + buffers,
                compiler_params=pltpu.CompilerParams(
                    vmem_limit_bytes=VMEM_BYTES,
                    dimension_semantics=("arbitrary",) * len(grid),
                ),
                cost_estimate=pl.CostEstimate(
                    flops=flops, bytes_accessed=moved, transcendentals=0
                ),
                name=name,
            )(*marks, *operands)
            self.marks = (min(jax.tree.leaves(results), key=lambda leaf: leaf.size),)
            return results

        return run

    def before_next(self, value):
        self.marks += (value,)

    def after_last(self, value):
        return lax.optimization_barrier((value, self.marks))[0]


def whole(shape):
    return pl.BlockSpec(
        shape, lambda step: (0,) * len(shape), pipeline_mode=pl.Buffered(buffer_count=1)
    )


def pair_bias(layout_ref, start, rows, causal):
    turned = layout_ref[...].T
    queries = pl.ds(start, rows)
    allowed = turned[:, 0:1] == layout_ref[2:3, queries]
    if causal:
        allowed = allowed & (turned[:, 1:2] <= layout_ref[1:2, queries])
    return jnp.where(allowed, 0.0, MASKED).astype(F32)


def head_rows_only(block, head, scale=None):
    lanes = lax.broadcasted_iota(jnp.int32, block.shape, 1) // HEAD
    if scale is not None:
        block = block * jnp.asarray(scale, block.dtype)
    return jnp.where(lanes == head, block, jnp.zeros_like(block))


def over_keys(combine, values):
    parts = values.reshape(8, values.shape[0] // 8, values.shape[1])
    return combine(combine(parts, axis=0), axis=0, keepdims=True)


def attend_block(queries, key_rows, values_turned, bias, heads):
    scores = []
    for head in range(heads):
        picked = head_rows_only(queries, head, HEAD ** (-0.5))
        scores.append(dot_nt(key_rows, picked) + bias)
    largest = [over_keys(jnp.max, score) for score in scores]
    contexts = []
    totals = []
    for head in range(heads):
        weights = jnp.exp(scores[head] - largest[head])
        total = over_keys(jnp.sum, weights)
        context = dot_nn(
            values_turned[head * HEAD : (head + 1) * HEAD, :], weights.astype(BF16)
        )
        contexts.append(context * (1.0 / total))
        totals.append(largest[head] + jnp.log(total))
    return jnp.concatenate(contexts, axis=0).T, jnp.concatenate(totals, axis=0)


def out_parts(rows, out_near, out_far, step, send_refs, keep_ref):
    half = out_near.shape[0]
    near = dot_nt(rows, out_near)
    far = dot_nt(rows, out_far)

    @pl.when(step == 0)
    def _():
        if len(send_refs) == 1:
            send_refs[0][:, :half] = near.astype(BF16)
            send_refs[0][:, half:] = far.astype(BF16)
        else:
            send_refs[0][...] = near.astype(BF16)
            send_refs[1][...] = far.astype(BF16)

    @pl.when(step == 1)
    def _():
        keep_ref[:, :half] = near
        keep_ref[:, half:] = far


def part_shapes(rows, half, halves):
    sends = [(rows, half)] * 2 if halves else [(rows, 2 * half)]
    return sends + [(rows, 2 * half)], [BF16] * len(sends) + [F32]


def part_outs(rows, half, halves):
    shapes, kinds = part_shapes(rows, half, halves)
    return [jax.ShapeDtypeStruct(shape, kind) for shape, kind in zip(shapes, kinds)]


def part_specs(rows, half, halves):
    return [whole(shape) for shape in part_shapes(rows, half, halves)[0]]


def attend_tail(
    step, qkv_ref, turned_ref, layout_ref, causal, out_near, out_far, first_row, outs, heads
):
    context_ref, total_ref, *send_refs, keep_ref = outs
    rows = keep_ref.shape[0]
    wide = context_ref.shape[1]
    start = pl.multiple_of(first_row + (1 - step) * rows, rows)
    bias = pair_bias(layout_ref, start, rows, causal)
    context, totals = attend_block(
        qkv_ref[pl.ds(start, rows), :wide],
        qkv_ref[:, wide : 2 * wide],
        turned_ref[...],
        bias,
        heads,
    )
    context = context.astype(BF16)
    context_ref[...] = context
    total_ref[...] = totals
    out_parts(context, out_near, out_far, step, send_refs, keep_ref)


def attend_far_kernel(causal, is_cross, heads, *refs):
    normed_refs = memory_refs = refs[:4]
    refs = refs[4:]
    if is_cross:
        memory_refs, refs = refs[:4], refs[4:]
    full_near_ref, full_far_ref, bias_ref = refs[:3]
    layout_ref = refs[3]
    qkv_ref, context_ref, *outs, turned_ref = refs[4:]
    step = pl.program_id(0)
    rows = outs[-1].shape[0]
    wide = context_ref.shape[1]

    @pl.when(step == 0)
    def _():
        def project(source_refs, begin, end, biases):
            for index in range(4):
                part = source_refs[index][...]
                values = wide_dot(part, full_near_ref[:, begin:end], full_far_ref[:, begin:end])
                span = slice(index * rows, (index + 1) * rows)
                for place, which in enumerate(range(begin // wide, end // wide)):
                    piece = values[:, place * wide : (place + 1) * wide]
                    if biases[which] is not None:
                        piece = piece + bias_ref[biases[which] : biases[which] + 1, :]
                    qkv_ref[span, which * wide : (which + 1) * wide] = piece.astype(BF16)

        biases = (0, None, 1)
        if is_cross:
            project(normed_refs, 0, wide, biases)
            project(memory_refs, wide, 3 * wide, biases)
        else:
            project(normed_refs, 0, 3 * wide, biases)
        turned_ref[...] = qkv_ref[:, 2 * wide :].T

    attend_tail(
        step,
        qkv_ref,
        turned_ref,
        layout_ref,
        causal,
        full_near_ref[:, 3 * wide :],
        full_far_ref[:, 3 * wide :],
        2 * rows,
        (context_ref, *outs),
        heads,
    )


def attend_near_kernel(causal, heads, *refs):
    qkv_ref, out_near_ref, out_far_ref = refs[:3]
    layout_ref = refs[3]
    context_ref, *outs, turned_ref = refs[4:]
    step = pl.program_id(0)
    wide = context_ref.shape[1]

    @pl.when(step == 0)
    def _():
        turned_ref[...] = qkv_ref[:, 2 * wide :].T

    attend_tail(
        step,
        qkv_ref,
        turned_ref,
        layout_ref,
        causal,
        out_near_ref[...],
        out_far_ref[...],
        0,
        (context_ref, *outs),
        heads,
    )


def attention_forward(order, moves, full, normed, memory, biases, layout, causal, first):
    length = layout.shape[1]
    rows = length // 4
    width = full[0].shape[1]
    wide = width // 4
    heads = wide // HEAD
    half = full[0].shape[0]
    is_cross = memory is not normed
    sources = tuple(normed) + (tuple(memory) if is_cross else ())
    pairs = 4 * rows * length // 2 * wide * heads

    half_outs = [
        jax.ShapeDtypeStruct((2 * rows, wide), BF16),
        jax.ShapeDtypeStruct((heads, 2 * rows), F32),
    ]
    half_specs = [
        pl.BlockSpec((rows, wide), lambda step: (1 - step, 0)),
        pl.BlockSpec((heads, rows), lambda step: (0, 1 - step)),
    ]
    turned = pltpu.VMEM((wide, length), BF16)
    qkv, context_far, totals_far, send_far, keep_far = order.call(
        partial(attend_far_kernel, causal, is_cross, heads),
        (2,),
        [whole((rows, 2 * half))] * len(sources)
        + [whole((half, width))] * 2
        + [whole(biases.shape), whole(layout.shape)],
        [whole((length, 3 * wide))] + half_specs + part_specs(rows, half, False),
        [jax.ShapeDtypeStruct((length, 3 * wide), BF16)]
        + half_outs
        + part_outs(rows, half, False),
        [turned],
        2 * length * 2 * half * 3 * wide + pairs,
        12 * length * 2 * half,
        "attend_far",
    )(*sources, *full, biases, layout)
    arrived = moves.cross(send_far, keep_far, first)
    yield
    context_near, totals_near, *near = order.call(
        partial(attend_near_kernel, causal, heads),
        (2,),
        [whole((length, 3 * wide))]
        + [pl.BlockSpec((half, wide), lambda step: (0, 3))] * 2
        + [whole(layout.shape)],
        half_specs + part_specs(rows, half, True),
        half_outs + part_outs(rows, half, True),
        [turned],
        pairs,
        6 * length * 2 * half,
        "attend_near",
    )(qkv, *full, layout)
    branch = moves.parts(near, arrived)
    yield branch, (qkv, (context_near, context_far), (totals_near, totals_far))


def attend_back_kernel(causal, heads, *refs):
    qkv_ref, first_ref, out_near_ref, out_far_ref = refs[:4]
    context_refs, total_refs, layout_ref = refs[4:6], refs[6:8], refs[8]
    grad_refs = (first_ref, *refs[9:12])
    grads_ref, sums_ref = refs[12:14]
    keys_turned_ref, key_sum_ref, value_sum_ref, grad_ref, context_ref, total_ref = refs[14:]
    step = pl.program_id(0)
    rows = context_ref.shape[0]
    wide = context_ref.shape[1]
    scale = HEAD ** (-0.5)

    @pl.when(step == 0)
    def _():
        keys_turned_ref[...] = qkv_ref[:, wide : 2 * wide].T
        key_sum_ref[...] = jnp.zeros_like(key_sum_ref)
        value_sum_ref[...] = jnp.zeros_like(value_sum_ref)

    for loaded in (*context_refs, *total_refs):
        loaded.ready()
    for index in range(4):

        @pl.when(step == index)
        def _(index=index):
            span = slice((index % 2) * rows, (index % 2 + 1) * rows)
            grad_refs[index].wait_here()
            grad_ref[...] = grad_refs[index][...]
            context_ref[...] = context_refs[index // 2][span, :]
            total_ref[...] = total_refs[index // 2][:, span]

    context_grad = wide_dot(grad_ref[...], out_near_ref, out_far_ref).astype(BF16)
    products = (context_grad.astype(F32) * context_ref[...].astype(F32)).T
    start = pl.multiple_of(step * rows, rows)
    bias = pair_bias(layout_ref, start, rows, causal)
    queries = qkv_ref[pl.ds(start, rows), :wide]
    key_rows = qkv_ref[:, wide : 2 * wide]
    value_rows = qkv_ref[:, 2 * wide :]
    query_grads = []
    for head in range(heads):
        span = slice(head * HEAD, (head + 1) * HEAD)
        picked = head_rows_only(queries, head, scale)
        picked_grad = head_rows_only(context_grad, head)
        scores = dot_nt(key_rows, picked) + bias
        weights = jnp.exp(scores - total_ref[head : head + 1, :])
        weight_grad = dot_nt(value_rows, picked_grad)
        diagonal = jnp.sum(products[span, :], axis=0, keepdims=True)
        score_grad = (weights * (weight_grad - diagonal)).astype(BF16)
        value_sum_ref[...] += dot_nn(weights.astype(BF16), picked_grad)
        key_sum_ref[...] += dot_nn(score_grad, picked)
        query_grads.append(dot_nn(keys_turned_ref[span, :], score_grad))
    query_grad = jnp.concatenate(query_grads, axis=0).T * scale
    grads_ref[pl.ds(start, rows), :wide] = query_grad.astype(BF16)

    @pl.when(step == 3)
    def _():
        grads_ref[:, wide : 2 * wide] = key_sum_ref[...].astype(BF16)
        grads_ref[:, 2 * wide :] = value_sum_ref[...].astype(BF16)
        for place, begin in ((0, 0), (1, 2 * wide)):
            values = grads_ref[:, begin : begin + wide].astype(F32)
            sums_ref[place : place + 1, :] = jnp.sum(values, axis=0, keepdims=True)


def spread_kernel(begin, end, rows_ref, near_ref, far_ref, *outs):
    step = pl.program_id(0)
    part = rows_ref[:, begin:end]
    out_parts(part, near_ref[:, begin:end], far_ref[:, begin:end], step, outs[:-1], outs[-1])


def spread_rows(order, grads, full, begin, end, first):
    rows = grads.shape[0] // 4
    half = full[0].shape[0]
    wide = grads.shape[1]
    return order.call(
        partial(spread_kernel, begin, end),
        (2,),
        [pl.BlockSpec((rows, wide), lambda step: (first + 1 - step, 0))]
        + [whole((half, wide))] * 2,
        part_specs(rows, half, first == 0),
        part_outs(rows, half, first == 0),
        [],
        4 * rows * 2 * half * (end - begin),
        6 * rows * 2 * half + 4 * half * wide,
        "spread_rows",
    )(grads, *full)


def later_half(step, size):
    return pl.ds(pl.multiple_of((1 - step) * size, size), size)


def rows_dot(left_refs, right, begin, end, columns=slice(None)):
    total = None
    for index, left_ref in enumerate(left_refs):
        rows = left_ref.shape[0]
        if isinstance(right, tuple):
            first = (index % 2) * rows
            part = right[index // 2][first : first + rows, begin:end]
        else:
            part = right[index * rows : (index + 1) * rows, begin:end]
        product = dot_tn(left_ref[:, columns], part)
        total = product if total is None else total + product
    return total


def attention_weight_kernel(is_cross, *refs):
    normed_refs = memory_refs = refs[:4]
    refs = refs[4:]
    if is_cross:
        memory_refs, refs = refs[:4], refs[4:]
    upstream_refs, grads_ref, context_refs, outs = refs[:4], refs[4], refs[5:7], refs[7:]
    send_ref, keep_ref = outs
    step = pl.program_id(0)
    wide = context_refs[0].shape[1]
    columns = later_half(step, send_ref.shape[0])
    if is_cross:
        pieces = [
            rows_dot(normed_refs, grads_ref, 0, wide, columns),
            rows_dot(memory_refs, grads_ref, wide, 3 * wide, columns),
        ]
    else:
        pieces = [rows_dot(normed_refs, grads_ref, 0, 3 * wide, columns)]
    pieces.append(rows_dot(upstream_refs, tuple(context_refs), 0, wide, columns))

    @pl.when(step == 0)
    def _():
        send_ref[...] = jnp.concatenate(pieces, axis=1).astype(BF16)

    @pl.when(step == 1)
    def _():
        keep_ref[...] = jnp.concatenate(pieces, axis=1)


def attention_weights(order, normed, memory, upstream, grads, contexts):
    rows, width = normed[0].shape
    wide = contexts[0].shape[1]
    is_cross = memory is not normed
    sources = tuple(normed) + (tuple(memory) if is_cross else ()) + tuple(upstream)
    half = width // 2
    outs = (half, 4 * wide)
    return order.call(
        partial(attention_weight_kernel, is_cross),
        (2,),
        [Load((rows, width))] * len(sources)
        + [whole(grads.shape)]
        + [Load((2 * rows, wide))] * 2,
        [whole(outs)] * 2,
        [jax.ShapeDtypeStruct(outs, BF16), pltpu.HBM(outs, F32)],
        [],
        8 * rows * width * 4 * wide,
        2 * rows * width * (len(sources) + 4) + 6 * half * 4 * wide,
        "attention_weights",
    )(*sources, grads, *contexts)


def attention_backward(order, full, upstream_rows, stored, layout, causal):
    qkv, contexts, totals = stored
    length = qkv.shape[0]
    rows = length // 4
    wide = qkv.shape[1] // 3
    heads = wide // HEAD
    half = full[0].shape[0]
    return order.call(
        partial(attend_back_kernel, causal, heads),
        (4,),
        [Load(qkv.shape), Load((rows, 2 * half))]
        + [Load((half, wide), (0, 3 * wide))] * 2
        + [Load((2 * rows, wide))] * 2
        + [Load((heads, 2 * rows))] * 2
        + [Load(layout.shape)]
        + [Load((rows, 2 * half))] * 3,
        [whole(qkv.shape), whole((2, wide))],
        [jax.ShapeDtypeStruct(qkv.shape, BF16), jax.ShapeDtypeStruct((2, wide), F32)],
        [
            pltpu.VMEM((wide, length), BF16),
            pltpu.VMEM((length, wide), F32),
            pltpu.VMEM((length, wide), F32),
            pltpu.VMEM((rows, 2 * half), BF16),
            pltpu.VMEM((rows, wide), BF16),
            pltpu.VMEM((heads, rows), F32),
        ],
        10 * length * length * wide * heads,
        12 * length * 2 * half,
        "attend_back",
    )(qkv, upstream_rows[0], *full, *contexts, *totals, layout, *upstream_rows[1:])


GELU_SCALE = 0.7978845608028654
GELU_CUBE = 0.044715


def feed_kernel(own_ref, near_ref, up_near, up_far, down_near, down_far, bias_ref, *outs):
    activated_ref, slope_ref, *send_refs, keep_ref = outs
    step = pl.program_id(0)
    rows = jnp.where(step == 0, near_ref[...], own_ref[...])
    pre_act = wide_dot(rows, up_near[...], up_far[...]) + bias_ref[...]
    square = pre_act * pre_act
    bent = jnp.tanh(GELU_SCALE * pre_act * (1.0 + GELU_CUBE * square))
    activated = (0.5 * pre_act * (1.0 + bent)).astype(BF16)
    inner = GELU_SCALE * (1.0 + 3.0 * GELU_CUBE * square)
    slope = 0.5 * (1.0 + bent) + 0.5 * pre_act * (1.0 - bent * bent) * inner
    activated_ref[...] = activated
    slope_ref[...] = slope.astype(BF16)
    out_parts(activated, down_near[...], down_far[...], step, send_refs, keep_ref)


def feed_forward(order, up_full, down_full, pair_rows, unit_bias, halves):
    rows = pair_rows[0].shape[0]
    half, units = up_full[0].shape
    return order.call(
        feed_kernel,
        (2,),
        [whole((rows, 2 * half))] * 2 + [whole((half, units))] * 4 + [whole((1, units))],
        [pl.BlockSpec((rows, units), lambda step: (1 - step, 0))] * 2
        + part_specs(rows, half, halves),
        [jax.ShapeDtypeStruct((2 * rows, units), BF16)] * 2 + part_outs(rows, half, halves),
        [],
        16 * rows * half * units,
        20 * rows * units + 8 * half * units,
        "feed_forward",
    )(*pair_rows, *up_full, *down_full, unit_bias)


def feed_back_kernel(
    own_ref, near_ref, slope_ref, up_near, up_far, down_near, down_far, *outs
):
    grad_ref, sum_ref, *send_refs, keep_ref = outs
    step = pl.program_id(0)
    rows = jnp.where(step == 0, near_ref[...], own_ref[...])
    act_grad = wide_dot(rows, down_near[...], down_far[...])
    pre_grad = (act_grad * slope_ref[...].astype(F32)).astype(BF16)
    grad_ref[...] = pre_grad

    @pl.when(step == 0)
    def _():
        sum_ref[...] = jnp.zeros_like(sum_ref)

    sum_ref[...] += jnp.sum(pre_grad.astype(F32), axis=0, keepdims=True)
    out_parts(pre_grad, up_near[...], up_far[...], step, send_refs, keep_ref)


def feed_weight_kernel(*refs):
    left_refs, right_refs, (send_ref, keep_ref) = refs[:4], refs[4:6], refs[6:]
    step = pl.program_id(0)
    part = rows_dot(left_refs, tuple(right_refs), 0, send_ref.shape[1])

    @pl.when(step == 0)
    def _():
        send_ref[...] = part.astype(BF16)

    @pl.when(step == 1)
    def _():
        keep_ref[...] = part


def feed_weights(order, left, right):
    rows, width = left[0].shape
    units = right[0].shape[1]
    half = width // 2
    outs = (half, units)
    return order.call(
        feed_weight_kernel,
        (2,),
        [pl.BlockSpec((rows, half), lambda step: (0, 1 - step))] * 4
        + [whole((2 * rows, units))] * 2,
        [whole(outs)] * 2,
        [jax.ShapeDtypeStruct(outs, BF16), pltpu.HBM(outs, F32)],
        [],
        8 * rows * width * units,
        8 * rows * (width + units) + 6 * half * units,
        "feed_weights",
    )(*left, *right)


def feed_backward(order, up_full, down_full, pair_rows, slope, halves):
    rows = pair_rows[0].shape[0]
    half, units = up_full[0].shape
    return order.call(
        feed_back_kernel,
        (2,),
        [whole((rows, 2 * half))] * 2
        + [pl.BlockSpec((rows, units), lambda step: (1 - step, 0))]
        + [whole((half, units))] * 4,
        [pl.BlockSpec((rows, units), lambda step: (1 - step, 0)), whole((1, units))]
        + part_specs(rows, half, halves),
        [
            jax.ShapeDtypeStruct((2 * rows, units), BF16),
            jax.ShapeDtypeStruct((1, units), F32),
        ]
        + part_outs(rows, half, halves),
        [],
        16 * rows * half * units,
        20 * rows * units + 8 * half * units,
        "feed_backward",
    )(*pair_rows, slope, *up_full, *down_full)


def attention_shard_kernel(in_ref, out_ref, shard_ref):
    wide = in_ref.shape[3]
    for which in range(3):
        shard_ref[:, which * wide : (which + 1) * wide] = in_ref[0, which].astype(BF16)
    shard_ref[:, 3 * wide :] = out_ref[0].T.astype(BF16)


def attention_shard(order, attention_in, attention_out, slot_id):
    rows, wide = attention_in.shape[2:]
    return order.call(
        attention_shard_kernel,
        (1,),
        [
            pl.BlockSpec((1, 3, rows, wide), lambda step: (slot_id, 0, 0, 0)),
            pl.BlockSpec((1, wide, rows), lambda step: (slot_id, 0, 0)),
        ],
        whole((rows, 4 * wide)),
        jax.ShapeDtypeStruct((rows, 4 * wide), BF16),
        [],
        0,
        24 * rows * wide,
        "attention_shard",
    )(attention_in, attention_out)


def feed_shard_kernel(up_ref, down_ref, up_shard_ref, down_shard_ref):
    up_shard_ref[...] = up_ref[0].astype(BF16)
    down_shard_ref[...] = down_ref[0].T.astype(BF16)


def feed_shard(order, hidden_in, hidden_out, slot_id):
    rows, units = hidden_in.shape[1:]
    return order.call(
        feed_shard_kernel,
        (1,),
        [
            pl.BlockSpec((1, rows, units), lambda step: (slot_id, 0, 0)),
            pl.BlockSpec((1, units, rows), lambda step: (slot_id, 0, 0)),
        ],
        [whole((rows, units))] * 2,
        [jax.ShapeDtypeStruct((rows, units), BF16)] * 2,
        [],
        0,
        12 * rows * units,
        "feed_shard",
    )(hidden_in, hidden_out)


class Norms:
    def __init__(self, order, table, y):
        self.order = order
        self.table = table
        self.y = jnp.zeros((1,), jnp.int32) if y is None else y.astype(jnp.int32).reshape(1)
        self.ordered = y is None

    def enter(self, flag, values):
        if self.ordered:
            return values
        size = values.shape[1] // 8
        blocks = [values[:, index * size : (index + 1) * size] for index in range(8)]
        first = jnp.concatenate(blocks[0::2], axis=1)
        second = jnp.concatenate(blocks[1::2], axis=1)
        return jnp.concatenate(
            [jnp.where(flag == 0, first, second), jnp.where(flag == 0, second, first)], axis=1
        )

    def leave(self, flag, values):
        if self.ordered:
            return values
        half = values.shape[1] // 2
        near, far = values[:, :half], values[:, half:]
        first = jnp.where(flag == 0, near, far)
        second = jnp.where(flag == 0, far, near)
        size = half // 4
        blocks = []
        for index in range(4):
            span = slice(index * size, (index + 1) * size)
            blocks += [first[:, span], second[:, span]]
        return jnp.concatenate(blocks, axis=1)

    def sum_parts(self, parts):
        keep, first, second, arrived = [part.astype(F32) for part in parts]
        return keep + jnp.concatenate([first, second], axis=1) + arrived

    def call(self, compute, operands, free, outs, sums, name):
        rows, width = operands[0].shape
        blocks = 4
        block = rows // blocks
        count = len(operands)

        def kernel(flag_ref, *refs):
            in_refs, refs = refs[:count], refs[count:]
            table_ref, refs = refs[0], refs[1:]
            out_refs, refs = refs[: len(outs)], refs[len(outs) :]
            if sums:
                sums_ref, refs = refs[0], refs[1:]
            in_buffers, refs = refs[:count], refs[count:]
            out_buffers, (in_marks, out_marks) = refs[: len(outs)], refs[len(outs) :]

            def span(index):
                return pl.ds(index * block, block)

            arriving = [
                [
                    pltpu.make_async_copy(
                        ref.at[span(index)], buffer.at[span(index)], in_marks.at[place, index]
                    )
                    for place, (ref, buffer) in enumerate(zip(in_refs, in_buffers))
                ]
                for index in range(blocks)
            ]
            for copies in arriving:
                for copy in copies:
                    copy.start()
            total = None
            leaving = []
            for index, copies in enumerate(arriving):
                for copy in copies:
                    copy.wait()
                values = [buffer[span(index), :] for buffer in in_buffers]
                results, added = compute(flag_ref[0], values, table_ref)
                for place, (ref, buffer) in enumerate(zip(out_refs, out_buffers)):
                    buffer[span(index), :] = results[place].astype(buffer.dtype)
                    copy = pltpu.make_async_copy(
                        buffer.at[span(index)], ref.at[span(index)], out_marks.at[place, index]
                    )
                    copy.start()
                    leaving.append(copy)
                if sums:
                    total = added if total is None else [a + b for a, b in zip(total, added)]
            if sums:
                values = self.leave(flag_ref[0], jnp.concatenate(total, axis=0))
                sums_ref[...] = values
            for copy in leaving:
                copy.wait()

        results = self.order.call(
            kernel,
            (1,),
            [pl.BlockSpec(memory_space=pltpu.SMEM)]
            + [
                pl.BlockSpec(memory_space=pl.ANY if place in free else pltpu.HBM)
                for place in range(count)
            ]
            + [whole(self.table.shape)],
            [pl.BlockSpec(memory_space=pltpu.HBM)] * len(outs)
            + [whole((sums, width))] * (1 if sums else 0),
            [pltpu.HBM((rows, width), kind) for kind in outs]
            + [jax.ShapeDtypeStruct((sums, width), F32)] * (1 if sums else 0),
            [pltpu.VMEM(operand.shape, operand.dtype) for operand in operands]
            + [pltpu.VMEM((rows, width), kind) for kind in outs]
            + [
                pltpu.SemaphoreType.DMA((count, blocks)),
                pltpu.SemaphoreType.DMA((len(outs), blocks)),
            ],
            20 * rows * width,
            sum(operand.size * operand.dtype.itemsize for operand in operands),
            name,
        )(
            self.y,
            *[
                operand
                if place in free
                else pltpu.with_memory_space_constraint(operand, pltpu.HBM)
                for place, operand in enumerate(operands)
            ],
            self.table,
        )
        return results

    def forward(self, index, base, parts=(), bias=None, low=True, full=False):
        def compute(flag, values, table_ref):
            hidden = values[0].astype(F32)
            if parts:
                hidden = hidden + self.sum_parts(values[1:]) + table_ref[bias : bias + 1, :]
            else:
                hidden = self.enter(flag, hidden)
            center = hidden - jnp.mean(hidden, axis=-1, keepdims=True)
            spread = jnp.mean(center * center, axis=-1, keepdims=True)
            normed = center * lax.rsqrt(spread + NORM_EPS) * table_ref[index : index + 1, :]
            normed = normed + table_ref[7 + index : 8 + index, :]
            results = [hidden]
            if low:
                results.append(normed)
            if full:
                results.append(self.leave(flag, normed))
            return results, None

        outs = [F32] + [BF16] * low + [F32] * full
        free = range(1, 1 + len(parts))
        return self.call(compute, (base, *parts), free, outs, 0, "norm_forward")

    def backward(self, index, hidden, parts, cotangent=None, flow=None, low=True, last=False):
        extras = [value for value in (cotangent, flow) if value is not None]

        def compute(flag, values, table_ref):
            values, others, passing = values[0], list(values[1:]), None
            if flow is not None:
                passing = others.pop()
            upstream = self.enter(flag, others.pop()) if cotangent is not None else None
            if parts:
                summed = self.sum_parts(others)
                upstream = summed if upstream is None else upstream + summed
            center = values - jnp.mean(values, axis=-1, keepdims=True)
            spread = jnp.mean(center * center, axis=-1, keepdims=True)
            scale = lax.rsqrt(spread + NORM_EPS)
            unit = center * scale
            pulled = upstream * table_ref[index : index + 1, :]
            level = jnp.mean(pulled, axis=-1, keepdims=True)
            tilt = jnp.mean(pulled * unit, axis=-1, keepdims=True)
            grad = scale * (pulled - level - unit * tilt)
            if flow is not None:
                grad = grad + passing
            added = [
                jnp.sum(value, axis=0, keepdims=True) for value in (upstream * unit, upstream, grad)
            ]
            results = [self.leave(flag, grad) if last else grad]
            if low:
                results.append(grad)
            return results, added

        grad, *rest, sums = self.call(
            compute,
            (hidden, *parts, *extras),
            range(1, 1 + len(parts)),
            [F32] + [BF16] * low,
            3,
            "norm_backward",
        )
        return grad, sums, *rest


def squares_kernel(copies, *refs):
    *value_refs, out_ref = refs
    total = jnp.zeros((1, 1), F32)
    for index, value_ref in enumerate(value_refs):
        values = value_ref[...].astype(F32)
        square = jnp.sum(values * values, keepdims=True).reshape(1, 1)
        if copies and index == len(value_refs) - 1:
            square = square * (1.0 / copies)
        total = total + square
    out_ref[...] = total


def sum_of_squares(order, arrays, small=None, copies=0):
    operands = (*arrays, small) if copies else arrays
    return order.call(
        partial(squares_kernel, copies),
        (1,),
        [Load(operand.shape) for operand in operands],
        whole((1, 1)),
        jax.ShapeDtypeStruct((1, 1), F32),
        [],
        2 * sum(operand.size for operand in operands),
        sum(operand.size * operand.dtype.itemsize for operand in operands),
        "squares",
    )(*operands)


def clip_factor(square_sum):
    return jnp.minimum(1.0, CLIP_NORM / (jnp.sqrt(square_sum) + 1e-06))


def adam(gradient, weight, first_old, second_old, factor, step_rate, decay_rate):
    clipped = gradient * factor
    moment = BETA_FIRST * first_old + (1.0 - BETA_FIRST) * clipped
    second_new = BETA_SECOND * second_old + (1.0 - BETA_SECOND) * clipped * clipped
    fixed_first = moment / (1.0 - BETA_FIRST**STEP)
    fixed_second = second_new / (1.0 - BETA_SECOND**STEP)
    updated = weight - step_rate * (
        fixed_first / (jnp.sqrt(fixed_second) + ADAM_EPS) + decay_rate * weight
    )
    return clipped, second_new, updated


def update_kernel(cut, rates, count, *refs):
    square_ref, refs = refs[0], refs[1:]
    grad_refs, refs = refs[:count], refs[count:]
    in_refs, out_refs = refs[: 3 * len(rates)], refs[3 * len(rates) :]
    factor = clip_factor(square_ref[...])
    for index, gradient in enumerate(cut(grad_refs, pl.program_id(0))):
        values = [ref[...] for ref in in_refs[3 * index : 3 * index + 3]]
        shape = values[0].shape
        results = adam(
            gradient.reshape(shape), *values, factor.reshape((1,) * len(shape)), rates[index], MATRIX_DECAY
        )
        for out_ref, result in zip(out_refs[3 * index : 3 * index + 3], results):
            out_ref[...] = result


def small_update_kernel(square_ref, small_ref, *refs):
    in_refs, out_refs, bias_ref = refs[:6], refs[6:12], refs[12]
    factor = clip_factor(square_ref[...])
    small = small_ref[...]
    vector_grad = jnp.concatenate([small[:14], small[19:25], small[14:19]], axis=0)
    count = (small.shape[0] - 25) // 2
    unit_rows = [
        jnp.concatenate(
            [small[25 + slot * count + index][None] for index in range(count)], axis=1
        )
        for slot in range(2)
    ]
    for index, gradient in enumerate((vector_grad, jnp.concatenate(unit_rows, axis=0))):
        values = [ref[...] for ref in in_refs[3 * index : 3 * index + 3]]
        results = adam(gradient, *values, factor, VECTOR_RATE, 0.0)
        for out_ref, result in zip(out_refs[3 * index : 3 * index + 3], results):
            out_ref[...] = result
    bias_ref[...] = out_refs[0][23:25, :]


def small_update(order, square_sum, small, vector_arrays, unit_arrays):
    arrays = (*vector_arrays, *unit_arrays)
    outs = [jax.ShapeDtypeStruct(array.shape, F32) for array in arrays]
    outs.append(jax.ShapeDtypeStruct((2, arrays[0].shape[1]), F32))
    return order.call(
        small_update_kernel,
        (1,),
        [whole((1, 1)), whole(small.shape)] + [whole(array.shape) for array in arrays],
        [whole(out.shape) for out in outs],
        outs,
        [],
        0,
        0,
        "update_small",
    )(square_sum, small, *arrays)


def choose(refs, step):
    value = refs[0][...]
    for index in range(1, len(refs)):
        value = jnp.where(step == index, refs[index][...], value)
    return value.astype(F32)


def update(order, square_sum, gradients, groups, rates, cut, name):
    arrays = [array for group in groups for array in group]

    def spec(shape):
        return pl.BlockSpec((1,) + shape[1:], lambda step: (step,) + (0,) * (len(shape) - 1))

    outs = [jax.ShapeDtypeStruct(array.shape, F32) for array in arrays]
    return order.call(
        partial(update_kernel, cut, rates, len(gradients)),
        (arrays[0].shape[0],),
        [whole((1, 1))]
        + [whole(gradient.shape) for gradient in gradients]
        + [spec(array.shape) for array in arrays],
        [spec(out.shape) for out in outs],
        outs,
        [],
        20 * sum(array.size for array in arrays) // 3,
        8 * sum(array.size for array in arrays),
        name,
    )(square_sum, *gradients, *arrays)


def body(
    source_tokens,
    target_tokens,
    source_lengths,
    target_lengths,
    bucket_kinds,
    source_cotangent,
    target_cotangent,
    attention_in,
    attention_out,
    hidden_in,
    hidden_out,
    vectors,
    hidden_bias,
    first_attention_in,
    first_attention_out,
    first_hidden_in,
    first_hidden_out,
    first_vectors,
    first_hidden_bias,
    second_attention_in,
    second_attention_out,
    second_hidden_in,
    second_hidden_out,
    second_vectors,
    second_hidden_bias,
):
    order = Order()
    moves = TensorMoves(order)
    split = CrossRows(order) if lax.axis_size("dp") == 8 else PlainRows(order)
    assert bucket_kinds.shape[0] == 1
    shard_rows = attention_in.shape[2]
    head_width = attention_in.shape[3]
    unit_width = hidden_in.shape[2]
    shard_units = hidden_bias.shape[1]

    small_shard = jnp.concatenate([vectors, hidden_bias.reshape(-1, shard_rows)], axis=0)
    small = split.stack(small_shard.astype(BF16)).astype(F32)

    attn_full = [None] * 3
    up_full = [None] * 2
    down_full = [None] * 2
    attn_zero = split.start(attention_shard(order, attention_in, attention_out, 0))
    attn_one = split.start(attention_shard(order, attention_in, attention_out, 1))
    up_shard, down_shard = feed_shard(order, hidden_in, hidden_out, 0)
    up_zero, down_zero = split.start(up_shard), split.start(down_shard)
    attn_two = split.start(attention_shard(order, attention_in, attention_out, 2))
    up_shard, down_shard = feed_shard(order, hidden_in, hidden_out, 1)
    up_one, down_one = split.start(up_shard), split.start(down_shard)

    norms = Norms(order, small[:, :25].transpose(1, 0, 2).reshape(25, -1), split.y)
    count = head_width // shard_rows
    own_blocks = split.blocks(small, moves.me * count, count)
    head_bias = jnp.concatenate([block[14:20] for block in own_blocks], axis=1)
    unit_bias = jnp.concatenate(
        [block[25:].reshape(2, shard_units) for block in own_blocks], axis=1
    )

    block_rows = source_tokens.shape[0]
    places = jnp.concatenate(
        [
            (moves.me ^ index) * block_rows + jnp.arange(block_rows, dtype=jnp.int32)
            for index in range(moves.count)
        ]
    )
    source_items, source_live = item_codes(bucket_kinds[0], source_lengths[0], places)
    target_items, target_live = item_codes(bucket_kinds[0], target_lengths[0], places)

    def layout_of(key_codes, query_codes):
        rows = jnp.stack([key_codes, places, query_codes])
        return jnp.pad(rows, ((0, 5), (0, 0))).astype(F32)

    encoder_layout = layout_of(source_live, source_items)
    self_layout = layout_of(target_live, target_items)
    cross_layout = layout_of(source_live, target_items)

    source, low = norms.forward(0, source_tokens)
    source_norm_one = moves.gather(low)
    target, low = norms.forward(3, target_tokens)
    target_norm_one = moves.gather(low)

    attn_full[0] = split.finish(attn_zero)
    attention = attention_forward(
        order,
        moves,
        attn_full[0],
        source_norm_one,
        source_norm_one,
        head_bias[:2],
        encoder_layout,
        False,
        (target_norm_one[2],),
    )
    next(attention)
    order.before_next(attn_one)
    attn_full[1] = split.finish(attn_one)
    branch, source_attn_state = next(attention)
    up_zero = order.after_last(up_zero)
    order.before_next(up_zero)
    up_full[0] = split.finish(up_zero)
    source_mid, low = norms.forward(1, source, branch, 20)
    source_norm_two = moves.gather(low)

    attention = attention_forward(
        order,
        moves,
        attn_full[1],
        target_norm_one,
        target_norm_one,
        head_bias[2:4],
        self_layout,
        True,
        (source_norm_two[2], up_full[0][1]),
    )
    next(attention)
    branch, self_state = next(attention)
    order.before_next(down_zero)
    down_full[0] = split.finish(down_zero)
    target_mid, low = norms.forward(4, target, branch, 21)
    target_norm_two = moves.gather(low)

    def feed_pair(slot_id, normed, first=(), between=None):
        weights = up_full[slot_id], down_full[slot_id]
        bias = unit_bias[slot_id : slot_id + 1]
        far = feed_forward(order, *weights, normed[2:], bias, False)
        arrived = moves.cross(*far[2:], first)
        if between is not None:
            order.before_next(between)
        near = feed_forward(order, *weights, normed[:2], bias, True)
        return moves.parts(near[2:], arrived), (near[:2], far[:2])

    branch, source_ffn_state = feed_pair(0, source_norm_two, (target_norm_two[2],), attn_two)
    attn_full[2] = split.finish(attn_two)
    source_last, low, encoder_output = norms.forward(2, source_mid, branch, 23, full=True)
    memory = moves.gather(low)
    order.before_next(up_one)
    up_full[1] = split.finish(up_one)

    attention = attention_forward(
        order,
        moves,
        attn_full[2],
        target_norm_two,
        memory,
        head_bias[4:],
        cross_layout,
        False,
        (up_full[1][1],),
    )
    next(attention)
    order.before_next(down_one)
    branch, cross_state = next(attention)
    down_full[1] = split.finish(down_one)
    target_cross, low = norms.forward(5, target_mid, branch, 22)
    low = lax.optimization_barrier((low, down_full[1][1]))[0]
    target_norm_three = moves.gather(low)
    branch, target_ffn_state = feed_pair(1, target_norm_three)
    target_last, decoder_output = norms.forward(6, target_cross, branch, 24, low=False, full=True)

    def feed_back_pair(slot_id, rows, states, first=()):
        weights = up_full[slot_id], down_full[slot_id]
        near = feed_backward(order, *weights, rows[:2], states[0][1], True)
        if len(rows) < 4:
            rows = moves.gather_late(rows)
        far = feed_backward(order, *weights, rows[2:], states[1][1], False)
        parts = moves.parts(near[2:], moves.cross(*far[2:], first))
        return rows, parts, (near[0], far[0]), near[1] + far[1]

    def feed_weight_pair(upstream_rows, states, normed, pre_grads):
        up_send, up_keep = feed_weights(order, normed, pre_grads)
        up_arrived = split.send(up_send)
        activated = (states[0][0], states[1][0])
        down_send, down_keep = feed_weights(order, upstream_rows, activated)
        return (up_keep, up_arrived), (down_keep, split.send(down_send))

    target_flow, sums_six, low = norms.backward(6, target_last, (), target_cotangent)
    upstream_rows, parts, pre_grads, unit_sums_one = feed_back_pair(
        1, moves.gather_near(low), target_ffn_state
    )
    up_parts, down_parts = feed_weight_pair(
        upstream_rows, target_ffn_state, target_norm_three, pre_grads
    )
    target_flow, sums_five, low = norms.backward(5, target_cross, parts, None, target_flow)
    upstream_rows = moves.gather(low)

    up_grad_one = split.settle(*up_parts)
    grads, cross_sums = attention_backward(
        order, attn_full[2], upstream_rows, cross_state, cross_layout, False
    )
    memory_arrived = moves.cross(
        *spread_rows(order, grads, attn_full[2], head_width, 3 * head_width, 2), (down_parts[1],)
    )
    arrived = moves.cross(*spread_rows(order, grads, attn_full[2], 0, head_width, 2))
    near = spread_rows(order, grads, attn_full[2], head_width, 3 * head_width, 0)
    memory_parts = moves.parts(near, memory_arrived)
    near = spread_rows(order, grads, attn_full[2], 0, head_width, 0)
    parts = moves.parts(near, arrived)
    send, keep_two = attention_weights(
        order, target_norm_two, memory, upstream_rows, grads, cross_state[1]
    )
    arrived_two = split.send(send)
    down_grad_one = split.settle(*down_parts)
    source_flow, sums_two, low = norms.backward(2, source_last, memory_parts, source_cotangent)
    source_rows = moves.gather_near(lax.optimization_barrier((low, arrived))[0])
    target_flow, sums_four, low = norms.backward(4, target_mid, parts, None, target_flow)
    self_upstream = moves.gather(low)
    source_rows = moves.gather_late(source_rows)
    upstream_rows, parts, pre_grads, unit_sums_zero = feed_back_pair(
        0, source_rows, source_ffn_state, (arrived_two,)
    )
    attn_grad_two = split.settle(keep_two, arrived_two)
    up_parts, down_parts = feed_weight_pair(
        upstream_rows, source_ffn_state, source_norm_two, pre_grads
    )
    source_flow, sums_one, low = norms.backward(1, source_mid, parts, None, source_flow)
    upstream_rows = moves.gather(low)

    self_grads, self_sums = attention_backward(
        order, attn_full[1], self_upstream, self_state, self_layout, True
    )
    up_grad_zero = split.settle(*up_parts)
    self_arrived = moves.cross(
        *spread_rows(order, self_grads, attn_full[1], 0, 3 * head_width, 2), (upstream_rows[2],)
    )
    send, keep_one = attention_weights(
        order, target_norm_one, target_norm_one, self_upstream, self_grads, self_state[1]
    )
    arrived_one = split.send(send)
    near = spread_rows(order, self_grads, attn_full[1], 0, 3 * head_width, 0)
    self_parts = moves.parts(near, self_arrived)
    grads, source_sums = attention_backward(
        order, attn_full[0], upstream_rows, source_attn_state, encoder_layout, False
    )
    down_grad_zero = split.settle(*down_parts)
    send, keep_zero = attention_weights(
        order, source_norm_one, source_norm_one, upstream_rows, grads, source_attn_state[1]
    )
    arrived_zero = split.send(send)
    arrived = moves.cross(
        *spread_rows(order, grads, attn_full[0], 0, 3 * head_width, 2), (arrived_one, self_arrived)
    )
    attn_grad_one = split.settle(keep_one, arrived_one)
    near = spread_rows(order, grads, attn_full[0], 0, 3 * head_width, 0)
    parts = moves.parts(near, arrived)
    target_grad, sums_three = norms.backward(
        3, target, self_parts, None, target_flow, low=False, last=True
    )
    source_grad, sums_zero = norms.backward(
        0, source, parts, None, source_flow, low=False, last=True
    )

    norm_sums = (sums_zero, sums_one, sums_two, sums_three, sums_four, sums_five, sums_six)
    vector_rows = [sums[0:1] for sums in norm_sums] + [sums[1:2] for sums in norm_sums]
    vector_rows += [sums[2:3] for sums in (sums_one, sums_four, sums_five, sums_two, sums_six)]
    attn_grad_zero = split.settle(keep_zero, arrived_zero)
    early_squares = sum_of_squares(
        order,
        (attn_grad_one, attn_grad_two, up_grad_zero, up_grad_one, down_grad_zero, down_grad_one),
    )
    own_rows = [source_sums, self_sums, cross_sums]
    for sums in (unit_sums_zero, unit_sums_one):
        cut = sums.reshape(head_width // shard_rows, -1, shard_rows).transpose(1, 0, 2)
        own_rows.append(cut.reshape(-1, head_width))
    own_rows = jnp.concatenate(own_rows, axis=0)
    columns = jnp.arange(moves.count * head_width, dtype=jnp.int32) // head_width
    own_rows = jnp.where(columns[None, :] == moves.me, jnp.tile(own_rows, (1, moves.count)), 0.0)
    small_sum = split.spread(moves.total(jnp.concatenate(vector_rows + [own_rows], axis=0)))

    attn_grads = (attn_grad_zero, attn_grad_one, attn_grad_two)
    up_grads = (up_grad_zero, up_grad_one)
    down_grads = (down_grad_zero, down_grad_one)
    local_squares = early_squares + sum_of_squares(
        order, (attn_grad_zero,), small_sum, moves.count
    )
    square_sum = split.total(moves.total(local_squares))
    grad_norm = jnp.sqrt(square_sum)[0, 0]
    rate_in, rate_out, rate_down = (
        0.5 * D ** (-0.5),
        0.5 * (D // 8) ** (-0.5),
        0.5 * FF ** (-0.5),
    )

    def attention_cut(refs, step):
        values = choose(refs, step)
        inputs = [
            values[:, which * head_width : (which + 1) * head_width] for which in range(3)
        ]
        return jnp.stack(inputs), values[:, 3 * head_width :].T

    def up_cut(refs, step):
        return (choose(refs, step),)

    def down_cut(refs, step):
        return (choose(refs, step).T,)

    attn_new = update(
        order,
        square_sum,
        attn_grads,
        (
            (attention_in, first_attention_in, second_attention_in),
            (attention_out, first_attention_out, second_attention_out),
        ),
        (rate_in, rate_out),
        attention_cut,
        "update_attention",
    )
    up_new = update(
        order,
        square_sum,
        up_grads,
        ((hidden_in, first_hidden_in, second_hidden_in),),
        (rate_in,),
        up_cut,
        "update_up",
    )
    down_new = update(
        order,
        square_sum,
        down_grads,
        ((hidden_out, first_hidden_out, second_hidden_out),),
        (rate_down,),
        down_cut,
        "update_down",
    )
    *small_new, bias_grad = small_update(
        order,
        square_sum,
        small_sum,
        (vectors, first_vectors, second_vectors),
        (hidden_bias, first_hidden_bias, second_hidden_bias),
    )
    return (
        encoder_output,
        decoder_output,
        source_grad,
        target_grad,
        grad_norm,
        *attn_new,
        *up_new,
        *down_new,
        *small_new,
        bias_grad,
    )


def solution(mesh):
    placed = (
        P(("dp", "tensor"), None),
        P(("dp", "tensor"), None),
        P("dp", None),
        P("dp", None),
        P("dp"),
        P(("dp", "tensor"), None),
        P(("dp", "tensor"), None),
        P(None, None, "dp", "tensor"),
        P(None, "tensor", "dp"),
        P(None, "dp", "tensor"),
        P(None, "tensor", "dp"),
        P(None, "dp"),
        P(None, "dp"),
        P(None, None, "dp", "tensor"),
        P(None, "tensor", "dp"),
        P(None, "dp", "tensor"),
        P(None, "tensor", "dp"),
        P(None, "dp"),
        P(None, "dp"),
        P(None, None, "dp", "tensor"),
        P(None, "tensor", "dp"),
        P(None, "dp", "tensor"),
        P(None, "tensor", "dp"),
        P(None, "dp"),
        P(None, "dp"),
    )
    return jax.shard_map(
        body,
        mesh=mesh,
        in_specs=placed,
        out_specs=(
            P(("dp", "tensor"), None),
            P(("dp", "tensor"), None),
            P(("dp", "tensor"), None),
            P(("dp", "tensor"), None),
            P(),
            P(None, None, "dp", "tensor"),
            P(None, None, "dp", "tensor"),
            P(None, None, "dp", "tensor"),
            P(None, "tensor", "dp"),
            P(None, "tensor", "dp"),
            P(None, "tensor", "dp"),
            P(None, "dp", "tensor"),
            P(None, "dp", "tensor"),
            P(None, "dp", "tensor"),
            P(None, "tensor", "dp"),
            P(None, "tensor", "dp"),
            P(None, "tensor", "dp"),
            P(None, "dp"),
            P(None, "dp"),
            P(None, "dp"),
            P(None, "dp"),
            P(None, "dp"),
            P(None, "dp"),
            P(None, "dp"),
        ),
        check_vma=False,
    )
```

```python
from functools import partial

import jax
import jax.numpy as jnp
from jax import lax
from jax.experimental import pallas as pl
from jax.experimental.pallas import tpu as pltpu
from jax.sharding import PartitionSpec as P

D = 1024
FF = 4096
L = 1024
ITEMS = 8
STEP = 10
HEAD = 64
ITEM = 128


NORM_EPS = 1e-05
CLIP_NORM = 1.0
BETA_FIRST = 0.9
BETA_SECOND = 0.999
ADAM_EPS = 1e-08
MATRIX_DECAY = 0.01
MASKED = -1e30

BF16 = jnp.bfloat16
F32 = jnp.float32
VECTOR_RATE = 0.3
SMALL = 16384
VMEM_BYTES = 24 * 1024 * 1024


class TensorMoves:
    def __init__(self, order):
        self.order = order
        self.count = lax.axis_size("tensor")
        assert self.count == 4
        self.me = lax.axis_index("tensor")

    def swap(self, values, bit):
        pairs = [(index, index ^ bit) for index in range(self.count)]
        return lax.ppermute(values, "tensor", pairs)

    def gather(self, shard):
        return self.gather_far(self.gather_near(shard))

    def gather_near(self, shard):
        return shard, self.swap(shard, 1), self.swap(shard, 2)

    def gather_far(self, rows):
        return *rows, self.swap(rows[2], 1)

    def gather_late(self, rows):
        return *rows, self.swap(self.order.after_last(rows[2]), 1)

    def cross(self, send, keep, first=()):
        send = lax.optimization_barrier((send, first))[0]
        crossing = (keep + self.swap(send, 1).astype(F32)).astype(BF16)
        self.order.before_next(crossing)
        return self.swap(crossing, 2)

    def parts(self, near, arrived):
        first, second, keep = near
        return keep, self.swap(first, 1), self.swap(second, 1), arrived

    @property
    def steps(self):
        return [lambda values, bit=bit: values + self.swap(values, bit) for bit in (1, 2)]

    def total(self, values):
        for step in self.steps:
            values = step(values)
        return values


class PlainRows:
    def __init__(self, order):
        self.order = order
        self.count = lax.axis_size("dp")
        self.me = lax.axis_index("dp")
        self.y = None

    def start(self, shard):
        return lax.all_gather(shard, "dp", axis=0, tiled=True)

    def finish(self, full):
        half = full.shape[0] // 2
        return full[:half], full[half:]

    def blocks(self, stacked, first, count):
        return [
            lax.dynamic_index_in_dim(stacked, first + index, 0, False) for index in range(count)
        ]

    def send(self, far_part):
        return far_part

    def settle(self, near_part, arrived):
        values = jnp.concatenate([near_part, arrived.astype(F32)], 0)
        return lax.psum_scatter(values, "dp", scatter_dimension=0, tiled=True)

    def stack(self, shard):
        return lax.all_gather(shard, "dp", axis=0)

    def spread(self, values):
        return lax.psum_scatter(values, "dp", scatter_dimension=1, tiled=True)

    @property
    def steps(self):
        return [lambda values: lax.psum(values, "dp")]

    def total(self, values):
        for step in self.steps:
            values = step(values)
        return values


class CrossRows(PlainRows):
    ALONG_Z = [[0, 2, 4, 6], [1, 3, 5, 7]]

    def __init__(self, order):
        super().__init__(order)
        self.z = self.me // 2
        self.y = self.me % 2

    def swap(self, values, bits):
        pairs = [(index, index ^ bits) for index in range(self.count)]
        return lax.ppermute(values, "dp", pairs)

    def start(self, shard):
        return lax.all_gather(shard, "dp", axis=0, tiled=True, axis_index_groups=self.ALONG_Z)

    def finish(self, near):
        return near, self.swap(near, 1)

    def blocks(self, stacked, first, count):
        assert count == 2
        near = lax.dynamic_index_in_dim(stacked, first // 2, 0, False)
        far = lax.dynamic_index_in_dim(stacked, first // 2 + 4, 0, False)
        even = self.y == 0
        return [jnp.where(even, near, far), jnp.where(even, far, near)]

    def send(self, far_part):
        return self.swap(far_part, 1)

    def settle(self, near_part, arrived):
        near_part, arrived = self.order.after_last((near_part, arrived))
        part = (near_part + arrived.astype(F32)).astype(BF16)
        self.order.before_next(part)
        return lax.psum_scatter(
            part, "dp", scatter_dimension=0, tiled=True, axis_index_groups=self.ALONG_Z
        )

    def stack(self, shard):
        pieces = jnp.stack([shard] + [self.swap(shard, bits) for bits in (2, 4, 6)])
        near = jnp.stack(
            [lax.dynamic_index_in_dim(pieces, self.z ^ index, 0, False) for index in range(4)]
        )
        return jnp.concatenate([near, self.swap(near, 1)], axis=0)

    def spread(self, values):
        rows = values.shape[0]
        blocks = values.reshape(rows, 4, 2, -1)
        first, second = [blocks[:, :, index].reshape(rows, -1) for index in range(2)]
        even = self.y == 0
        part = jnp.where(even, first, second) + self.swap(jnp.where(even, second, first), 1)
        size = part.shape[1] // 4
        total = lax.dynamic_slice_in_dim(part, self.z * size, size, 1)
        for bits in (2, 4, 6):
            sent = lax.dynamic_slice_in_dim(part, (self.z ^ (bits // 2)) * size, size, 1)
            total = total + self.swap(sent, bits)
        return total

    @property
    def steps(self):
        return [lambda values, bits=bits: values + self.swap(values, bits) for bits in (1, 2, 4)]


def item_codes(row_kind, lengths, places):
    items = jnp.where(row_kind == 1, 0, places // ITEM)
    within = jnp.where(row_kind == 1, places, places % ITEM)
    limit = jnp.zeros_like(places)
    for index in range(ITEMS):
        limit = jnp.where(items == index, lengths[index], limit)
    return items, jnp.where(within < limit, items, -1)


def dot_nn(left, right):
    return jnp.dot(left, right, preferred_element_type=F32)


def dot_nt(left, right):
    return lax.dot_general(left, right, (((1,), (1,)), ((), ())), preferred_element_type=F32)


def dot_tn(left, right):
    return lax.dot_general(left, right, (((0,), (0,)), ((), ())), preferred_element_type=F32)


def wide_dot(rows, near, far):
    half = near.shape[0]
    return dot_nn(rows[:, :half], near[...]) + dot_nn(rows[:, half:], far[...])


class Load:
    def __init__(self, shape, start=None):
        self.shape = shape
        self.start = start or (0,) * len(shape)


class Loaded:
    def __init__(self, copy, buffer, step):
        self.copy = copy
        self.buffer = buffer
        self.step = step
        self.waited = False

    @property
    def shape(self):
        return self.buffer.shape

    def ready(self):
        if not self.waited:
            self.waited = True
            pl.when(self.step == 0)(self.copy.wait)

    def wait_here(self):
        self.waited = True
        self.copy.wait()

    def __getitem__(self, where):
        self.ready()
        return self.buffer[where]


class Order:
    def __init__(self):
        self.marks = ()

    def call(self, kernel, grid, in_specs, out_specs, out_shapes, scratch, flops, moved, name):
        marks = [
            pltpu.with_memory_space_constraint(mark, pltpu.HBM) if mark.size > SMALL else mark
            for mark in self.marks
        ]
        loads = [(place, spec) for place, spec in enumerate(in_specs) if isinstance(spec, Load)]
        hbm = pl.BlockSpec(memory_space=pltpu.HBM)

        def marked(*refs):
            refs = list(refs[len(marks) :])
            step = pl.program_id(0)
            loaded = []
            if loads:
                *refs, semaphores = refs
                buffers = refs[-len(loads) :]
                refs = refs[: -len(loads)]
                for index, (place, spec) in enumerate(loads):
                    source = refs[place].at[
                        tuple(pl.ds(first, size) for first, size in zip(spec.start, spec.shape))
                    ]
                    copy = pltpu.make_async_copy(source, buffers[index], semaphores.at[index])
                    loaded.append(Loaded(copy, buffers[index], step))
                    refs[place] = loaded[-1]

                @pl.when(step == 0)
                def _():
                    for item in loaded:
                        item.copy.start()

            kernel(*refs)
            for item in loaded:
                item.ready()

        def run(*operands):
            operands = list(operands)
            buffers = []
            for place, spec in loads:
                buffers.append(pltpu.VMEM(spec.shape, operands[place].dtype))
                operands[place] = pltpu.with_memory_space_constraint(operands[place], pltpu.HBM)
            if loads:
                buffers.append(pltpu.SemaphoreType.DMA((len(loads),)))
            results = pl.pallas_call(
                marked,
                grid=grid,
                in_specs=[
                    hbm if mark.size > SMALL else pl.BlockSpec(memory_space=pl.ANY)
                    for mark in marks
                ]
                + [hbm if isinstance(spec, Load) else spec for spec in in_specs],
                out_specs=out_specs,
                out_shape=out_shapes,
                scratch_shapes=list(scratch) + buffers,
                compiler_params=pltpu.CompilerParams(
                    vmem_limit_bytes=VMEM_BYTES,
                    dimension_semantics=("arbitrary",) * len(grid),
                ),
                cost_estimate=pl.CostEstimate(
                    flops=flops, bytes_accessed=moved, transcendentals=0
                ),
                name=name,
            )(*marks, *operands)
            self.marks = (min(jax.tree.leaves(results), key=lambda leaf: leaf.size),)
            return results

        return run

    def before_next(self, value):
        self.marks += (value,)

    def after_last(self, value):
        return lax.optimization_barrier((value, self.marks))[0]


def whole(shape):
    return pl.BlockSpec(
        shape, lambda step: (0,) * len(shape), pipeline_mode=pl.Buffered(buffer_count=1)
    )


def pair_bias(layout_ref, start, rows, causal):
    turned = layout_ref[...].T
    queries = pl.ds(start, rows)
    allowed = turned[:, 0:1] == layout_ref[2:3, queries]
    if causal:
        allowed = allowed & (turned[:, 1:2] <= layout_ref[1:2, queries])
    return jnp.where(allowed, 0.0, MASKED).astype(F32)


def head_rows_only(block, head, scale=None):
    lanes = lax.broadcasted_iota(jnp.int32, block.shape, 1) // HEAD
    if scale is not None:
        block = block * jnp.asarray(scale, block.dtype)
    return jnp.where(lanes == head, block, jnp.zeros_like(block))


def over_keys(combine, values):
    parts = values.reshape(8, values.shape[0] // 8, values.shape[1])
    return combine(combine(parts, axis=0), axis=0, keepdims=True)


def attend_block(queries, key_rows, values_turned, bias, heads):
    scores = []
    for head in range(heads):
        picked = head_rows_only(queries, head, HEAD ** (-0.5))
        scores.append(dot_nt(key_rows, picked) + bias)
    largest = [over_keys(jnp.max, score) for score in scores]
    contexts = []
    totals = []
    for head in range(heads):
        weights = jnp.exp(scores[head] - largest[head])
        total = over_keys(jnp.sum, weights)
        context = dot_nn(
            values_turned[head * HEAD : (head + 1) * HEAD, :], weights.astype(BF16)
        )
        contexts.append(context * (1.0 / total))
        totals.append(largest[head] + jnp.log(total))
    return jnp.concatenate(contexts, axis=0).T, jnp.concatenate(totals, axis=0)


def out_parts(rows, out_near, out_far, step, send_refs, keep_ref):
    half = out_near.shape[0]
    near = dot_nt(rows, out_near)
    far = dot_nt(rows, out_far)

    @pl.when(step == 0)
    def _():
        if len(send_refs) == 1:
            send_refs[0][:, :half] = near.astype(BF16)
            send_refs[0][:, half:] = far.astype(BF16)
        else:
            send_refs[0][...] = near.astype(BF16)
            send_refs[1][...] = far.astype(BF16)

    @pl.when(step == 1)
    def _():
        keep_ref[:, :half] = near
        keep_ref[:, half:] = far


def part_shapes(rows, half, halves):
    sends = [(rows, half)] * 2 if halves else [(rows, 2 * half)]
    return sends + [(rows, 2 * half)], [BF16] * len(sends) + [F32]


def part_outs(rows, half, halves):
    shapes, kinds = part_shapes(rows, half, halves)
    return [jax.ShapeDtypeStruct(shape, kind) for shape, kind in zip(shapes, kinds)]


def part_specs(rows, half, halves):
    return [whole(shape) for shape in part_shapes(rows, half, halves)[0]]


def attend_tail(
    step, qkv_ref, turned_ref, layout_ref, causal, out_near, out_far, first_row, outs, heads
):
    context_ref, total_ref, *send_refs, keep_ref = outs
    rows = keep_ref.shape[0]
    wide = context_ref.shape[1]
    start = pl.multiple_of(first_row + (1 - step) * rows, rows)
    bias = pair_bias(layout_ref, start, rows, causal)
    context, totals = attend_block(
        qkv_ref[pl.ds(start, rows), :wide],
        qkv_ref[:, wide : 2 * wide],
        turned_ref[...],
        bias,
        heads,
    )
    context = context.astype(BF16)
    context_ref[...] = context
    total_ref[...] = totals
    out_parts(context, out_near, out_far, step, send_refs, keep_ref)


def attend_far_kernel(causal, is_cross, heads, *refs):
    normed_refs = memory_refs = refs[:4]
    refs = refs[4:]
    if is_cross:
        memory_refs, refs = refs[:4], refs[4:]
    full_near_ref, full_far_ref, bias_ref = refs[:3]
    layout_ref = refs[3]
    qkv_ref, context_ref, *outs, turned_ref = refs[4:]
    step = pl.program_id(0)
    rows = outs[-1].shape[0]
    wide = context_ref.shape[1]

    @pl.when(step == 0)
    def _():
        def project(source_refs, begin, end, biases):
            for index in range(4):
                part = source_refs[index][...]
                values = wide_dot(part, full_near_ref[:, begin:end], full_far_ref[:, begin:end])
                span = slice(index * rows, (index + 1) * rows)
                for place, which in enumerate(range(begin // wide, end // wide)):
                    piece = values[:, place * wide : (place + 1) * wide]
                    if biases[which] is not None:
                        piece = piece + bias_ref[biases[which] : biases[which] + 1, :]
                    qkv_ref[span, which * wide : (which + 1) * wide] = piece.astype(BF16)

        biases = (0, None, 1)
        if is_cross:
            project(normed_refs, 0, wide, biases)
            project(memory_refs, wide, 3 * wide, biases)
        else:
            project(normed_refs, 0, 3 * wide, biases)
        turned_ref[...] = qkv_ref[:, 2 * wide :].T

    attend_tail(
        step,
        qkv_ref,
        turned_ref,
        layout_ref,
        causal,
        full_near_ref[:, 3 * wide :],
        full_far_ref[:, 3 * wide :],
        2 * rows,
        (context_ref, *outs),
        heads,
    )


def attend_near_kernel(causal, heads, *refs):
    qkv_ref, out_near_ref, out_far_ref = refs[:3]
    layout_ref = refs[3]
    context_ref, *outs, turned_ref = refs[4:]
    step = pl.program_id(0)
    wide = context_ref.shape[1]

    @pl.when(step == 0)
    def _():
        turned_ref[...] = qkv_ref[:, 2 * wide :].T

    attend_tail(
        step,
        qkv_ref,
        turned_ref,
        layout_ref,
        causal,
        out_near_ref[...],
        out_far_ref[...],
        0,
        (context_ref, *outs),
        heads,
    )


def attention_forward(order, moves, full, normed, memory, biases, layout, causal, first):
    length = layout.shape[1]
    rows = length // 4
    width = full[0].shape[1]
    wide = width // 4
    heads = wide // HEAD
    half = full[0].shape[0]
    is_cross = memory is not normed
    sources = tuple(normed) + (tuple(memory) if is_cross else ())
    pairs = 4 * rows * length // 2 * wide * heads

    half_outs = [
        jax.ShapeDtypeStruct((2 * rows, wide), BF16),
        jax.ShapeDtypeStruct((heads, 2 * rows), F32),
    ]
    half_specs = [
        pl.BlockSpec((rows, wide), lambda step: (1 - step, 0)),
        pl.BlockSpec((heads, rows), lambda step: (0, 1 - step)),
    ]
    turned = pltpu.VMEM((wide, length), BF16)
    qkv, context_far, totals_far, send_far, keep_far = order.call(
        partial(attend_far_kernel, causal, is_cross, heads),
        (2,),
        [whole((rows, 2 * half))] * len(sources)
        + [whole((half, width))] * 2
        + [whole(biases.shape), whole(layout.shape)],
        [whole((length, 3 * wide))] + half_specs + part_specs(rows, half, False),
        [jax.ShapeDtypeStruct((length, 3 * wide), BF16)]
        + half_outs
        + part_outs(rows, half, False),
        [turned],
        2 * length * 2 * half * 3 * wide + pairs,
        12 * length * 2 * half,
        "attend_far",
    )(*sources, *full, biases, layout)
    arrived = moves.cross(send_far, keep_far, first)
    yield
    context_near, totals_near, *near = order.call(
        partial(attend_near_kernel, causal, heads),
        (2,),
        [whole((length, 3 * wide))]
        + [pl.BlockSpec((half, wide), lambda step: (0, 3))] * 2
        + [whole(layout.shape)],
        half_specs + part_specs(rows, half, True),
        half_outs + part_outs(rows, half, True),
        [turned],
        pairs,
        6 * length * 2 * half,
        "attend_near",
    )(qkv, *full, layout)
    branch = moves.parts(near, arrived)
    yield branch, (qkv, (context_near, context_far), (totals_near, totals_far))


def attend_back_kernel(causal, heads, *refs):
    qkv_ref, first_ref, out_near_ref, out_far_ref = refs[:4]
    context_refs, total_refs, layout_ref = refs[4:6], refs[6:8], refs[8]
    grad_refs = (first_ref, *refs[9:12])
    grads_ref, sums_ref = refs[12:14]
    keys_turned_ref, key_sum_ref, value_sum_ref, grad_ref, context_ref, total_ref = refs[14:]
    step = pl.program_id(0)
    rows = context_ref.shape[0]
    wide = context_ref.shape[1]
    scale = HEAD ** (-0.5)

    @pl.when(step == 0)
    def _():
        keys_turned_ref[...] = qkv_ref[:, wide : 2 * wide].T
        key_sum_ref[...] = jnp.zeros_like(key_sum_ref)
        value_sum_ref[...] = jnp.zeros_like(value_sum_ref)

    for loaded in (*context_refs, *total_refs):
        loaded.ready()
    for index in range(4):

        @pl.when(step == index)
        def _(index=index):
            span = slice((index % 2) * rows, (index % 2 + 1) * rows)
            grad_refs[index].wait_here()
            grad_ref[...] = grad_refs[index][...]
            context_ref[...] = context_refs[index // 2][span, :]
            total_ref[...] = total_refs[index // 2][:, span]

    context_grad = wide_dot(grad_ref[...], out_near_ref, out_far_ref).astype(BF16)
    products_turned = (context_grad.astype(F32) * context_ref[...].astype(F32)).T
    start = pl.multiple_of(step * rows, rows)
    bias = pair_bias(layout_ref, start, rows, causal)
    queries = qkv_ref[pl.ds(start, rows), :wide]
    key_rows = qkv_ref[:, wide : 2 * wide]
    value_rows = qkv_ref[:, 2 * wide :]
    query_grads = []

    def products(head):
        picked = head_rows_only(queries, head, scale)
        picked_grad = head_rows_only(context_grad, head)
        scores = dot_nt(key_rows, picked) + bias
        return picked, picked_grad, scores, dot_nt(value_rows, picked_grad)

    ahead = products(0)
    for head in range(heads):
        picked, picked_grad, scores, weight_grad = ahead
        if head + 1 < heads:
            ahead = products(head + 1)
        span = slice(head * HEAD, (head + 1) * HEAD)
        weights = jnp.exp(scores - total_ref[head : head + 1, :])
        diagonal = jnp.sum(products_turned[span, :], axis=0, keepdims=True)
        score_grad = (weights * (weight_grad - diagonal)).astype(BF16)
        value_sum_ref[...] += dot_nn(weights.astype(BF16), picked_grad)
        key_sum_ref[...] += dot_nn(score_grad, picked)
        query_grads.append(dot_nn(keys_turned_ref[span, :], score_grad))
    query_grad = jnp.concatenate(query_grads, axis=0).T * scale
    grads_ref[pl.ds(start, rows), :wide] = query_grad.astype(BF16)

    @pl.when(step == 3)
    def _():
        grads_ref[:, wide : 2 * wide] = key_sum_ref[...].astype(BF16)
        grads_ref[:, 2 * wide :] = value_sum_ref[...].astype(BF16)
        for place, begin in ((0, 0), (1, 2 * wide)):
            values = grads_ref[:, begin : begin + wide].astype(F32)
            sums_ref[place : place + 1, :] = jnp.sum(values, axis=0, keepdims=True)


def spread_kernel(begin, end, rows_ref, near_ref, far_ref, *outs):
    step = pl.program_id(0)
    part = rows_ref[:, begin:end]
    out_parts(part, near_ref[:, begin:end], far_ref[:, begin:end], step, outs[:-1], outs[-1])


def spread_rows(order, grads, full, begin, end, first):
    rows = grads.shape[0] // 4
    half = full[0].shape[0]
    wide = grads.shape[1]
    return order.call(
        partial(spread_kernel, begin, end),
        (2,),
        [pl.BlockSpec((rows, wide), lambda step: (first + 1 - step, 0))]
        + [whole((half, wide))] * 2,
        part_specs(rows, half, first == 0),
        part_outs(rows, half, first == 0),
        [],
        4 * rows * 2 * half * (end - begin),
        6 * rows * 2 * half + 4 * half * wide,
        "spread_rows",
    )(grads, *full)


def later_half(step, size):
    return pl.ds(pl.multiple_of((1 - step) * size, size), size)


def rows_dot(left_refs, right, begin, end, columns=slice(None)):
    total = None
    for index, left_ref in enumerate(left_refs):
        rows = left_ref.shape[0]
        if isinstance(right, tuple):
            first = (index % 2) * rows
            part = right[index // 2][first : first + rows, begin:end]
        else:
            part = right[index * rows : (index + 1) * rows, begin:end]
        product = dot_tn(left_ref[:, columns], part)
        total = product if total is None else total + product
    return total


def attention_weight_kernel(is_cross, *refs):
    normed_refs = memory_refs = refs[:4]
    refs = refs[4:]
    if is_cross:
        memory_refs, refs = refs[:4], refs[4:]
    upstream_refs, grads_ref, context_refs, outs = refs[:4], refs[4], refs[5:7], refs[7:]
    send_ref, keep_ref = outs
    step = pl.program_id(0)
    wide = context_refs[0].shape[1]
    columns = later_half(step, send_ref.shape[0])
    if is_cross:
        pieces = [
            rows_dot(normed_refs, grads_ref, 0, wide, columns),
            rows_dot(memory_refs, grads_ref, wide, 3 * wide, columns),
        ]
    else:
        pieces = [rows_dot(normed_refs, grads_ref, 0, 3 * wide, columns)]
    pieces.append(rows_dot(upstream_refs, tuple(context_refs), 0, wide, columns))

    @pl.when(step == 0)
    def _():
        send_ref[...] = jnp.concatenate(pieces, axis=1).astype(BF16)

    @pl.when(step == 1)
    def _():
        keep_ref[...] = jnp.concatenate(pieces, axis=1)


def attention_weights(order, normed, memory, upstream, grads, contexts):
    rows, width = normed[0].shape
    wide = contexts[0].shape[1]
    is_cross = memory is not normed
    sources = tuple(normed) + (tuple(memory) if is_cross else ()) + tuple(upstream)
    half = width // 2
    outs = (half, 4 * wide)
    return order.call(
        partial(attention_weight_kernel, is_cross),
        (2,),
        [Load((rows, width))] * len(sources)
        + [whole(grads.shape)]
        + [Load((2 * rows, wide))] * 2,
        [whole(outs)] * 2,
        [jax.ShapeDtypeStruct(outs, BF16), pltpu.HBM(outs, F32)],
        [],
        8 * rows * width * 4 * wide,
        2 * rows * width * (len(sources) + 4) + 6 * half * 4 * wide,
        "attention_weights",
    )(*sources, grads, *contexts)


def attention_backward(order, full, upstream_rows, stored, layout, causal):
    qkv, contexts, totals = stored
    length = qkv.shape[0]
    rows = length // 4
    wide = qkv.shape[1] // 3
    heads = wide // HEAD
    half = full[0].shape[0]
    return order.call(
        partial(attend_back_kernel, causal, heads),
        (4,),
        [Load(qkv.shape), Load((rows, 2 * half))]
        + [Load((half, wide), (0, 3 * wide))] * 2
        + [Load((2 * rows, wide))] * 2
        + [Load((heads, 2 * rows))] * 2
        + [Load(layout.shape)]
        + [Load((rows, 2 * half))] * 3,
        [whole(qkv.shape), whole((2, wide))],
        [jax.ShapeDtypeStruct(qkv.shape, BF16), jax.ShapeDtypeStruct((2, wide), F32)],
        [
            pltpu.VMEM((wide, length), BF16),
            pltpu.VMEM((length, wide), F32),
            pltpu.VMEM((length, wide), F32),
            pltpu.VMEM((rows, 2 * half), BF16),
            pltpu.VMEM((rows, wide), BF16),
            pltpu.VMEM((heads, rows), F32),
        ],
        10 * length * length * wide * heads,
        12 * length * 2 * half,
        "attend_back",
    )(qkv, upstream_rows[0], *full, *contexts, *totals, layout, *upstream_rows[1:])


GELU_SCALE = 0.7978845608028654
GELU_CUBE = 0.044715


def feed_kernel(own_ref, near_ref, up_near, up_far, down_near, down_far, bias_ref, *outs):
    activated_ref, slope_ref, *send_refs, keep_ref = outs
    step = pl.program_id(0)
    rows = jnp.where(step == 0, near_ref[...], own_ref[...])
    pre_act = wide_dot(rows, up_near[...], up_far[...]) + bias_ref[...]
    square = pre_act * pre_act
    bent = jnp.tanh(GELU_SCALE * pre_act * (1.0 + GELU_CUBE * square))
    activated = (0.5 * pre_act * (1.0 + bent)).astype(BF16)
    inner = GELU_SCALE * (1.0 + 3.0 * GELU_CUBE * square)
    slope = 0.5 * (1.0 + bent) + 0.5 * pre_act * (1.0 - bent * bent) * inner
    activated_ref[...] = activated
    slope_ref[...] = slope.astype(BF16)
    out_parts(activated, down_near[...], down_far[...], step, send_refs, keep_ref)


def feed_forward(order, up_full, down_full, pair_rows, unit_bias, halves):
    rows = pair_rows[0].shape[0]
    half, units = up_full[0].shape
    return order.call(
        feed_kernel,
        (2,),
        [whole((rows, 2 * half))] * 2 + [whole((half, units))] * 4 + [whole((1, units))],
        [pl.BlockSpec((rows, units), lambda step: (1 - step, 0))] * 2
        + part_specs(rows, half, halves),
        [jax.ShapeDtypeStruct((2 * rows, units), BF16)] * 2 + part_outs(rows, half, halves),
        [],
        16 * rows * half * units,
        20 * rows * units + 8 * half * units,
        "feed_forward",
    )(*pair_rows, *up_full, *down_full, unit_bias)


def feed_back_kernel(
    own_ref, near_ref, slope_ref, up_near, up_far, down_near, down_far, *outs
):
    grad_ref, sum_ref, *send_refs, keep_ref = outs
    step = pl.program_id(0)
    rows = jnp.where(step == 0, near_ref[...], own_ref[...])
    act_grad = wide_dot(rows, down_near[...], down_far[...])
    pre_grad = (act_grad * slope_ref[...].astype(F32)).astype(BF16)
    grad_ref[...] = pre_grad

    @pl.when(step == 0)
    def _():
        sum_ref[...] = jnp.zeros_like(sum_ref)

    sum_ref[...] += jnp.sum(pre_grad.astype(F32), axis=0, keepdims=True)
    out_parts(pre_grad, up_near[...], up_far[...], step, send_refs, keep_ref)


def feed_weight_kernel(*refs):
    left_refs, right_refs, (send_ref, keep_ref) = refs[:4], refs[4:6], refs[6:]
    step = pl.program_id(0)
    part = rows_dot(left_refs, tuple(right_refs), 0, send_ref.shape[1])

    @pl.when(step == 0)
    def _():
        send_ref[...] = part.astype(BF16)

    @pl.when(step == 1)
    def _():
        keep_ref[...] = part


def feed_weights(order, left, right):
    rows, width = left[0].shape
    units = right[0].shape[1]
    half = width // 2
    outs = (half, units)
    return order.call(
        feed_weight_kernel,
        (2,),
        [pl.BlockSpec((rows, half), lambda step: (0, 1 - step))] * 4
        + [whole((2 * rows, units))] * 2,
        [whole(outs)] * 2,
        [jax.ShapeDtypeStruct(outs, BF16), pltpu.HBM(outs, F32)],
        [],
        8 * rows * width * units,
        8 * rows * (width + units) + 6 * half * units,
        "feed_weights",
    )(*left, *right)


def feed_backward(order, up_full, down_full, pair_rows, slope, halves):
    rows = pair_rows[0].shape[0]
    half, units = up_full[0].shape
    return order.call(
        feed_back_kernel,
        (2,),
        [whole((rows, 2 * half))] * 2
        + [pl.BlockSpec((rows, units), lambda step: (1 - step, 0))]
        + [whole((half, units))] * 4,
        [pl.BlockSpec((rows, units), lambda step: (1 - step, 0)), whole((1, units))]
        + part_specs(rows, half, halves),
        [
            jax.ShapeDtypeStruct((2 * rows, units), BF16),
            jax.ShapeDtypeStruct((1, units), F32),
        ]
        + part_outs(rows, half, halves),
        [],
        16 * rows * half * units,
        20 * rows * units + 8 * half * units,
        "feed_backward",
    )(*pair_rows, slope, *up_full, *down_full)


def attention_shard_kernel(in_ref, out_ref, shard_ref):
    wide = in_ref.shape[3]
    for which in range(3):
        shard_ref[:, which * wide : (which + 1) * wide] = in_ref[0, which].astype(BF16)
    shard_ref[:, 3 * wide :] = out_ref[0].T.astype(BF16)


def attention_shard(order, attention_in, attention_out, slot_id):
    rows, wide = attention_in.shape[2:]
    return order.call(
        attention_shard_kernel,
        (1,),
        [
            pl.BlockSpec((1, 3, rows, wide), lambda step: (slot_id, 0, 0, 0)),
            pl.BlockSpec((1, wide, rows), lambda step: (slot_id, 0, 0)),
        ],
        whole((rows, 4 * wide)),
        jax.ShapeDtypeStruct((rows, 4 * wide), BF16),
        [],
        0,
        24 * rows * wide,
        "attention_shard",
    )(attention_in, attention_out)


def feed_shard_kernel(up_ref, down_ref, up_shard_ref, down_shard_ref):
    up_shard_ref[...] = up_ref[0].astype(BF16)
    down_shard_ref[...] = down_ref[0].T.astype(BF16)


def feed_shard(order, hidden_in, hidden_out, slot_id):
    rows, units = hidden_in.shape[1:]
    return order.call(
        feed_shard_kernel,
        (1,),
        [
            pl.BlockSpec((1, rows, units), lambda step: (slot_id, 0, 0)),
            pl.BlockSpec((1, units, rows), lambda step: (slot_id, 0, 0)),
        ],
        [whole((rows, units))] * 2,
        [jax.ShapeDtypeStruct((rows, units), BF16)] * 2,
        [],
        0,
        12 * rows * units,
        "feed_shard",
    )(hidden_in, hidden_out)


class Norms:
    def __init__(self, order, table, y):
        self.order = order
        self.table = table
        self.y = jnp.zeros((1,), jnp.int32) if y is None else y.astype(jnp.int32).reshape(1)
        self.ordered = y is None

    def enter(self, flag, values):
        if self.ordered:
            return values
        size = values.shape[1] // 8
        blocks = [values[:, index * size : (index + 1) * size] for index in range(8)]
        first = jnp.concatenate(blocks[0::2], axis=1)
        second = jnp.concatenate(blocks[1::2], axis=1)
        return jnp.concatenate(
            [jnp.where(flag == 0, first, second), jnp.where(flag == 0, second, first)], axis=1
        )

    def leave(self, flag, values):
        if self.ordered:
            return values
        half = values.shape[1] // 2
        near, far = values[:, :half], values[:, half:]
        first = jnp.where(flag == 0, near, far)
        second = jnp.where(flag == 0, far, near)
        size = half // 4
        blocks = []
        for index in range(4):
            span = slice(index * size, (index + 1) * size)
            blocks += [first[:, span], second[:, span]]
        return jnp.concatenate(blocks, axis=1)

    def sum_parts(self, parts):
        keep, first, second, arrived = [part.astype(F32) for part in parts]
        return keep + jnp.concatenate([first, second], axis=1) + arrived

    def call(self, compute, operands, free, outs, sums, name):
        rows, width = operands[0].shape
        blocks = 2
        block = rows // blocks
        count = len(operands)

        def kernel(flag_ref, *refs):
            in_refs, refs = refs[:count], refs[count:]
            table_ref, refs = refs[0], refs[1:]
            out_refs, refs = refs[: len(outs)], refs[len(outs) :]
            if sums:
                sums_ref, refs = refs[0], refs[1:]
            in_buffers, refs = refs[:count], refs[count:]
            out_buffers, (in_marks, out_marks) = refs[: len(outs)], refs[len(outs) :]

            def span(index):
                return pl.ds(index * block, block)

            arriving = [
                [
                    pltpu.make_async_copy(
                        ref.at[span(index)], buffer.at[span(index)], in_marks.at[place, index]
                    )
                    for place, (ref, buffer) in enumerate(zip(in_refs, in_buffers))
                ]
                for index in range(blocks)
            ]
            for copies in arriving:
                for copy in copies:
                    copy.start()
            total = None
            leaving = []
            for index, copies in enumerate(arriving):
                for copy in copies:
                    copy.wait()
                values = [buffer[span(index), :] for buffer in in_buffers]
                results, added = compute(flag_ref[0], values, table_ref)
                for place, (ref, buffer) in enumerate(zip(out_refs, out_buffers)):
                    buffer[span(index), :] = results[place].astype(buffer.dtype)
                    copy = pltpu.make_async_copy(
                        buffer.at[span(index)], ref.at[span(index)], out_marks.at[place, index]
                    )
                    copy.start()
                    leaving.append(copy)
                if sums:
                    total = added if total is None else [a + b for a, b in zip(total, added)]
            if sums:
                values = self.leave(flag_ref[0], jnp.concatenate(total, axis=0))
                sums_ref[...] = values
            for copy in leaving:
                copy.wait()

        results = self.order.call(
            kernel,
            (1,),
            [pl.BlockSpec(memory_space=pltpu.SMEM)]
            + [
                pl.BlockSpec(memory_space=pl.ANY if place in free else pltpu.HBM)
                for place in range(count)
            ]
            + [whole(self.table.shape)],
            [pl.BlockSpec(memory_space=pltpu.HBM)] * len(outs)
            + [whole((sums, width))] * (1 if sums else 0),
            [pltpu.HBM((rows, width), kind) for kind in outs]
            + [jax.ShapeDtypeStruct((sums, width), F32)] * (1 if sums else 0),
            [pltpu.VMEM(operand.shape, operand.dtype) for operand in operands]
            + [pltpu.VMEM((rows, width), kind) for kind in outs]
            + [
                pltpu.SemaphoreType.DMA((count, blocks)),
                pltpu.SemaphoreType.DMA((len(outs), blocks)),
            ],
            20 * rows * width,
            sum(operand.size * operand.dtype.itemsize for operand in operands),
            name,
        )(
            self.y,
            *[
                operand
                if place in free
                else pltpu.with_memory_space_constraint(operand, pltpu.HBM)
                for place, operand in enumerate(operands)
            ],
            self.table,
        )
        return results

    def forward(self, index, base, parts=(), bias=None, low=True, full=False):
        def compute(flag, values, table_ref):
            hidden = values[0].astype(F32)
            if parts:
                hidden = hidden + self.sum_parts(values[1:]) + table_ref[bias : bias + 1, :]
            else:
                hidden = self.enter(flag, hidden)
            center = hidden - jnp.mean(hidden, axis=-1, keepdims=True)
            spread = jnp.mean(center * center, axis=-1, keepdims=True)
            normed = center * lax.rsqrt(spread + NORM_EPS) * table_ref[index : index + 1, :]
            normed = normed + table_ref[7 + index : 8 + index, :]
            results = [hidden]
            if low:
                results.append(normed)
            if full:
                results.append(self.leave(flag, normed))
            return results, None

        outs = [F32] + [BF16] * low + [F32] * full
        free = range(1, 1 + len(parts))
        return self.call(compute, (base, *parts), free, outs, 0, "norm_forward")

    def backward(self, index, hidden, parts, cotangent=None, flow=None, low=True, last=False):
        extras = [value for value in (cotangent, flow) if value is not None]

        def compute(flag, values, table_ref):
            values, others, passing = values[0], list(values[1:]), None
            if flow is not None:
                passing = others.pop()
            upstream = self.enter(flag, others.pop()) if cotangent is not None else None
            if parts:
                summed = self.sum_parts(others)
                upstream = summed if upstream is None else upstream + summed
            center = values - jnp.mean(values, axis=-1, keepdims=True)
            spread = jnp.mean(center * center, axis=-1, keepdims=True)
            scale = lax.rsqrt(spread + NORM_EPS)
            unit = center * scale
            pulled = upstream * table_ref[index : index + 1, :]
            level = jnp.mean(pulled, axis=-1, keepdims=True)
            tilt = jnp.mean(pulled * unit, axis=-1, keepdims=True)
            grad = scale * (pulled - level - unit * tilt)
            if flow is not None:
                grad = grad + passing
            added = [
                jnp.sum(value, axis=0, keepdims=True) for value in (upstream * unit, upstream, grad)
            ]
            results = [self.leave(flag, grad) if last else grad]
            if low:
                results.append(grad)
            return results, added

        grad, *rest, sums = self.call(
            compute,
            (hidden, *parts, *extras),
            range(1, 1 + len(parts)),
            [F32] + [BF16] * low,
            3,
            "norm_backward",
        )
        return grad, sums, *rest


def squares_kernel(copies, *refs):
    *value_refs, out_ref = refs
    total = jnp.zeros((1, 1), F32)
    for index, value_ref in enumerate(value_refs):
        values = value_ref[...].astype(F32)
        square = jnp.sum(values * values, keepdims=True).reshape(1, 1)
        if copies and index == len(value_refs) - 1:
            square = square * (1.0 / copies)
        total = total + square
    out_ref[...] = total


def sum_of_squares(order, arrays, small=None, copies=0):
    operands = (*arrays, small) if copies else arrays
    return order.call(
        partial(squares_kernel, copies),
        (1,),
        [Load(operand.shape) for operand in operands],
        whole((1, 1)),
        jax.ShapeDtypeStruct((1, 1), F32),
        [],
        2 * sum(operand.size for operand in operands),
        sum(operand.size * operand.dtype.itemsize for operand in operands),
        "squares",
    )(*operands)


def clip_factor(square_sum):
    return jnp.minimum(1.0, CLIP_NORM / (jnp.sqrt(square_sum) + 1e-06))


def adam(gradient, weight, first_old, second_old, factor, step_rate, decay_rate):
    clipped = gradient * factor
    moment = BETA_FIRST * first_old + (1.0 - BETA_FIRST) * clipped
    second_new = BETA_SECOND * second_old + (1.0 - BETA_SECOND) * clipped * clipped
    fixed_first = moment / (1.0 - BETA_FIRST**STEP)
    fixed_second = second_new / (1.0 - BETA_SECOND**STEP)
    updated = weight - step_rate * (
        fixed_first / (jnp.sqrt(fixed_second) + ADAM_EPS) + decay_rate * weight
    )
    return clipped, second_new, updated


def update_kernel(cut, rates, count, *refs):
    square_ref, refs = refs[0], refs[1:]
    grad_refs, refs = refs[:count], refs[count:]
    in_refs, out_refs = refs[: 3 * len(rates)], refs[3 * len(rates) :]
    factor = clip_factor(square_ref[...])
    for index, gradient in enumerate(cut(grad_refs, pl.program_id(0))):
        values = [ref[...] for ref in in_refs[3 * index : 3 * index + 3]]
        shape = values[0].shape
        results = adam(
            gradient.reshape(shape), *values, factor.reshape((1,) * len(shape)), rates[index], MATRIX_DECAY
        )
        for out_ref, result in zip(out_refs[3 * index : 3 * index + 3], results):
            out_ref[...] = result


def small_update_kernel(square_ref, small_ref, *refs):
    in_refs, out_refs, bias_ref = refs[:6], refs[6:12], refs[12]
    factor = clip_factor(square_ref[...])
    small = small_ref[...]
    vector_grad = jnp.concatenate([small[:14], small[19:25], small[14:19]], axis=0)
    count = (small.shape[0] - 25) // 2
    unit_rows = [
        jnp.concatenate(
            [small[25 + slot * count + index][None] for index in range(count)], axis=1
        )
        for slot in range(2)
    ]
    for index, gradient in enumerate((vector_grad, jnp.concatenate(unit_rows, axis=0))):
        values = [ref[...] for ref in in_refs[3 * index : 3 * index + 3]]
        results = adam(gradient, *values, factor, VECTOR_RATE, 0.0)
        for out_ref, result in zip(out_refs[3 * index : 3 * index + 3], results):
            out_ref[...] = result
    bias_ref[...] = out_refs[0][23:25, :]


def small_update(order, square_sum, small, vector_arrays, unit_arrays):
    arrays = (*vector_arrays, *unit_arrays)
    outs = [jax.ShapeDtypeStruct(array.shape, F32) for array in arrays]
    outs.append(jax.ShapeDtypeStruct((2, arrays[0].shape[1]), F32))
    return order.call(
        small_update_kernel,
        (1,),
        [whole((1, 1)), whole(small.shape)] + [whole(array.shape) for array in arrays],
        [whole(out.shape) for out in outs],
        outs,
        [],
        0,
        0,
        "update_small",
    )(square_sum, small, *arrays)


def choose(refs, step):
    value = refs[0][...]
    for index in range(1, len(refs)):
        value = jnp.where(step == index, refs[index][...], value)
    return value.astype(F32)


def update(order, square_sum, gradients, groups, rates, cut, name):
    arrays = [array for group in groups for array in group]

    def spec(shape):
        return pl.BlockSpec((1,) + shape[1:], lambda step: (step,) + (0,) * (len(shape) - 1))

    outs = [jax.ShapeDtypeStruct(array.shape, F32) for array in arrays]
    return order.call(
        partial(update_kernel, cut, rates, len(gradients)),
        (arrays[0].shape[0],),
        [whole((1, 1))]
        + [whole(gradient.shape) for gradient in gradients]
        + [spec(array.shape) for array in arrays],
        [spec(out.shape) for out in outs],
        outs,
        [],
        20 * sum(array.size for array in arrays) // 3,
        8 * sum(array.size for array in arrays),
        name,
    )(square_sum, *gradients, *arrays)


def body(
    source_tokens,
    target_tokens,
    source_lengths,
    target_lengths,
    bucket_kinds,
    source_cotangent,
    target_cotangent,
    attention_in,
    attention_out,
    hidden_in,
    hidden_out,
    vectors,
    hidden_bias,
    first_attention_in,
    first_attention_out,
    first_hidden_in,
    first_hidden_out,
    first_vectors,
    first_hidden_bias,
    second_attention_in,
    second_attention_out,
    second_hidden_in,
    second_hidden_out,
    second_vectors,
    second_hidden_bias,
):
    order = Order()
    moves = TensorMoves(order)
    split = CrossRows(order) if lax.axis_size("dp") == 8 else PlainRows(order)
    assert bucket_kinds.shape[0] == 1
    shard_rows = attention_in.shape[2]
    head_width = attention_in.shape[3]
    unit_width = hidden_in.shape[2]
    shard_units = hidden_bias.shape[1]

    small_shard = jnp.concatenate([vectors, hidden_bias.reshape(-1, shard_rows)], axis=0)
    small = split.stack(small_shard.astype(BF16)).astype(F32)

    attn_full = [None] * 3
    up_full = [None] * 2
    down_full = [None] * 2
    attn_zero = split.start(attention_shard(order, attention_in, attention_out, 0))
    attn_one = split.start(attention_shard(order, attention_in, attention_out, 1))
    up_shard, down_shard = feed_shard(order, hidden_in, hidden_out, 0)
    up_zero, down_zero = split.start(up_shard), split.start(down_shard)
    attn_two = split.start(attention_shard(order, attention_in, attention_out, 2))
    up_shard, down_shard = feed_shard(order, hidden_in, hidden_out, 1)
    up_one, down_one = split.start(up_shard), split.start(down_shard)

    norms = Norms(order, small[:, :25].transpose(1, 0, 2).reshape(25, -1), split.y)
    count = head_width // shard_rows
    own_blocks = split.blocks(small, moves.me * count, count)
    head_bias = jnp.concatenate([block[14:20] for block in own_blocks], axis=1)
    unit_bias = jnp.concatenate(
        [block[25:].reshape(2, shard_units) for block in own_blocks], axis=1
    )

    block_rows = source_tokens.shape[0]
    places = jnp.concatenate(
        [
            (moves.me ^ index) * block_rows + jnp.arange(block_rows, dtype=jnp.int32)
            for index in range(moves.count)
        ]
    )
    source_items, source_live = item_codes(bucket_kinds[0], source_lengths[0], places)
    target_items, target_live = item_codes(bucket_kinds[0], target_lengths[0], places)

    def layout_of(key_codes, query_codes):
        rows = jnp.stack([key_codes, places, query_codes])
        return jnp.pad(rows, ((0, 5), (0, 0))).astype(F32)

    encoder_layout = layout_of(source_live, source_items)
    self_layout = layout_of(target_live, target_items)
    cross_layout = layout_of(source_live, target_items)

    source, low = norms.forward(0, source_tokens)
    source_norm_one = moves.gather(low)
    target, low = norms.forward(3, target_tokens)
    target_norm_one = moves.gather(low)

    attn_full[0] = split.finish(attn_zero)
    attention = attention_forward(
        order,
        moves,
        attn_full[0],
        source_norm_one,
        source_norm_one,
        head_bias[:2],
        encoder_layout,
        False,
        (target_norm_one[2],),
    )
    next(attention)
    order.before_next(attn_one)
    attn_full[1] = split.finish(attn_one)
    branch, source_attn_state = next(attention)
    up_zero = order.after_last(up_zero)
    order.before_next(up_zero)
    up_full[0] = split.finish(up_zero)
    source_mid, low = norms.forward(1, source, branch, 20)
    source_norm_two = moves.gather(low)

    attention = attention_forward(
        order,
        moves,
        attn_full[1],
        target_norm_one,
        target_norm_one,
        head_bias[2:4],
        self_layout,
        True,
        (source_norm_two[2], up_full[0][1]),
    )
    next(attention)
    branch, self_state = next(attention)
    order.before_next(down_zero)
    down_full[0] = split.finish(down_zero)
    target_mid, low = norms.forward(4, target, branch, 21)
    target_norm_two = moves.gather(low)

    def feed_pair(slot_id, normed, first=(), between=None):
        weights = up_full[slot_id], down_full[slot_id]
        bias = unit_bias[slot_id : slot_id + 1]
        far = feed_forward(order, *weights, normed[2:], bias, False)
        arrived = moves.cross(*far[2:], first)
        if between is not None:
            order.before_next(between)
        near = feed_forward(order, *weights, normed[:2], bias, True)
        return moves.parts(near[2:], arrived), (near[:2], far[:2])

    branch, source_ffn_state = feed_pair(0, source_norm_two, (target_norm_two[2],), attn_two)
    attn_full[2] = split.finish(attn_two)
    source_last, low, encoder_output = norms.forward(2, source_mid, branch, 23, full=True)
    memory = moves.gather(low)
    order.before_next(up_one)
    up_full[1] = split.finish(up_one)

    attention = attention_forward(
        order,
        moves,
        attn_full[2],
        target_norm_two,
        memory,
        head_bias[4:],
        cross_layout,
        False,
        (up_full[1][1],),
    )
    next(attention)
    order.before_next(down_one)
    branch, cross_state = next(attention)
    down_full[1] = split.finish(down_one)
    target_cross, low = norms.forward(5, target_mid, branch, 22)
    low = lax.optimization_barrier((low, down_full[1][1]))[0]
    target_norm_three = moves.gather(low)
    branch, target_ffn_state = feed_pair(1, target_norm_three)
    target_last, decoder_output = norms.forward(6, target_cross, branch, 24, low=False, full=True)

    def feed_back_pair(slot_id, rows, states, first=()):
        weights = up_full[slot_id], down_full[slot_id]
        near = feed_backward(order, *weights, rows[:2], states[0][1], True)
        if len(rows) < 4:
            rows = moves.gather_late(rows)
        far = feed_backward(order, *weights, rows[2:], states[1][1], False)
        parts = moves.parts(near[2:], moves.cross(*far[2:], first))
        return rows, parts, (near[0], far[0]), near[1] + far[1]

    def feed_weight_pair(upstream_rows, states, normed, pre_grads):
        up_send, up_keep = feed_weights(order, normed, pre_grads)
        up_arrived = split.send(up_send)
        activated = (states[0][0], states[1][0])
        down_send, down_keep = feed_weights(order, upstream_rows, activated)
        return (up_keep, up_arrived), (down_keep, split.send(down_send))

    target_flow, sums_six, low = norms.backward(6, target_last, (), target_cotangent)
    upstream_rows, parts, pre_grads, unit_sums_one = feed_back_pair(
        1, moves.gather_near(low), target_ffn_state
    )
    up_parts, down_parts = feed_weight_pair(
        upstream_rows, target_ffn_state, target_norm_three, pre_grads
    )
    target_flow, sums_five, low = norms.backward(5, target_cross, parts, None, target_flow)
    upstream_rows = moves.gather(low)

    up_grad_one = split.settle(*up_parts)
    grads, cross_sums = attention_backward(
        order, attn_full[2], upstream_rows, cross_state, cross_layout, False
    )
    memory_arrived = moves.cross(
        *spread_rows(order, grads, attn_full[2], head_width, 3 * head_width, 2), (down_parts[1],)
    )
    arrived = moves.cross(*spread_rows(order, grads, attn_full[2], 0, head_width, 2))
    near = spread_rows(order, grads, attn_full[2], head_width, 3 * head_width, 0)
    memory_parts = moves.parts(near, memory_arrived)
    near = spread_rows(order, grads, attn_full[2], 0, head_width, 0)
    parts = moves.parts(near, arrived)
    send, keep_two = attention_weights(
        order, target_norm_two, memory, upstream_rows, grads, cross_state[1]
    )
    arrived_two = split.send(send)
    down_grad_one = split.settle(*down_parts)
    source_flow, sums_two, low = norms.backward(2, source_last, memory_parts, source_cotangent)
    source_rows = moves.gather_near(lax.optimization_barrier((low, arrived))[0])
    target_flow, sums_four, low = norms.backward(4, target_mid, parts, None, target_flow)
    self_upstream = moves.gather(low)
    source_rows = moves.gather_late(source_rows)
    upstream_rows, parts, pre_grads, unit_sums_zero = feed_back_pair(
        0, source_rows, source_ffn_state, (arrived_two,)
    )
    attn_grad_two = split.settle(keep_two, arrived_two)
    up_parts, down_parts = feed_weight_pair(
        upstream_rows, source_ffn_state, source_norm_two, pre_grads
    )
    source_flow, sums_one, low = norms.backward(1, source_mid, parts, None, source_flow)
    upstream_rows = moves.gather(low)

    self_grads, self_sums = attention_backward(
        order, attn_full[1], self_upstream, self_state, self_layout, True
    )
    up_grad_zero = split.settle(*up_parts)
    self_arrived = moves.cross(
        *spread_rows(order, self_grads, attn_full[1], 0, 3 * head_width, 2), (upstream_rows[2],)
    )
    send, keep_one = attention_weights(
        order, target_norm_one, target_norm_one, self_upstream, self_grads, self_state[1]
    )
    arrived_one = split.send(send)
    near = spread_rows(order, self_grads, attn_full[1], 0, 3 * head_width, 0)
    self_parts = moves.parts(near, self_arrived)
    grads, source_sums = attention_backward(
        order, attn_full[0], upstream_rows, source_attn_state, encoder_layout, False
    )
    down_grad_zero = split.settle(*down_parts)
    send, keep_zero = attention_weights(
        order, source_norm_one, source_norm_one, upstream_rows, grads, source_attn_state[1]
    )
    arrived_zero = split.send(send)
    arrived = moves.cross(
        *spread_rows(order, grads, attn_full[0], 0, 3 * head_width, 2), (arrived_one, self_arrived)
    )
    attn_grad_one = split.settle(keep_one, arrived_one)
    near = spread_rows(order, grads, attn_full[0], 0, 3 * head_width, 0)
    parts = moves.parts(near, arrived)
    target_grad, sums_three = norms.backward(
        3, target, self_parts, None, target_flow, low=False, last=True
    )
    source_grad, sums_zero = norms.backward(
        0, source, parts, None, source_flow, low=False, last=True
    )

    norm_sums = (sums_zero, sums_one, sums_two, sums_three, sums_four, sums_five, sums_six)
    vector_rows = [sums[0:1] for sums in norm_sums] + [sums[1:2] for sums in norm_sums]
    vector_rows += [sums[2:3] for sums in (sums_one, sums_four, sums_five, sums_two, sums_six)]
    attn_grad_zero = split.settle(keep_zero, arrived_zero)
    early_squares = sum_of_squares(
        order,
        (attn_grad_one, attn_grad_two, up_grad_zero, up_grad_one, down_grad_zero, down_grad_one),
    )
    own_rows = [source_sums, self_sums, cross_sums]
    for sums in (unit_sums_zero, unit_sums_one):
        cut = sums.reshape(head_width // shard_rows, -1, shard_rows).transpose(1, 0, 2)
        own_rows.append(cut.reshape(-1, head_width))
    own_rows = jnp.concatenate(own_rows, axis=0)
    columns = jnp.arange(moves.count * head_width, dtype=jnp.int32) // head_width
    own_rows = jnp.where(columns[None, :] == moves.me, jnp.tile(own_rows, (1, moves.count)), 0.0)
    small_sum = split.spread(moves.total(jnp.concatenate(vector_rows + [own_rows], axis=0)))

    attn_grads = (attn_grad_zero, attn_grad_one, attn_grad_two)
    up_grads = (up_grad_zero, up_grad_one)
    down_grads = (down_grad_zero, down_grad_one)
    local_squares = early_squares + sum_of_squares(
        order, (attn_grad_zero,), small_sum, moves.count
    )
    square_sum = split.total(moves.total(local_squares))
    grad_norm = jnp.sqrt(square_sum)[0, 0]
    rate_in, rate_out, rate_down = (
        0.5 * D ** (-0.5),
        0.5 * (D // 8) ** (-0.5),
        0.5 * FF ** (-0.5),
    )

    def attention_cut(refs, step):
        values = choose(refs, step)
        inputs = [
            values[:, which * head_width : (which + 1) * head_width] for which in range(3)
        ]
        return jnp.stack(inputs), values[:, 3 * head_width :].T

    def up_cut(refs, step):
        return (choose(refs, step),)

    def down_cut(refs, step):
        return (choose(refs, step).T,)

    attn_new = update(
        order,
        square_sum,
        attn_grads,
        (
            (attention_in, first_attention_in, second_attention_in),
            (attention_out, first_attention_out, second_attention_out),
        ),
        (rate_in, rate_out),
        attention_cut,
        "update_attention",
    )
    up_new = update(
        order,
        square_sum,
        up_grads,
        ((hidden_in, first_hidden_in, second_hidden_in),),
        (rate_in,),
        up_cut,
        "update_up",
    )
    down_new = update(
        order,
        square_sum,
        down_grads,
        ((hidden_out, first_hidden_out, second_hidden_out),),
        (rate_down,),
        down_cut,
        "update_down",
    )
    *small_new, bias_grad = small_update(
        order,
        square_sum,
        small_sum,
        (vectors, first_vectors, second_vectors),
        (hidden_bias, first_hidden_bias, second_hidden_bias),
    )
    return (
        encoder_output,
        decoder_output,
        source_grad,
        target_grad,
        grad_norm,
        *attn_new,
        *up_new,
        *down_new,
        *small_new,
        bias_grad,
    )


def solution(mesh):
    placed = (
        P(("dp", "tensor"), None),
        P(("dp", "tensor"), None),
        P("dp", None),
        P("dp", None),
        P("dp"),
        P(("dp", "tensor"), None),
        P(("dp", "tensor"), None),
        P(None, None, "dp", "tensor"),
        P(None, "tensor", "dp"),
        P(None, "dp", "tensor"),
        P(None, "tensor", "dp"),
        P(None, "dp"),
        P(None, "dp"),
        P(None, None, "dp", "tensor"),
        P(None, "tensor", "dp"),
        P(None, "dp", "tensor"),
        P(None, "tensor", "dp"),
        P(None, "dp"),
        P(None, "dp"),
        P(None, None, "dp", "tensor"),
        P(None, "tensor", "dp"),
        P(None, "dp", "tensor"),
        P(None, "tensor", "dp"),
        P(None, "dp"),
        P(None, "dp"),
    )
    return jax.shard_map(
        body,
        mesh=mesh,
        in_specs=placed,
        out_specs=(
            P(("dp", "tensor"), None),
            P(("dp", "tensor"), None),
            P(("dp", "tensor"), None),
            P(("dp", "tensor"), None),
            P(),
            P(None, None, "dp", "tensor"),
            P(None, None, "dp", "tensor"),
            P(None, None, "dp", "tensor"),
            P(None, "tensor", "dp"),
            P(None, "tensor", "dp"),
            P(None, "tensor", "dp"),
            P(None, "dp", "tensor"),
            P(None, "dp", "tensor"),
            P(None, "dp", "tensor"),
            P(None, "tensor", "dp"),
            P(None, "tensor", "dp"),
            P(None, "tensor", "dp"),
            P(None, "dp"),
            P(None, "dp"),
            P(None, "dp"),
            P(None, "dp"),
            P(None, "dp"),
            P(None, "dp"),
            P(None, "dp"),
        ),
        check_vma=False,
    )
```

```python
from functools import partial

import jax
import jax.numpy as jnp
from jax import lax
from jax.experimental import pallas as pl
from jax.experimental.pallas import tpu as pltpu
from jax.sharding import PartitionSpec as P

D = 1024
FF = 4096
L = 1024
ITEMS = 8
STEP = 10
HEAD = 64
ITEM = 128


NORM_EPS = 1e-05
CLIP_NORM = 1.0
BETA_FIRST = 0.9
BETA_SECOND = 0.999
ADAM_EPS = 1e-08
MATRIX_DECAY = 0.01
MASKED = -1e30

BF16 = jnp.bfloat16
F32 = jnp.float32
VECTOR_RATE = 0.3
SMALL = 16384
VMEM_BYTES = 24 * 1024 * 1024


class TensorMoves:
    def __init__(self, order):
        self.order = order
        self.count = lax.axis_size("tensor")
        assert self.count == 4
        self.me = lax.axis_index("tensor")

    def swap(self, values, bit):
        pairs = [(index, index ^ bit) for index in range(self.count)]
        return lax.ppermute(values, "tensor", pairs)

    def gather(self, shard):
        return self.gather_far(self.gather_near(shard))

    def gather_near(self, shard):
        return shard, self.swap(shard, 1), self.swap(shard, 2)

    def gather_far(self, rows):
        return *rows, self.swap(rows[2], 1)

    def gather_late(self, rows):
        return *rows, self.swap(self.order.after_last(rows[2]), 1)

    def cross(self, send, keep, first=()):
        send = lax.optimization_barrier((send, first))[0]
        crossing = (keep.astype(F32) + self.swap(send, 1).astype(F32)).astype(BF16)
        self.order.before_next(crossing)
        return self.swap(crossing, 2)

    def parts(self, near, arrived):
        first, second, keep = near
        return keep, self.swap(first, 1), self.swap(second, 1), arrived

    @property
    def steps(self):
        return [lambda values, bit=bit: values + self.swap(values, bit) for bit in (1, 2)]

    def total(self, values):
        for step in self.steps:
            values = step(values)
        return values


class PlainRows:
    def __init__(self, order):
        self.order = order
        self.count = lax.axis_size("dp")
        self.me = lax.axis_index("dp")
        self.y = None

    def start(self, shard):
        return lax.all_gather(shard, "dp", axis=0, tiled=True)

    def finish(self, full):
        half = full.shape[0] // 2
        return full[:half], full[half:]

    def blocks(self, stacked, first, count):
        return [
            lax.dynamic_index_in_dim(stacked, first + index, 0, False) for index in range(count)
        ]

    def send(self, far_part):
        return far_part

    def settle(self, near_part, arrived):
        values = jnp.concatenate([near_part, arrived.astype(F32)], 0)
        return lax.psum_scatter(values, "dp", scatter_dimension=0, tiled=True)

    def stack(self, shard):
        return lax.all_gather(shard, "dp", axis=0)

    def spread(self, values):
        return lax.psum_scatter(values, "dp", scatter_dimension=1, tiled=True)

    @property
    def steps(self):
        return [lambda values: lax.psum(values, "dp")]

    def total(self, values):
        for step in self.steps:
            values = step(values)
        return values


class CrossRows(PlainRows):
    ALONG_Z = [[0, 2, 4, 6], [1, 3, 5, 7]]

    def __init__(self, order):
        super().__init__(order)
        self.z = self.me // 2
        self.y = self.me % 2

    def swap(self, values, bits):
        pairs = [(index, index ^ bits) for index in range(self.count)]
        return lax.ppermute(values, "dp", pairs)

    def start(self, shard):
        return lax.all_gather(shard, "dp", axis=0, tiled=True, axis_index_groups=self.ALONG_Z)

    def finish(self, near):
        return near, self.swap(near, 1)

    def blocks(self, stacked, first, count):
        assert count == 2
        near = lax.dynamic_index_in_dim(stacked, first // 2, 0, False)
        far = lax.dynamic_index_in_dim(stacked, first // 2 + 4, 0, False)
        even = self.y == 0
        return [jnp.where(even, near, far), jnp.where(even, far, near)]

    def send(self, far_part):
        return self.swap(far_part, 1)

    def settle(self, near_part, arrived):
        near_part, arrived = self.order.after_last((near_part, arrived))
        part = (near_part + arrived.astype(F32)).astype(BF16)
        self.order.before_next(part)
        return lax.psum_scatter(
            part, "dp", scatter_dimension=0, tiled=True, axis_index_groups=self.ALONG_Z
        )

    def stack(self, shard):
        pieces = jnp.stack([shard] + [self.swap(shard, bits) for bits in (2, 4, 6)])
        near = jnp.stack(
            [lax.dynamic_index_in_dim(pieces, self.z ^ index, 0, False) for index in range(4)]
        )
        return jnp.concatenate([near, self.swap(near, 1)], axis=0)

    def spread(self, values):
        rows = values.shape[0]
        blocks = values.reshape(rows, 4, 2, -1)
        first, second = [blocks[:, :, index].reshape(rows, -1) for index in range(2)]
        even = self.y == 0
        part = jnp.where(even, first, second) + self.swap(jnp.where(even, second, first), 1)
        size = part.shape[1] // 4
        total = lax.dynamic_slice_in_dim(part, self.z * size, size, 1)
        for bits in (2, 4, 6):
            sent = lax.dynamic_slice_in_dim(part, (self.z ^ (bits // 2)) * size, size, 1)
            total = total + self.swap(sent, bits)
        return total

    @property
    def steps(self):
        return [lambda values, bits=bits: values + self.swap(values, bits) for bits in (1, 2, 4)]


def item_codes(row_kind, lengths, places):
    items = jnp.where(row_kind == 1, 0, places // ITEM)
    within = jnp.where(row_kind == 1, places, places % ITEM)
    limit = jnp.zeros_like(places)
    for index in range(ITEMS):
        limit = jnp.where(items == index, lengths[index], limit)
    return items, jnp.where(within < limit, items, -1)


def dot_nn(left, right):
    return jnp.dot(left, right, preferred_element_type=F32)


def dot_nt(left, right):
    return lax.dot_general(left, right, (((1,), (1,)), ((), ())), preferred_element_type=F32)


def dot_tn(left, right):
    return lax.dot_general(left, right, (((0,), (0,)), ((), ())), preferred_element_type=F32)


def wide_dot(rows, near, far):
    half = near.shape[0]
    return dot_nn(rows[:, :half], near[...]) + dot_nn(rows[:, half:], far[...])


class Load:
    def __init__(self, shape, start=None):
        self.shape = shape
        self.start = start or (0,) * len(shape)


class Loaded:
    def __init__(self, copy, buffer, step):
        self.copy = copy
        self.buffer = buffer
        self.step = step
        self.waited = False

    @property
    def shape(self):
        return self.buffer.shape

    def ready(self):
        if not self.waited:
            self.waited = True
            pl.when(self.step == 0)(self.copy.wait)

    def wait_here(self):
        self.waited = True
        self.copy.wait()

    def __getitem__(self, where):
        self.ready()
        return self.buffer[where]


class Order:
    def __init__(self):
        self.marks = ()

    def call(self, kernel, grid, in_specs, out_specs, out_shapes, scratch, flops, moved, name):
        marks = [
            pltpu.with_memory_space_constraint(mark, pltpu.HBM) if mark.size > SMALL else mark
            for mark in self.marks
        ]
        loads = [(place, spec) for place, spec in enumerate(in_specs) if isinstance(spec, Load)]
        hbm = pl.BlockSpec(memory_space=pltpu.HBM)

        def marked(*refs):
            refs = list(refs[len(marks) :])
            step = pl.program_id(0)
            loaded = []
            if loads:
                *refs, semaphores = refs
                buffers = refs[-len(loads) :]
                refs = refs[: -len(loads)]
                for index, (place, spec) in enumerate(loads):
                    source = refs[place].at[
                        tuple(pl.ds(first, size) for first, size in zip(spec.start, spec.shape))
                    ]
                    copy = pltpu.make_async_copy(source, buffers[index], semaphores.at[index])
                    loaded.append(Loaded(copy, buffers[index], step))
                    refs[place] = loaded[-1]

                @pl.when(step == 0)
                def _():
                    for item in loaded:
                        item.copy.start()

            kernel(*refs)
            for item in loaded:
                item.ready()

        def run(*operands):
            operands = list(operands)
            buffers = []
            for place, spec in loads:
                buffers.append(pltpu.VMEM(spec.shape, operands[place].dtype))
                operands[place] = pltpu.with_memory_space_constraint(operands[place], pltpu.HBM)
            if loads:
                buffers.append(pltpu.SemaphoreType.DMA((len(loads),)))
            results = pl.pallas_call(
                marked,
                grid=grid,
                in_specs=[
                    hbm if mark.size > SMALL else pl.BlockSpec(memory_space=pl.ANY)
                    for mark in marks
                ]
                + [hbm if isinstance(spec, Load) else spec for spec in in_specs],
                out_specs=out_specs,
                out_shape=out_shapes,
                scratch_shapes=list(scratch) + buffers,
                compiler_params=pltpu.CompilerParams(
                    vmem_limit_bytes=VMEM_BYTES,
                    dimension_semantics=("arbitrary",) * len(grid),
                ),
                cost_estimate=pl.CostEstimate(
                    flops=flops, bytes_accessed=moved, transcendentals=0
                ),
                name=name,
            )(*marks, *operands)
            self.marks = (min(jax.tree.leaves(results), key=lambda leaf: leaf.size),)
            return results

        return run

    def before_next(self, value):
        self.marks += (value,)

    def after_last(self, value):
        return lax.optimization_barrier((value, self.marks))[0]


def whole(shape):
    return pl.BlockSpec(
        shape, lambda step: (0,) * len(shape), pipeline_mode=pl.Buffered(buffer_count=1)
    )


def pair_bias(layout_ref, start, rows, causal):
    turned = layout_ref[...].T
    queries = pl.ds(start, rows)
    allowed = turned[:, 0:1] == layout_ref[2:3, queries]
    if causal:
        allowed = allowed & (turned[:, 1:2] <= layout_ref[1:2, queries])
    return jnp.where(allowed, 0.0, MASKED).astype(F32)


def head_rows_only(block, head, scale=None):
    lanes = lax.broadcasted_iota(jnp.int32, block.shape, 1) // HEAD
    if scale is not None:
        block = block * jnp.asarray(scale, block.dtype)
    return jnp.where(lanes == head, block, jnp.zeros_like(block))


def over_keys(combine, values):
    parts = values.reshape(8, values.shape[0] // 8, values.shape[1])
    return combine(combine(parts, axis=0), axis=0, keepdims=True)


def attend_block(queries, key_rows, values_turned, bias, heads):
    scores = []
    for head in range(heads):
        picked = head_rows_only(queries, head, HEAD ** (-0.5))
        scores.append(dot_nt(key_rows, picked) + bias)
    largest = [over_keys(jnp.max, score) for score in scores]
    contexts = []
    totals = []
    for head in range(heads):
        weights = jnp.exp(scores[head] - largest[head])
        total = over_keys(jnp.sum, weights)
        context = dot_nn(
            values_turned[head * HEAD : (head + 1) * HEAD, :], weights.astype(BF16)
        )
        contexts.append(context * (1.0 / total))
        totals.append(largest[head] + jnp.log(total))
    return jnp.concatenate(contexts, axis=0).T, jnp.concatenate(totals, axis=0)


def out_parts(rows, out_near, out_far, step, send_refs, keep_ref):
    half = out_near.shape[0]
    near = dot_nt(rows, out_near)
    far = dot_nt(rows, out_far)

    @pl.when(step == 0)
    def _():
        if len(send_refs) == 1:
            send_refs[0][:, :half] = near.astype(BF16)
            send_refs[0][:, half:] = far.astype(BF16)
        else:
            send_refs[0][...] = near.astype(BF16)
            send_refs[1][...] = far.astype(BF16)

    @pl.when(step == 1)
    def _():
        keep_ref[:, :half] = near.astype(keep_ref.dtype)
        keep_ref[:, half:] = far.astype(keep_ref.dtype)


def part_shapes(rows, half, halves):
    sends = [(rows, half)] * 2 if halves else [(rows, 2 * half)]
    return sends + [(rows, 2 * half)], [BF16] * len(sends) + [F32 if halves else BF16]


def part_outs(rows, half, halves):
    shapes, kinds = part_shapes(rows, half, halves)
    return [jax.ShapeDtypeStruct(shape, kind) for shape, kind in zip(shapes, kinds)]


def part_specs(rows, half, halves):
    return [whole(shape) for shape in part_shapes(rows, half, halves)[0]]


def attend_tail(
    step, qkv_ref, turned_ref, layout_ref, causal, out_near, out_far, first_row, outs, heads
):
    context_ref, total_ref, *send_refs, keep_ref = outs
    rows = keep_ref.shape[0]
    wide = context_ref.shape[1]
    start = pl.multiple_of(first_row + (1 - step) * rows, rows)
    bias = pair_bias(layout_ref, start, rows, causal)
    context, totals = attend_block(
        qkv_ref[pl.ds(start, rows), :wide],
        qkv_ref[:, wide : 2 * wide],
        turned_ref[...],
        bias,
        heads,
    )
    context = context.astype(BF16)
    context_ref[...] = context
    total_ref[...] = totals
    out_parts(context, out_near, out_far, step, send_refs, keep_ref)


def attend_far_kernel(causal, is_cross, heads, *refs):
    normed_refs = memory_refs = refs[:4]
    refs = refs[4:]
    if is_cross:
        memory_refs, refs = refs[:4], refs[4:]
    full_near_ref, full_far_ref, bias_ref = refs[:3]
    layout_ref = refs[3]
    qkv_ref, context_ref, *outs, turned_ref = refs[4:]
    step = pl.program_id(0)
    rows = outs[-1].shape[0]
    wide = context_ref.shape[1]

    @pl.when(step == 0)
    def _():
        def project(source_refs, begin, end, biases):
            for index in range(4):
                part = source_refs[index][...]
                values = wide_dot(part, full_near_ref[:, begin:end], full_far_ref[:, begin:end])
                span = slice(index * rows, (index + 1) * rows)
                for place, which in enumerate(range(begin // wide, end // wide)):
                    piece = values[:, place * wide : (place + 1) * wide]
                    if biases[which] is not None:
                        piece = piece + bias_ref[biases[which] : biases[which] + 1, :]
                    qkv_ref[span, which * wide : (which + 1) * wide] = piece.astype(BF16)

        biases = (0, None, 1)
        if is_cross:
            project(normed_refs, 0, wide, biases)
            project(memory_refs, wide, 3 * wide, biases)
        else:
            project(normed_refs, 0, 3 * wide, biases)
        turned_ref[...] = qkv_ref[:, 2 * wide :].T

    attend_tail(
        step,
        qkv_ref,
        turned_ref,
        layout_ref,
        causal,
        full_near_ref[:, 3 * wide :],
        full_far_ref[:, 3 * wide :],
        2 * rows,
        (context_ref, *outs),
        heads,
    )


def attend_near_kernel(causal, heads, *refs):
    qkv_ref, out_near_ref, out_far_ref = refs[:3]
    layout_ref = refs[3]
    context_ref, *outs, turned_ref = refs[4:]
    step = pl.program_id(0)
    wide = context_ref.shape[1]

    @pl.when(step == 0)
    def _():
        turned_ref[...] = qkv_ref[:, 2 * wide :].T

    attend_tail(
        step,
        qkv_ref,
        turned_ref,
        layout_ref,
        causal,
        out_near_ref[...],
        out_far_ref[...],
        0,
        (context_ref, *outs),
        heads,
    )


def attention_forward(order, moves, full, normed, memory, biases, layout, causal, first):
    length = layout.shape[1]
    rows = length // 4
    width = full[0].shape[1]
    wide = width // 4
    heads = wide // HEAD
    half = full[0].shape[0]
    is_cross = memory is not normed
    sources = tuple(normed) + (tuple(memory) if is_cross else ())
    pairs = 4 * rows * length // 2 * wide * heads

    half_outs = [
        jax.ShapeDtypeStruct((2 * rows, wide), BF16),
        jax.ShapeDtypeStruct((heads, 2 * rows), F32),
    ]
    half_specs = [
        pl.BlockSpec((rows, wide), lambda step: (1 - step, 0)),
        pl.BlockSpec((heads, rows), lambda step: (0, 1 - step)),
    ]
    turned = pltpu.VMEM((wide, length), BF16)
    qkv, context_far, totals_far, send_far, keep_far = order.call(
        partial(attend_far_kernel, causal, is_cross, heads),
        (2,),
        [whole((rows, 2 * half))] * len(sources)
        + [whole((half, width))] * 2
        + [whole(biases.shape), whole(layout.shape)],
        [whole((length, 3 * wide))] + half_specs + part_specs(rows, half, False),
        [jax.ShapeDtypeStruct((length, 3 * wide), BF16)]
        + half_outs
        + part_outs(rows, half, False),
        [turned],
        2 * length * 2 * half * 3 * wide + pairs,
        12 * length * 2 * half,
        "attend_far",
    )(*sources, *full, biases, layout)
    arrived = moves.cross(send_far, keep_far, first)
    yield
    context_near, totals_near, *near = order.call(
        partial(attend_near_kernel, causal, heads),
        (2,),
        [whole((length, 3 * wide))]
        + [pl.BlockSpec((half, wide), lambda step: (0, 3))] * 2
        + [whole(layout.shape)],
        half_specs + part_specs(rows, half, True),
        half_outs + part_outs(rows, half, True),
        [turned],
        pairs,
        6 * length * 2 * half,
        "attend_near",
    )(qkv, *full, layout)
    branch = moves.parts(near, arrived)
    yield branch, (qkv, (context_near, context_far), (totals_near, totals_far))


def attend_back_kernel(causal, heads, *refs):
    qkv_ref, first_ref, out_near_ref, out_far_ref = refs[:4]
    context_refs, total_refs, layout_ref = refs[4:6], refs[6:8], refs[8]
    grad_refs = (first_ref, *refs[9:12])
    grads_ref, sums_ref = refs[12:14]
    keys_turned_ref, key_sum_ref, value_sum_ref, grad_ref, context_ref, total_ref = refs[14:]
    step = pl.program_id(0)
    rows = context_ref.shape[0]
    wide = context_ref.shape[1]
    scale = HEAD ** (-0.5)

    @pl.when(step == 0)
    def _():
        keys_turned_ref[...] = qkv_ref[:, wide : 2 * wide].T
        key_sum_ref[...] = jnp.zeros_like(key_sum_ref)
        value_sum_ref[...] = jnp.zeros_like(value_sum_ref)

    for loaded in (*context_refs, *total_refs):
        loaded.ready()
    for index in range(4):

        @pl.when(step == index)
        def _(index=index):
            span = slice((index % 2) * rows, (index % 2 + 1) * rows)
            grad_refs[index].wait_here()
            grad_ref[...] = grad_refs[index][...]
            context_ref[...] = context_refs[index // 2][span, :]
            total_ref[...] = total_refs[index // 2][:, span]

    context_grad = wide_dot(grad_ref[...], out_near_ref, out_far_ref).astype(BF16)
    products_turned = (context_grad.astype(F32) * context_ref[...].astype(F32)).T
    start = pl.multiple_of(step * rows, rows)
    bias = pair_bias(layout_ref, start, rows, causal)
    queries = qkv_ref[pl.ds(start, rows), :wide]
    key_rows = qkv_ref[:, wide : 2 * wide]
    value_rows = qkv_ref[:, 2 * wide :]
    query_grads = []

    def products(head):
        picked = head_rows_only(queries, head, scale)
        picked_grad = head_rows_only(context_grad, head)
        scores = dot_nt(key_rows, picked) + bias
        return picked, picked_grad, scores, dot_nt(value_rows, picked_grad)

    ahead = products(0)
    for head in range(heads):
        picked, picked_grad, scores, weight_grad = ahead
        if head + 1 < heads:
            ahead = products(head + 1)
        span = slice(head * HEAD, (head + 1) * HEAD)
        weights = jnp.exp(scores - total_ref[head : head + 1, :])
        diagonal = jnp.sum(products_turned[span, :], axis=0, keepdims=True)
        score_grad = (weights * (weight_grad - diagonal)).astype(BF16)
        value_sum_ref[...] += dot_nn(weights.astype(BF16), picked_grad)
        key_sum_ref[...] += dot_nn(score_grad, picked)
        query_grads.append(dot_nn(keys_turned_ref[span, :], score_grad))
    query_grad = jnp.concatenate(query_grads, axis=0).T * scale
    grads_ref[pl.ds(start, rows), :wide] = query_grad.astype(BF16)

    @pl.when(step == 3)
    def _():
        grads_ref[:, wide : 2 * wide] = key_sum_ref[...].astype(BF16)
        grads_ref[:, 2 * wide :] = value_sum_ref[...].astype(BF16)
        for place, begin in ((0, 0), (1, 2 * wide)):
            values = grads_ref[:, begin : begin + wide].astype(F32)
            sums_ref[place : place + 1, :] = jnp.sum(values, axis=0, keepdims=True)


def spread_kernel(begin, end, rows_ref, near_ref, far_ref, *outs):
    step = pl.program_id(0)
    part = rows_ref[:, begin:end]
    out_parts(part, near_ref[:, begin:end], far_ref[:, begin:end], step, outs[:-1], outs[-1])


def spread_rows(order, grads, full, begin, end, first):
    rows = grads.shape[0] // 4
    half = full[0].shape[0]
    wide = grads.shape[1]
    return order.call(
        partial(spread_kernel, begin, end),
        (2,),
        [pl.BlockSpec((rows, wide), lambda step: (first + 1 - step, 0))]
        + [whole((half, wide))] * 2,
        part_specs(rows, half, first == 0),
        part_outs(rows, half, first == 0),
        [],
        4 * rows * 2 * half * (end - begin),
        6 * rows * 2 * half + 4 * half * wide,
        "spread_rows",
    )(grads, *full)


def later_half(step, size):
    return pl.ds(pl.multiple_of((1 - step) * size, size), size)


def rows_dot(left_refs, right, begin, end, columns=slice(None)):
    total = None
    for index, left_ref in enumerate(left_refs):
        rows = left_ref.shape[0]
        if isinstance(right, tuple):
            first = (index % 2) * rows
            part = right[index // 2][first : first + rows, begin:end]
        else:
            part = right[index * rows : (index + 1) * rows, begin:end]
        product = dot_tn(left_ref[:, columns], part)
        total = product if total is None else total + product
    return total


def attention_weight_kernel(is_cross, *refs):
    normed_refs = memory_refs = refs[:4]
    refs = refs[4:]
    if is_cross:
        memory_refs, refs = refs[:4], refs[4:]
    upstream_refs, grads_ref, context_refs, outs = refs[:4], refs[4], refs[5:7], refs[7:]
    send_ref, keep_ref = outs
    step = pl.program_id(0)
    wide = context_refs[0].shape[1]
    columns = later_half(step, send_ref.shape[0])
    if is_cross:
        pieces = [
            rows_dot(normed_refs, grads_ref, 0, wide, columns),
            rows_dot(memory_refs, grads_ref, wide, 3 * wide, columns),
        ]
    else:
        pieces = [rows_dot(normed_refs, grads_ref, 0, 3 * wide, columns)]
    pieces.append(rows_dot(upstream_refs, tuple(context_refs), 0, wide, columns))

    @pl.when(step == 0)
    def _():
        send_ref[...] = jnp.concatenate(pieces, axis=1).astype(BF16)

    @pl.when(step == 1)
    def _():
        keep_ref[...] = jnp.concatenate(pieces, axis=1)


def attention_weights(order, normed, memory, upstream, grads, contexts):
    rows, width = normed[0].shape
    wide = contexts[0].shape[1]
    is_cross = memory is not normed
    sources = tuple(normed) + (tuple(memory) if is_cross else ()) + tuple(upstream)
    half = width // 2
    outs = (half, 4 * wide)
    return order.call(
        partial(attention_weight_kernel, is_cross),
        (2,),
        [Load((rows, width))] * len(sources)
        + [whole(grads.shape)]
        + [Load((2 * rows, wide))] * 2,
        [whole(outs)] * 2,
        [jax.ShapeDtypeStruct(outs, BF16), pltpu.HBM(outs, F32)],
        [],
        8 * rows * width * 4 * wide,
        2 * rows * width * (len(sources) + 4) + 6 * half * 4 * wide,
        "attention_weights",
    )(*sources, grads, *contexts)


def attention_backward(order, full, upstream_rows, stored, layout, causal):
    qkv, contexts, totals = stored
    length = qkv.shape[0]
    rows = length // 4
    wide = qkv.shape[1] // 3
    heads = wide // HEAD
    half = full[0].shape[0]
    return order.call(
        partial(attend_back_kernel, causal, heads),
        (4,),
        [Load(qkv.shape), Load((rows, 2 * half))]
        + [Load((half, wide), (0, 3 * wide))] * 2
        + [Load((2 * rows, wide))] * 2
        + [Load((heads, 2 * rows))] * 2
        + [Load(layout.shape)]
        + [Load((rows, 2 * half))] * 3,
        [whole(qkv.shape), whole((2, wide))],
        [jax.ShapeDtypeStruct(qkv.shape, BF16), jax.ShapeDtypeStruct((2, wide), F32)],
        [
            pltpu.VMEM((wide, length), BF16),
            pltpu.VMEM((length, wide), F32),
            pltpu.VMEM((length, wide), F32),
            pltpu.VMEM((rows, 2 * half), BF16),
            pltpu.VMEM((rows, wide), BF16),
            pltpu.VMEM((heads, rows), F32),
        ],
        10 * length * length * wide * heads,
        12 * length * 2 * half,
        "attend_back",
    )(qkv, upstream_rows[0], *full, *contexts, *totals, layout, *upstream_rows[1:])


GELU_SCALE = 0.7978845608028654
GELU_CUBE = 0.044715


def feed_kernel(own_ref, near_ref, up_near, up_far, down_near, down_far, bias_ref, *outs):
    activated_ref, slope_ref, *send_refs, keep_ref = outs
    step = pl.program_id(0)
    rows = jnp.where(step == 0, near_ref[...], own_ref[...])
    pre_act = wide_dot(rows, up_near[...], up_far[...]) + bias_ref[...]
    square = pre_act * pre_act
    bent = jnp.tanh(GELU_SCALE * pre_act * (1.0 + GELU_CUBE * square))
    activated = (0.5 * pre_act * (1.0 + bent)).astype(BF16)
    inner = GELU_SCALE * (1.0 + 3.0 * GELU_CUBE * square)
    slope = 0.5 * (1.0 + bent) + 0.5 * pre_act * (1.0 - bent * bent) * inner
    activated_ref[...] = activated
    slope_ref[...] = slope.astype(BF16)
    out_parts(activated, down_near[...], down_far[...], step, send_refs, keep_ref)


def feed_forward(order, up_full, down_full, pair_rows, unit_bias, halves):
    rows = pair_rows[0].shape[0]
    half, units = up_full[0].shape
    return order.call(
        feed_kernel,
        (2,),
        [whole((rows, 2 * half))] * 2 + [whole((half, units))] * 4 + [whole((1, units))],
        [pl.BlockSpec((rows, units), lambda step: (1 - step, 0))] * 2
        + part_specs(rows, half, halves),
        [jax.ShapeDtypeStruct((2 * rows, units), BF16)] * 2 + part_outs(rows, half, halves),
        [],
        16 * rows * half * units,
        20 * rows * units + 8 * half * units,
        "feed_forward",
    )(*pair_rows, *up_full, *down_full, unit_bias)


def feed_back_kernel(
    own_ref, near_ref, slope_ref, up_near, up_far, down_near, down_far, *outs
):
    grad_ref, sum_ref, *send_refs, keep_ref = outs
    step = pl.program_id(0)
    rows = jnp.where(step == 0, near_ref[...], own_ref[...])
    act_grad = wide_dot(rows, down_near[...], down_far[...])
    pre_grad = (act_grad * slope_ref[...].astype(F32)).astype(BF16)
    grad_ref[...] = pre_grad

    @pl.when(step == 0)
    def _():
        sum_ref[...] = jnp.zeros_like(sum_ref)

    sum_ref[...] += jnp.sum(pre_grad.astype(F32), axis=0, keepdims=True)
    out_parts(pre_grad, up_near[...], up_far[...], step, send_refs, keep_ref)


def feed_weight_kernel(*refs):
    left_refs, right_refs, (send_ref, keep_ref) = refs[:4], refs[4:6], refs[6:]
    step = pl.program_id(0)
    part = rows_dot(left_refs, tuple(right_refs), 0, send_ref.shape[1])

    @pl.when(step == 0)
    def _():
        send_ref[...] = part.astype(BF16)

    @pl.when(step == 1)
    def _():
        keep_ref[...] = part


def feed_weights(order, left, right):
    rows, width = left[0].shape
    units = right[0].shape[1]
    half = width // 2
    outs = (half, units)
    return order.call(
        feed_weight_kernel,
        (2,),
        [pl.BlockSpec((rows, half), lambda step: (0, 1 - step))] * 4
        + [whole((2 * rows, units))] * 2,
        [whole(outs)] * 2,
        [jax.ShapeDtypeStruct(outs, BF16), pltpu.HBM(outs, F32)],
        [],
        8 * rows * width * units,
        8 * rows * (width + units) + 6 * half * units,
        "feed_weights",
    )(*left, *right)


def feed_backward(order, up_full, down_full, pair_rows, slope, halves):
    rows = pair_rows[0].shape[0]
    half, units = up_full[0].shape
    return order.call(
        feed_back_kernel,
        (2,),
        [whole((rows, 2 * half))] * 2
        + [pl.BlockSpec((rows, units), lambda step: (1 - step, 0))]
        + [whole((half, units))] * 4,
        [pl.BlockSpec((rows, units), lambda step: (1 - step, 0)), whole((1, units))]
        + part_specs(rows, half, halves),
        [
            jax.ShapeDtypeStruct((2 * rows, units), BF16),
            jax.ShapeDtypeStruct((1, units), F32),
        ]
        + part_outs(rows, half, halves),
        [],
        16 * rows * half * units,
        20 * rows * units + 8 * half * units,
        "feed_backward",
    )(*pair_rows, slope, *up_full, *down_full)


def attention_shard_kernel(in_ref, out_ref, shard_ref):
    wide = in_ref.shape[3]
    for which in range(3):
        shard_ref[:, which * wide : (which + 1) * wide] = in_ref[0, which].astype(BF16)
    shard_ref[:, 3 * wide :] = out_ref[0].T.astype(BF16)


def attention_shard(order, attention_in, attention_out, slot_id):
    rows, wide = attention_in.shape[2:]
    return order.call(
        attention_shard_kernel,
        (1,),
        [
            pl.BlockSpec((1, 3, rows, wide), lambda step: (slot_id, 0, 0, 0)),
            pl.BlockSpec((1, wide, rows), lambda step: (slot_id, 0, 0)),
        ],
        whole((rows, 4 * wide)),
        jax.ShapeDtypeStruct((rows, 4 * wide), BF16),
        [],
        0,
        24 * rows * wide,
        "attention_shard",
    )(attention_in, attention_out)


def feed_shard_kernel(up_ref, down_ref, up_shard_ref, down_shard_ref):
    up_shard_ref[...] = up_ref[0].astype(BF16)
    down_shard_ref[...] = down_ref[0].T.astype(BF16)


def feed_shard(order, hidden_in, hidden_out, slot_id):
    rows, units = hidden_in.shape[1:]
    return order.call(
        feed_shard_kernel,
        (1,),
        [
            pl.BlockSpec((1, rows, units), lambda step: (slot_id, 0, 0)),
            pl.BlockSpec((1, units, rows), lambda step: (slot_id, 0, 0)),
        ],
        [whole((rows, units))] * 2,
        [jax.ShapeDtypeStruct((rows, units), BF16)] * 2,
        [],
        0,
        12 * rows * units,
        "feed_shard",
    )(hidden_in, hidden_out)


class Norms:
    def __init__(self, order, table, y):
        self.order = order
        self.table = table
        self.y = jnp.zeros((1,), jnp.int32) if y is None else y.astype(jnp.int32).reshape(1)
        self.ordered = y is None

    def enter(self, flag, values):
        if self.ordered:
            return values
        size = values.shape[1] // 8
        blocks = [values[:, index * size : (index + 1) * size] for index in range(8)]
        first = jnp.concatenate(blocks[0::2], axis=1)
        second = jnp.concatenate(blocks[1::2], axis=1)
        return jnp.concatenate(
            [jnp.where(flag == 0, first, second), jnp.where(flag == 0, second, first)], axis=1
        )

    def leave(self, flag, values):
        if self.ordered:
            return values
        half = values.shape[1] // 2
        near, far = values[:, :half], values[:, half:]
        first = jnp.where(flag == 0, near, far)
        second = jnp.where(flag == 0, far, near)
        size = half // 4
        blocks = []
        for index in range(4):
            span = slice(index * size, (index + 1) * size)
            blocks += [first[:, span], second[:, span]]
        return jnp.concatenate(blocks, axis=1)

    def sum_parts(self, parts):
        keep, first, second, arrived = [part.astype(F32) for part in parts]
        return keep + jnp.concatenate([first, second], axis=1) + arrived

    def call(self, compute, operands, free, outs, sums, name):
        rows, width = operands[0].shape
        blocks = 2
        block = rows // blocks
        count = len(operands)

        def kernel(flag_ref, *refs):
            in_refs, refs = refs[:count], refs[count:]
            table_ref, refs = refs[0], refs[1:]
            out_refs, refs = refs[: len(outs)], refs[len(outs) :]
            if sums:
                sums_ref, refs = refs[0], refs[1:]
            in_buffers, refs = refs[:count], refs[count:]
            out_buffers, (in_marks, out_marks) = refs[: len(outs)], refs[len(outs) :]

            def span(index):
                return pl.ds(index * block, block)

            arriving = [
                [
                    pltpu.make_async_copy(
                        ref.at[span(index)], buffer.at[span(index)], in_marks.at[place, index]
                    )
                    for place, (ref, buffer) in enumerate(zip(in_refs, in_buffers))
                ]
                for index in range(blocks)
            ]
            for copies in arriving:
                for copy in copies:
                    copy.start()
            total = None
            leaving = []
            for index, copies in enumerate(arriving):
                for copy in copies:
                    copy.wait()
                values = [buffer[span(index), :] for buffer in in_buffers]
                results, added = compute(flag_ref[0], values, table_ref)
                for place, (ref, buffer) in enumerate(zip(out_refs, out_buffers)):
                    buffer[span(index), :] = results[place].astype(buffer.dtype)
                    copy = pltpu.make_async_copy(
                        buffer.at[span(index)], ref.at[span(index)], out_marks.at[place, index]
                    )
                    copy.start()
                    leaving.append(copy)
                if sums:
                    total = added if total is None else [a + b for a, b in zip(total, added)]
            if sums:
                values = self.leave(flag_ref[0], jnp.concatenate(total, axis=0))
                sums_ref[...] = values
            for copy in leaving:
                copy.wait()

        results = self.order.call(
            kernel,
            (1,),
            [pl.BlockSpec(memory_space=pltpu.SMEM)]
            + [
                pl.BlockSpec(memory_space=pl.ANY if place in free else pltpu.HBM)
                for place in range(count)
            ]
            + [whole(self.table.shape)],
            [pl.BlockSpec(memory_space=pltpu.HBM)] * len(outs)
            + [whole((sums, width))] * (1 if sums else 0),
            [pltpu.HBM((rows, width), kind) for kind in outs]
            + [jax.ShapeDtypeStruct((sums, width), F32)] * (1 if sums else 0),
            [pltpu.VMEM(operand.shape, operand.dtype) for operand in operands]
            + [pltpu.VMEM((rows, width), kind) for kind in outs]
            + [
                pltpu.SemaphoreType.DMA((count, blocks)),
                pltpu.SemaphoreType.DMA((len(outs), blocks)),
            ],
            20 * rows * width,
            sum(operand.size * operand.dtype.itemsize for operand in operands),
            name,
        )(
            self.y,
            *[
                operand
                if place in free
                else pltpu.with_memory_space_constraint(operand, pltpu.HBM)
                for place, operand in enumerate(operands)
            ],
            self.table,
        )
        return results

    def forward(self, index, base, parts=(), bias=None, low=True, full=False):
        def compute(flag, values, table_ref):
            hidden = values[0].astype(F32)
            if parts:
                hidden = hidden + self.sum_parts(values[1:]) + table_ref[bias : bias + 1, :]
            else:
                hidden = self.enter(flag, hidden)
            center = hidden - jnp.mean(hidden, axis=-1, keepdims=True)
            spread = jnp.mean(center * center, axis=-1, keepdims=True)
            normed = center * lax.rsqrt(spread + NORM_EPS) * table_ref[index : index + 1, :]
            normed = normed + table_ref[7 + index : 8 + index, :]
            results = [hidden]
            if low:
                results.append(normed)
            if full:
                results.append(self.leave(flag, normed))
            return results, None

        outs = [F32] + [BF16] * low + [F32] * full
        free = range(1, 1 + len(parts))
        return self.call(compute, (base, *parts), free, outs, 0, "norm_forward")

    def backward(self, index, hidden, parts, cotangent=None, flow=None, low=True, last=False):
        extras = [value for value in (cotangent, flow) if value is not None]

        def compute(flag, values, table_ref):
            values, others, passing = values[0], list(values[1:]), None
            if flow is not None:
                passing = others.pop()
            upstream = self.enter(flag, others.pop()) if cotangent is not None else None
            if parts:
                summed = self.sum_parts(others)
                upstream = summed if upstream is None else upstream + summed
            center = values - jnp.mean(values, axis=-1, keepdims=True)
            spread = jnp.mean(center * center, axis=-1, keepdims=True)
            scale = lax.rsqrt(spread + NORM_EPS)
            unit = center * scale
            pulled = upstream * table_ref[index : index + 1, :]
            level = jnp.mean(pulled, axis=-1, keepdims=True)
            tilt = jnp.mean(pulled * unit, axis=-1, keepdims=True)
            grad = scale * (pulled - level - unit * tilt)
            if flow is not None:
                grad = grad + passing
            added = [
                jnp.sum(value, axis=0, keepdims=True) for value in (upstream * unit, upstream, grad)
            ]
            results = [self.leave(flag, grad) if last else grad]
            if low:
                results.append(grad)
            return results, added

        grad, *rest, sums = self.call(
            compute,
            (hidden, *parts, *extras),
            range(1, 1 + len(parts)),
            [F32] + [BF16] * low,
            3,
            "norm_backward",
        )
        return grad, sums, *rest


def squares_kernel(copies, *refs):
    *value_refs, out_ref = refs
    total = jnp.zeros((1, 1), F32)
    for index, value_ref in enumerate(value_refs):
        values = value_ref[...].astype(F32)
        square = jnp.sum(values * values, keepdims=True).reshape(1, 1)
        if copies and index == len(value_refs) - 1:
            square = square * (1.0 / copies)
        total = total + square
    out_ref[...] = total


def sum_of_squares(order, arrays, small=None, copies=0):
    operands = (*arrays, small) if copies else arrays
    return order.call(
        partial(squares_kernel, copies),
        (1,),
        [Load(operand.shape) for operand in operands],
        whole((1, 1)),
        jax.ShapeDtypeStruct((1, 1), F32),
        [],
        2 * sum(operand.size for operand in operands),
        sum(operand.size * operand.dtype.itemsize for operand in operands),
        "squares",
    )(*operands)


def clip_factor(square_sum):
    return jnp.minimum(1.0, CLIP_NORM / (jnp.sqrt(square_sum) + 1e-06))


def adam(gradient, weight, first_old, second_old, factor, step_rate, decay_rate):
    clipped = gradient * factor
    moment = BETA_FIRST * first_old + (1.0 - BETA_FIRST) * clipped
    second_new = BETA_SECOND * second_old + (1.0 - BETA_SECOND) * clipped * clipped
    fixed_first = moment / (1.0 - BETA_FIRST**STEP)
    fixed_second = second_new / (1.0 - BETA_SECOND**STEP)
    updated = weight - step_rate * (
        fixed_first / (jnp.sqrt(fixed_second) + ADAM_EPS) + decay_rate * weight
    )
    return clipped, second_new, updated


def update_kernel(cut, rates, count, *refs):
    square_ref, refs = refs[0], refs[1:]
    grad_refs, refs = refs[:count], refs[count:]
    in_refs, out_refs = refs[: 3 * len(rates)], refs[3 * len(rates) :]
    factor = clip_factor(square_ref[...])
    for index, gradient in enumerate(cut(grad_refs, pl.program_id(0))):
        values = [ref[...] for ref in in_refs[3 * index : 3 * index + 3]]
        shape = values[0].shape
        results = adam(
            gradient.reshape(shape), *values, factor.reshape((1,) * len(shape)), rates[index], MATRIX_DECAY
        )
        for out_ref, result in zip(out_refs[3 * index : 3 * index + 3], results):
            out_ref[...] = result


def small_update_kernel(square_ref, small_ref, *refs):
    in_refs, out_refs, bias_ref = refs[:6], refs[6:12], refs[12]
    factor = clip_factor(square_ref[...])
    small = small_ref[...]
    vector_grad = jnp.concatenate([small[:14], small[19:25], small[14:19]], axis=0)
    count = (small.shape[0] - 25) // 2
    unit_rows = [
        jnp.concatenate(
            [small[25 + slot * count + index][None] for index in range(count)], axis=1
        )
        for slot in range(2)
    ]
    for index, gradient in enumerate((vector_grad, jnp.concatenate(unit_rows, axis=0))):
        values = [ref[...] for ref in in_refs[3 * index : 3 * index + 3]]
        results = adam(gradient, *values, factor, VECTOR_RATE, 0.0)
        for out_ref, result in zip(out_refs[3 * index : 3 * index + 3], results):
            out_ref[...] = result
    bias_ref[...] = out_refs[0][23:25, :]


def small_update(order, square_sum, small, vector_arrays, unit_arrays):
    arrays = (*vector_arrays, *unit_arrays)
    outs = [jax.ShapeDtypeStruct(array.shape, F32) for array in arrays]
    outs.append(jax.ShapeDtypeStruct((2, arrays[0].shape[1]), F32))
    return order.call(
        small_update_kernel,
        (1,),
        [whole((1, 1)), whole(small.shape)] + [whole(array.shape) for array in arrays],
        [whole(out.shape) for out in outs],
        outs,
        [],
        0,
        0,
        "update_small",
    )(square_sum, small, *arrays)


def choose(refs, step):
    value = refs[0][...]
    for index in range(1, len(refs)):
        value = jnp.where(step == index, refs[index][...], value)
    return value.astype(F32)


def update(order, square_sum, gradients, groups, rates, cut, name):
    arrays = [array for group in groups for array in group]

    def spec(shape):
        return pl.BlockSpec((1,) + shape[1:], lambda step: (step,) + (0,) * (len(shape) - 1))

    outs = [jax.ShapeDtypeStruct(array.shape, F32) for array in arrays]
    return order.call(
        partial(update_kernel, cut, rates, len(gradients)),
        (arrays[0].shape[0],),
        [whole((1, 1))]
        + [whole(gradient.shape) for gradient in gradients]
        + [spec(array.shape) for array in arrays],
        [spec(out.shape) for out in outs],
        outs,
        [],
        20 * sum(array.size for array in arrays) // 3,
        8 * sum(array.size for array in arrays),
        name,
    )(square_sum, *gradients, *arrays)


def body(
    source_tokens,
    target_tokens,
    source_lengths,
    target_lengths,
    bucket_kinds,
    source_cotangent,
    target_cotangent,
    attention_in,
    attention_out,
    hidden_in,
    hidden_out,
    vectors,
    hidden_bias,
    first_attention_in,
    first_attention_out,
    first_hidden_in,
    first_hidden_out,
    first_vectors,
    first_hidden_bias,
    second_attention_in,
    second_attention_out,
    second_hidden_in,
    second_hidden_out,
    second_vectors,
    second_hidden_bias,
):
    order = Order()
    moves = TensorMoves(order)
    split = CrossRows(order) if lax.axis_size("dp") == 8 else PlainRows(order)
    assert bucket_kinds.shape[0] == 1
    shard_rows = attention_in.shape[2]
    head_width = attention_in.shape[3]
    unit_width = hidden_in.shape[2]
    shard_units = hidden_bias.shape[1]

    small_shard = jnp.concatenate([vectors, hidden_bias.reshape(-1, shard_rows)], axis=0)
    small = split.stack(small_shard.astype(BF16)).astype(F32)

    attn_full = [None] * 3
    up_full = [None] * 2
    down_full = [None] * 2
    attn_zero = split.start(attention_shard(order, attention_in, attention_out, 0))
    attn_one = split.start(attention_shard(order, attention_in, attention_out, 1))
    up_shard, down_shard = feed_shard(order, hidden_in, hidden_out, 0)
    up_zero, down_zero = split.start(up_shard), split.start(down_shard)
    attn_two = split.start(attention_shard(order, attention_in, attention_out, 2))
    up_shard, down_shard = feed_shard(order, hidden_in, hidden_out, 1)
    up_one, down_one = split.start(up_shard), split.start(down_shard)

    norms = Norms(order, small[:, :25].transpose(1, 0, 2).reshape(25, -1), split.y)
    count = head_width // shard_rows
    own_blocks = split.blocks(small, moves.me * count, count)
    head_bias = jnp.concatenate([block[14:20] for block in own_blocks], axis=1)
    unit_bias = jnp.concatenate(
        [block[25:].reshape(2, shard_units) for block in own_blocks], axis=1
    )

    block_rows = source_tokens.shape[0]
    places = jnp.concatenate(
        [
            (moves.me ^ index) * block_rows + jnp.arange(block_rows, dtype=jnp.int32)
            for index in range(moves.count)
        ]
    )
    source_items, source_live = item_codes(bucket_kinds[0], source_lengths[0], places)
    target_items, target_live = item_codes(bucket_kinds[0], target_lengths[0], places)

    def layout_of(key_codes, query_codes):
        rows = jnp.stack([key_codes, places, query_codes])
        return jnp.pad(rows, ((0, 5), (0, 0))).astype(F32)

    encoder_layout = layout_of(source_live, source_items)
    self_layout = layout_of(target_live, target_items)
    cross_layout = layout_of(source_live, target_items)

    source, low = norms.forward(0, source_tokens)
    source_norm_one = moves.gather(low)
    target, low = norms.forward(3, target_tokens)
    target_norm_one = moves.gather(low)

    attn_full[0] = split.finish(attn_zero)
    attention = attention_forward(
        order,
        moves,
        attn_full[0],
        source_norm_one,
        source_norm_one,
        head_bias[:2],
        encoder_layout,
        False,
        (target_norm_one[2],),
    )
    next(attention)
    order.before_next(attn_one)
    attn_full[1] = split.finish(attn_one)
    branch, source_attn_state = next(attention)
    up_zero = order.after_last(up_zero)
    order.before_next(up_zero)
    up_full[0] = split.finish(up_zero)
    source_mid, low = norms.forward(1, source, branch, 20)
    source_norm_two = moves.gather(low)

    attention = attention_forward(
        order,
        moves,
        attn_full[1],
        target_norm_one,
        target_norm_one,
        head_bias[2:4],
        self_layout,
        True,
        (source_norm_two[2], up_full[0][1]),
    )
    next(attention)
    branch, self_state = next(attention)
    order.before_next(down_zero)
    down_full[0] = split.finish(down_zero)
    target_mid, low = norms.forward(4, target, branch, 21)
    target_norm_two = moves.gather(low)

    def feed_pair(slot_id, normed, first=(), between=None):
        weights = up_full[slot_id], down_full[slot_id]
        bias = unit_bias[slot_id : slot_id + 1]
        far = feed_forward(order, *weights, normed[2:], bias, False)
        arrived = moves.cross(*far[2:], first)
        if between is not None:
            order.before_next(between)
        near = feed_forward(order, *weights, normed[:2], bias, True)
        return moves.parts(near[2:], arrived), (near[:2], far[:2])

    branch, source_ffn_state = feed_pair(0, source_norm_two, (target_norm_two[2],), attn_two)
    attn_full[2] = split.finish(attn_two)
    source_last, low, encoder_output = norms.forward(2, source_mid, branch, 23, full=True)
    memory = moves.gather(low)
    order.before_next(up_one)
    up_full[1] = split.finish(up_one)

    attention = attention_forward(
        order,
        moves,
        attn_full[2],
        target_norm_two,
        memory,
        head_bias[4:],
        cross_layout,
        False,
        (up_full[1][1],),
    )
    next(attention)
    order.before_next(down_one)
    branch, cross_state = next(attention)
    down_full[1] = split.finish(down_one)
    target_cross, low = norms.forward(5, target_mid, branch, 22)
    low = lax.optimization_barrier((low, down_full[1][1]))[0]
    target_norm_three = moves.gather(low)
    branch, target_ffn_state = feed_pair(1, target_norm_three)
    target_last, decoder_output = norms.forward(6, target_cross, branch, 24, low=False, full=True)

    def feed_back_pair(slot_id, rows, states, first=()):
        weights = up_full[slot_id], down_full[slot_id]
        near = feed_backward(order, *weights, rows[:2], states[0][1], True)
        if len(rows) < 4:
            rows = moves.gather_late(rows)
        far = feed_backward(order, *weights, rows[2:], states[1][1], False)
        parts = moves.parts(near[2:], moves.cross(*far[2:], first))
        return rows, parts, (near[0], far[0]), near[1] + far[1]

    def feed_weight_pair(upstream_rows, states, normed, pre_grads):
        up_send, up_keep = feed_weights(order, normed, pre_grads)
        up_arrived = split.send(up_send)
        activated = (states[0][0], states[1][0])
        down_send, down_keep = feed_weights(order, upstream_rows, activated)
        return (up_keep, up_arrived), (down_keep, split.send(down_send))

    target_flow, sums_six, low = norms.backward(6, target_last, (), target_cotangent)
    upstream_rows, parts, pre_grads, unit_sums_one = feed_back_pair(
        1, moves.gather_near(low), target_ffn_state
    )
    up_parts, down_parts = feed_weight_pair(
        upstream_rows, target_ffn_state, target_norm_three, pre_grads
    )
    target_flow, sums_five, low = norms.backward(5, target_cross, parts, None, target_flow)
    upstream_rows = moves.gather(low)

    up_grad_one = split.settle(*up_parts)
    grads, cross_sums = attention_backward(
        order, attn_full[2], upstream_rows, cross_state, cross_layout, False
    )
    memory_arrived = moves.cross(
        *spread_rows(order, grads, attn_full[2], head_width, 3 * head_width, 2), (down_parts[1],)
    )
    arrived = moves.cross(*spread_rows(order, grads, attn_full[2], 0, head_width, 2))
    near = spread_rows(order, grads, attn_full[2], head_width, 3 * head_width, 0)
    memory_parts = moves.parts(near, memory_arrived)
    near = spread_rows(order, grads, attn_full[2], 0, head_width, 0)
    parts = moves.parts(near, arrived)
    send, keep_two = attention_weights(
        order, target_norm_two, memory, upstream_rows, grads, cross_state[1]
    )
    arrived_two = split.send(send)
    down_grad_one = split.settle(*down_parts)
    source_flow, sums_two, low = norms.backward(2, source_last, memory_parts, source_cotangent)
    source_rows = moves.gather_near(lax.optimization_barrier((low, arrived))[0])
    target_flow, sums_four, low = norms.backward(4, target_mid, parts, None, target_flow)
    self_upstream = moves.gather(low)
    source_rows = moves.gather_late(source_rows)
    upstream_rows, parts, pre_grads, unit_sums_zero = feed_back_pair(
        0, source_rows, source_ffn_state, (arrived_two,)
    )
    attn_grad_two = split.settle(keep_two, arrived_two)
    up_parts, down_parts = feed_weight_pair(
        upstream_rows, source_ffn_state, source_norm_two, pre_grads
    )
    source_flow, sums_one, low = norms.backward(1, source_mid, parts, None, source_flow)
    upstream_rows = moves.gather(low)

    self_grads, self_sums = attention_backward(
        order, attn_full[1], self_upstream, self_state, self_layout, True
    )
    up_grad_zero = split.settle(*up_parts)
    self_arrived = moves.cross(
        *spread_rows(order, self_grads, attn_full[1], 0, 3 * head_width, 2), (upstream_rows[2],)
    )
    send, keep_one = attention_weights(
        order, target_norm_one, target_norm_one, self_upstream, self_grads, self_state[1]
    )
    arrived_one = split.send(send)
    near = spread_rows(order, self_grads, attn_full[1], 0, 3 * head_width, 0)
    self_parts = moves.parts(near, self_arrived)
    grads, source_sums = attention_backward(
        order, attn_full[0], upstream_rows, source_attn_state, encoder_layout, False
    )
    down_grad_zero = split.settle(*down_parts)
    send, keep_zero = attention_weights(
        order, source_norm_one, source_norm_one, upstream_rows, grads, source_attn_state[1]
    )
    arrived_zero = split.send(send)
    arrived = moves.cross(
        *spread_rows(order, grads, attn_full[0], 0, 3 * head_width, 2), (arrived_one, self_arrived)
    )
    attn_grad_one = split.settle(keep_one, arrived_one)
    near = spread_rows(order, grads, attn_full[0], 0, 3 * head_width, 0)
    parts = moves.parts(near, arrived)
    target_grad, sums_three = norms.backward(
        3, target, self_parts, None, target_flow, low=False, last=True
    )
    source_grad, sums_zero = norms.backward(
        0, source, parts, None, source_flow, low=False, last=True
    )

    norm_sums = (sums_zero, sums_one, sums_two, sums_three, sums_four, sums_five, sums_six)
    vector_rows = [sums[0:1] for sums in norm_sums] + [sums[1:2] for sums in norm_sums]
    vector_rows += [sums[2:3] for sums in (sums_one, sums_four, sums_five, sums_two, sums_six)]
    attn_grad_zero = split.settle(keep_zero, arrived_zero)
    early_squares = sum_of_squares(
        order,
        (attn_grad_one, attn_grad_two, up_grad_zero, up_grad_one, down_grad_zero, down_grad_one),
    )
    own_rows = [source_sums, self_sums, cross_sums]
    for sums in (unit_sums_zero, unit_sums_one):
        cut = sums.reshape(head_width // shard_rows, -1, shard_rows).transpose(1, 0, 2)
        own_rows.append(cut.reshape(-1, head_width))
    own_rows = jnp.concatenate(own_rows, axis=0)
    columns = jnp.arange(moves.count * head_width, dtype=jnp.int32) // head_width
    own_rows = jnp.where(columns[None, :] == moves.me, jnp.tile(own_rows, (1, moves.count)), 0.0)
    small_sum = split.spread(moves.total(jnp.concatenate(vector_rows + [own_rows], axis=0)))

    attn_grads = (attn_grad_zero, attn_grad_one, attn_grad_two)
    up_grads = (up_grad_zero, up_grad_one)
    down_grads = (down_grad_zero, down_grad_one)
    local_squares = early_squares + sum_of_squares(
        order, (attn_grad_zero,), small_sum, moves.count
    )
    square_sum = split.total(moves.total(local_squares))
    grad_norm = jnp.sqrt(square_sum)[0, 0]
    rate_in, rate_out, rate_down = (
        0.5 * D ** (-0.5),
        0.5 * (D // 8) ** (-0.5),
        0.5 * FF ** (-0.5),
    )

    def attention_cut(refs, step):
        values = choose(refs, step)
        inputs = [
            values[:, which * head_width : (which + 1) * head_width] for which in range(3)
        ]
        return jnp.stack(inputs), values[:, 3 * head_width :].T

    def up_cut(refs, step):
        return (choose(refs, step),)

    def down_cut(refs, step):
        return (choose(refs, step).T,)

    attn_new = update(
        order,
        square_sum,
        attn_grads,
        (
            (attention_in, first_attention_in, second_attention_in),
            (attention_out, first_attention_out, second_attention_out),
        ),
        (rate_in, rate_out),
        attention_cut,
        "update_attention",
    )
    up_new = update(
        order,
        square_sum,
        up_grads,
        ((hidden_in, first_hidden_in, second_hidden_in),),
        (rate_in,),
        up_cut,
        "update_up",
    )
    down_new = update(
        order,
        square_sum,
        down_grads,
        ((hidden_out, first_hidden_out, second_hidden_out),),
        (rate_down,),
        down_cut,
        "update_down",
    )
    *small_new, bias_grad = small_update(
        order,
        square_sum,
        small_sum,
        (vectors, first_vectors, second_vectors),
        (hidden_bias, first_hidden_bias, second_hidden_bias),
    )
    return (
        encoder_output,
        decoder_output,
        source_grad,
        target_grad,
        grad_norm,
        *attn_new,
        *up_new,
        *down_new,
        *small_new,
        bias_grad,
    )


def solution(mesh):
    placed = (
        P(("dp", "tensor"), None),
        P(("dp", "tensor"), None),
        P("dp", None),
        P("dp", None),
        P("dp"),
        P(("dp", "tensor"), None),
        P(("dp", "tensor"), None),
        P(None, None, "dp", "tensor"),
        P(None, "tensor", "dp"),
        P(None, "dp", "tensor"),
        P(None, "tensor", "dp"),
        P(None, "dp"),
        P(None, "dp"),
        P(None, None, "dp", "tensor"),
        P(None, "tensor", "dp"),
        P(None, "dp", "tensor"),
        P(None, "tensor", "dp"),
        P(None, "dp"),
        P(None, "dp"),
        P(None, None, "dp", "tensor"),
        P(None, "tensor", "dp"),
        P(None, "dp", "tensor"),
        P(None, "tensor", "dp"),
        P(None, "dp"),
        P(None, "dp"),
    )
    return jax.shard_map(
        body,
        mesh=mesh,
        in_specs=placed,
        out_specs=(
            P(("dp", "tensor"), None),
            P(("dp", "tensor"), None),
            P(("dp", "tensor"), None),
            P(("dp", "tensor"), None),
            P(),
            P(None, None, "dp", "tensor"),
            P(None, None, "dp", "tensor"),
            P(None, None, "dp", "tensor"),
            P(None, "tensor", "dp"),
            P(None, "tensor", "dp"),
            P(None, "tensor", "dp"),
            P(None, "dp", "tensor"),
            P(None, "dp", "tensor"),
            P(None, "dp", "tensor"),
            P(None, "tensor", "dp"),
            P(None, "tensor", "dp"),
            P(None, "tensor", "dp"),
            P(None, "dp"),
            P(None, "dp"),
            P(None, "dp"),
            P(None, "dp"),
            P(None, "dp"),
            P(None, "dp"),
            P(None, "dp"),
        ),
        check_vma=False,
    )
```
